32 devices in a mesh: group: 2 (over y), shot: 4 (over z), line: 2 (over x), tm: 2 (over core).
Axes of the slice: x: 2, y: 2, z: 4, core: 2. Of those that a mesh axis runs over, the one named last changes fastest.
Arguments:
- initial_guess: bfloat16 [8, 256, 1024], P(('group', 'shot'), 'line', 'tm'), parts along dimension 0
- measured_mixtures: bfloat16 [4, 256, 1024], P('group', 'line'), parts along dimension 0
- launch_lags: int32 [8], P('group'), parts along dimension 0, may hold values from 0 to 127, as said below
- source_launch_order: int32 [8], P('group'), parts along dimension 0, may hold values from 0 to 3, each once
- station_portion_tallies: int32 [16], P('group'), parts along dimension 0, may hold values from 1 to 32, 128 in all
- source_entry_kernel: bfloat16 [4, 3, 64], replicated, may hold values from -1.75 to 1.75
- source_spaced_kernel: bfloat16 [3, 64, 64], replicated, may hold values from -0.4375 to 0.4375
- source_exit_kernel: bfloat16 [4, 64], replicated, may hold values from -0.5 to 0.5
- source_inner_offsets: float32 [2, 64], replicated, may hold values from -3 to 3
- station_entry_kernel: bfloat16 [4, 3, 64], replicated, may hold values from -1.75 to 1.75
- station_spaced_kernel: bfloat16 [3, 64, 64], replicated, may hold values from -0.4375 to 0.4375
- station_exit_kernel: bfloat16 [4, 64], replicated, may hold values from -0.5 to 0.5
- station_inner_offsets: float32 [2, 64], replicated, may hold values from -3 to 3
- learned_pace_factors: float32 [2], replicated, may hold values from 0.3 to 0.8
Outputs:
- deblended: bfloat16 [8, 256, 1024], P(('group', 'shot'), 'line', 'tm'), parts along dimension 0
The draws below stay inside these ranges and needn't reach their ends.
There are 2 independent parts, one for each index of `group`. The reference program is written for one: setup_inputs(seed, part) draws one part's arguments, and reference() takes and returns one part's arrays. A program takes and returns all parts, laid end to end along the dimension named above; an argument that names none is the same for every part. Nothing has to cross between parts.
Inputs may be any that keep to these rules, and one draw needn't show every extreme that they name: `launch_lags`: 0 and 127 both occur. `source_launch_order`: each shot once. `station_portion_tallies`: the counts sum to 128 and the largest equals 32.
All inputs are finite; a program needn't handle non-finite values.
Results may differ from the reference program's by a relative error of at most 0.013.
Values may be sent and summed in bfloat16 or wider, within the bound.
A program may use at most 64 MiB of HBM per device.

```python
import math
import jax
import jax.numpy as jnp
import numpy as np
from jax import lax

LINES = 16
RPL = 16
NT = 1024
FEAT = 64
DMAX = 128
ITERS = 2
TILE_SOURCES = 4
NG = 2
RB = 128
NP = 8
RCAP = 32
N_LINE = 2


def receiver_scales(key):
    sub_key = jax.random.fold_in(key, 11)
    return jnp.exp(jax.random.uniform(sub_key, (LINES * RPL,), jnp.float32, math.log(0.3), math.log(3.0)))


def time_decay():
    fraction = jnp.arange(NT, dtype=jnp.float32) / NT
    return jnp.exp(-math.log(3.0) * fraction)


def draw_initial_guess(key, part):
    rscale = receiver_scales(key)
    shape_full = (TILE_SOURCES, LINES * RPL, NT)
    sscale = jnp.exp(jax.random.uniform(jax.random.fold_in(key, 12), (TILE_SOURCES,), jnp.float32, math.log(0.5), math.log(2.0)))
    noise = jax.random.normal(jax.random.fold_in(key, 13), shape_full, jnp.float32)
    values = noise * sscale[:, None, None] * rscale[None, :, None] * time_decay()[None, None, :]
    return values.astype(jnp.bfloat16)


def draw_measured_mixtures(key, part):
    rscale = receiver_scales(key)
    shape_full = (NG, LINES * RPL, NT)
    noise = 1.4 * jax.random.normal(jax.random.fold_in(key, 15), shape_full, jnp.float32)
    values = noise * rscale[None, :, None] * time_decay()[None, None, :]
    return values.astype(jnp.bfloat16)


def draw_launch_lags(key, part):
    base = jax.random.randint(jax.random.fold_in(key, 21), (TILE_SOURCES,), 0, DMAX)
    lowest = jax.random.randint(jax.random.fold_in(key, 22), (), 0, TILE_SOURCES)
    highest = (lowest + 1 + jax.random.randint(jax.random.fold_in(key, 23), (), 0, TILE_SOURCES - 1)) % TILE_SOURCES
    return base.at[lowest].set(0).at[highest].set(DMAX - 1).astype(jnp.int32)


def split_up(amount, total, bound, skew):
    weights = [(1 << 20) // math.isqrt(grade ** skew) + 1 for grade in range(2, amount + 1)]
    spare, given = total - bound - (amount - 1), [1] * (amount - 1)
    while spare > 0:
        free = [i for i in range(amount - 1) if given[i] < bound]
        pool, budget = sum([weights[i] for i in free]), spare
        for i in free:
            more = min(bound - given[i], max(1, budget * weights[i] // pool), spare)
            given[i] = given[i] + more
            spare = spare - more
    return np.array([bound] + given)


def ragged(own_key, number_of, total, limit, lean):
    if number_of == 2:
        one = jax.random.randint(own_key, (), max(1, total - limit), min(limit, total - 1) + 1)
        return jnp.stack([one, total - one])
    sizes = jnp.asarray(split_up(number_of, total, limit, lean), jnp.int32)
    pairs = (number_of - 1) // 2
    giver, sink = sizes[1:1 + 2 * pairs:2], sizes[2:2 + 2 * pairs:2]
    room = jnp.minimum(giver - 1, limit - sink)
    shifted = jax.random.randint(jax.random.fold_in(own_key, 1), (pairs,), 0, 1 << 20) % (room + 1)
    sizes = sizes.at[1:1 + 2 * pairs:2].set(giver - shifted).at[2:2 + 2 * pairs:2].set(sink + shifted)
    return sizes[jax.random.permutation(jax.random.fold_in(own_key, 2), number_of)]


def centred(key, extent, deviation, limit, kind=jnp.bfloat16):
    entries = jax.random.normal(key, extent, jnp.float32) * deviation
    return jnp.minimum(jnp.maximum(entries, -limit), limit).astype(kind)


def setup_inputs(seed: int = 0, part: int = 0) -> dict:
    splits = jax.random.split(jax.random.key(seed), 15)
    part_splits = jax.random.split(jax.random.fold_in(splits[14], part), 15)
    return {
        "initial_guess": draw_initial_guess(jax.random.fold_in(jax.random.fold_in(splits[14], part), 71), part),
        "measured_mixtures": draw_measured_mixtures(jax.random.fold_in(jax.random.fold_in(splits[14], part), 71), part),
        "launch_lags": draw_launch_lags(jax.random.fold_in(jax.random.fold_in(splits[14], part), 71), part),
        "source_launch_order": jax.random.permutation(part_splits[3], TILE_SOURCES).astype(jnp.int32),
        "station_portion_tallies": ragged(part_splits[4], NP, RB, RCAP, 2).astype(jnp.int32),
        "source_entry_kernel": centred(splits[5], (4, 3, FEAT), 12 ** -0.5, 1.75),
        "source_spaced_kernel": centred(splits[6], (3, FEAT, FEAT), (3 * FEAT) ** -0.5, 0.4375),
        "source_exit_kernel": centred(splits[7], (4, FEAT), (2 * FEAT) ** -0.5, 0.5),
        "source_inner_offsets": centred(splits[8], (2, FEAT), 0.5, 3.0, jnp.float32),
        "station_entry_kernel": centred(splits[9], (4, 3, FEAT), 12 ** -0.5, 1.75),
        "station_spaced_kernel": centred(splits[10], (3, FEAT, FEAT), (3 * FEAT) ** -0.5, 0.4375),
        "station_exit_kernel": centred(splits[11], (4, FEAT), (2 * FEAT) ** -0.5, 0.5),
        "station_inner_offsets": centred(splits[12], (2, FEAT), 0.5, 3.0, jnp.float32),
        "learned_pace_factors": jnp.clip(jnp.exp(jax.random.uniform(splits[13], (ITERS,), jnp.float32, math.log(0.3), math.log(0.8))), 0.3, 0.8),
    }


MARGIN = 7
EPSILON = 1e-05

def network(padded, first_sample, full_len, weight_in, weight_mid, weight_out, bias_pair):
    batch = padded.shape[0]
    sample_extent = padded.shape[2] - 2 * MARGIN
    half_len = sample_extent // 2
    count_one = half_len + 6
    count_two = half_len + 2
    wide_in = padded.astype(jnp.float32)
    total_sum = jnp.zeros((batch, weight_in.shape[2], count_one), jnp.float32)
    for tap_index in range(4):
        tap_slice = wide_in[:, :, tap_index:tap_index + 2 * count_one - 1:2]
        total_sum = total_sum + jnp.einsum('bcv,cf->bfv', tap_slice, weight_in[tap_index].astype(jnp.float32), precision=lax.Precision.HIGHEST)
    where_one = first_sample // 2 - 3 + jnp.arange(count_one)
    keep_one = (where_one >= 0) & (where_one < full_len // 2)
    layer_one = jnp.where(keep_one, jax.nn.relu(total_sum + bias_pair[0][None, :, None]), 0.0).astype(jnp.bfloat16)
    wide_one = layer_one.astype(jnp.float32)
    total_two = jnp.zeros((batch, weight_mid.shape[2], count_two), jnp.float32)
    for tap_index in range(3):
        total_two = total_two + jnp.einsum('bgw,gf->bfw', wide_one[:, :, 2 * tap_index:2 * tap_index + count_two], weight_mid[tap_index].astype(jnp.float32), precision=lax.Precision.HIGHEST)
    where_two = first_sample // 2 - 1 + jnp.arange(count_two)
    keep_two = (where_two >= 0) & (where_two < full_len // 2)
    layer_two = jnp.where(keep_two, jax.nn.relu(total_two + bias_pair[1][None, :, None]), 0.0).astype(jnp.bfloat16)
    projected = jnp.einsum('bgw,kg->bkw', layer_two.astype(jnp.float32), weight_out.astype(jnp.float32), precision=lax.Precision.HIGHEST)
    even_part = projected[:, 1, 1:half_len + 1] + projected[:, 3, 0:half_len]
    odd_part = projected[:, 0, 2:half_len + 2] + projected[:, 2, 1:half_len + 1]
    return jnp.stack([even_part, odd_part], axis=2).reshape(batch, sample_extent)

def sections(station_portion_tallies, block_size):
    offsets = jnp.cumsum(station_portion_tallies) - station_portion_tallies
    places = jnp.arange(block_size, dtype=jnp.int32)
    owner_of = lax.optimization_barrier(jnp.sum((offsets[None, :] <= places[:, None]).astype(jnp.int32), axis=1)) - 1
    return (offsets, owner_of)

def receiver_pass(sorting_choice, rms_scale, weights):
    normed = (sorting_choice.astype(jnp.float32) / rms_scale[:, None, None]).astype(jnp.bfloat16)

    def one_receiver(trace_set):
        shot_count = trace_set.shape[0]
        edged_set = jnp.pad(trace_set, ((1, 1), (0, 0)))
        stacked = jnp.stack([edged_set[channel:channel + shot_count] for channel in range(3)], axis=1)
        inputs = jnp.pad(stacked, ((0, 0), (0, 0), (MARGIN, MARGIN)))
        return network(inputs, 0, trace_set.shape[1], *weights)
    shaped = lax.map(one_receiver, normed)
    return (sorting_choice.astype(jnp.float32) + rms_scale[:, None, None] * shaped).astype(jnp.bfloat16)

def mixture_leftover(sorting_choice, measured_mixtures_here, source_launch_order, launch_lags, correction_pace):
    channel_total, shot_count, sample_extent = sorting_choice.shape
    mixture_batches = measured_mixtures_here.shape[1]
    sources_within_mixture = shot_count // mixture_batches
    widened = jnp.pad(sorting_choice.astype(jnp.float32), ((0, 0), (0, 0), (DMAX, 0)))

    def fire_shot(column, delay_at):
        return lax.dynamic_slice_in_dim(column, (DMAX - delay_at).astype(jnp.int32), sample_extent, axis=1)
    launched_source_collection = jax.vmap(fire_shot, in_axes=(1, 0), out_axes=1)(widened, launch_lags)
    recording_mismatch = jnp.take(launched_source_collection, source_launch_order, axis=1).reshape(channel_total, mixture_batches, sources_within_mixture, sample_extent).sum(axis=2) - measured_mixtures_here.astype(jnp.float32)
    place_labels = jnp.arange(shot_count, dtype=jnp.int32)
    source_location = lax.optimization_barrier(jnp.sum(jnp.where(source_launch_order[None, :] == place_labels[:, None], place_labels[None, :], 0), axis=1)).astype(jnp.int32)
    group_of = source_location // sources_within_mixture
    late_pad = jnp.pad(recording_mismatch, ((0, 0), (0, 0), (0, DMAX)))

    def spread(group_at, delay_at):
        group_row = jnp.take(late_pad, group_at, axis=1)
        return lax.dynamic_slice_in_dim(group_row, delay_at.astype(jnp.int32), sample_extent, axis=1)
    pulled = jax.vmap(spread, in_axes=(0, 0), out_axes=1)(group_of, launch_lags)
    return (sorting_choice.astype(jnp.float32) - correction_pace * pulled).astype(jnp.bfloat16)

def reference(initial_guess, measured_mixtures, launch_lags, source_launch_order, station_portion_tallies, source_entry_kernel, source_spaced_kernel, source_exit_kernel, source_inner_offsets, station_entry_kernel, station_spaced_kernel, station_exit_kernel, station_inner_offsets, learned_pace_factors):
    shot_count, recv_all, full_len = initial_guess.shape
    block_size = recv_all // N_LINE
    offsets, owner_of = sections(station_portion_tallies, block_size)
    shot_weights = (source_entry_kernel, source_spaced_kernel, source_exit_kernel, source_inner_offsets)
    receiver_weights = (station_entry_kernel, station_spaced_kernel, station_exit_kernel, station_inner_offsets)
    measured_mixtures_here = jnp.transpose(measured_mixtures, (1, 0, 2))
    ballot = (owner_of[:, None] == jnp.arange(station_portion_tallies.shape[0], dtype=jnp.int32)[None, :]).astype(jnp.float32)

    def shot_network(shot_traces):
        line_grid = shot_traces.reshape(LINES, RPL, full_len)
        edged_set = jnp.pad(line_grid, ((1, 1), (0, 0), (0, 0)))
        stacked = jnp.stack([edged_set[channel:channel + LINES] for channel in range(3)], axis=2)
        inputs = jnp.pad(stacked.reshape(recv_all, 3, full_len), ((0, 0), (0, 0), (MARGIN, MARGIN)))
        correction = network(inputs, 0, full_len, *shot_weights)
        return (shot_traces.astype(jnp.float32) + correction).astype(jnp.bfloat16)
    current = initial_guess
    for unrolled_round_ordinal in range(ITERS):
        after_shot = lax.map(shot_network, current)
        sorting_choice = jnp.transpose(after_shot, (1, 0, 2))
        energy = lax.optimization_barrier(jnp.sum(jnp.square(sorting_choice.astype(jnp.float32)), axis=(1, 2)))
        blocks = energy.reshape(N_LINE, block_size)
        section_sum = jnp.dot(blocks, ballot, precision=lax.Precision.HIGHEST)
        denominator = (jnp.take(station_portion_tallies, owner_of) * (shot_count * full_len)).astype(jnp.float32)
        mean_power = jnp.take(section_sum, owner_of, axis=1) / denominator[None, :]
        rms_scale = jnp.sqrt(mean_power.reshape(recv_all) + EPSILON)
        sorting_choice = receiver_pass(sorting_choice, rms_scale, receiver_weights)
        sorting_choice = mixture_leftover(sorting_choice, measured_mixtures_here, source_launch_order, launch_lags, learned_pace_factors[unrolled_round_ordinal])
        current = jnp.transpose(sorting_choice, (1, 0, 2))
    return current
```

```python
import functools
import math

import jax
import jax.numpy as jnp
import numpy as np
from jax import lax
from jax.experimental import pallas as pl
from jax.experimental.pallas import tpu as pltpu
from jax.sharding import PartitionSpec as P

RPL = 16
ITERS = 2
EPSILON = 1e-05
C = 8
PACK = 4
TAPS = (1, 2, 3, 0)
F32, BF16 = jnp.float32, jnp.bfloat16
AXES = ("shot", "line", "tm")


def ahead(x, k):
    edge = pltpu.roll(x[:k], C - 1, 1)
    edge = jnp.where(lax.broadcasted_iota(jnp.int32, edge.shape, 1) == C - 1, 0.0, edge)
    return edge if k == x.shape[0] else jnp.concatenate([x[k:], edge], axis=0)


def behind(x, k):
    edge = pltpu.roll(x[x.shape[0] - k :], 1, 1)
    edge = jnp.where(lax.broadcasted_iota(jnp.int32, edge.shape, 1) == 0, 0.0, edge)
    return edge if k == x.shape[0] else jnp.concatenate([edge, x[: x.shape[0] - k]], axis=0)


def even_lanes(shape):
    return lax.broadcasted_iota(jnp.int32, shape, len(shape) - 1) < shape[-1] // 2


def net(x, w_in, pick, w_mid, w_out, place, bias, total, band):
    planes, _, lanes = x.shape
    rows = planes * C
    side = jnp.where(even_lanes(x.shape), ahead(x, 1), behind(x, 1))
    z = jnp.concatenate([x, side], axis=2).astype(BF16).reshape(rows, 2 * lanes)
    total[...] = jnp.zeros_like(total)
    wide = w_in.shape[1]
    feat = wide // PACK
    for j in range(3):
        tap = w_mid[j].astype(F32)
        for i in range(PACK):
            row = [tap if p == i else jnp.zeros_like(tap) for p in range(PACK)]
            at = (j * PACK + i) * feat
            band[at : at + feat, :] = jnp.concatenate(row, axis=1).astype(BF16)

    def step(q, carry):
        w_here = jnp.dot(pick[q], w_in[...], preferred_element_type=F32).astype(BF16)
        o_here = jnp.dot(w_out[...], place[q], preferred_element_type=F32).astype(BF16)
        h = jnp.dot(z, w_here, preferred_element_type=F32)
        h = jnp.maximum(h + bias[0:1, :], 0.0)
        cube = h.reshape(planes, C, wide)
        first = ahead(cube[:2], 2).reshape(2 * C, wide).astype(BF16)
        last = behind(cube[planes - 2 :], 2).reshape(2 * C, wide).astype(BF16)
        hb = h.astype(BF16)
        early = jnp.concatenate([last, hb[: rows - 2 * C]], axis=0)
        late = jnp.concatenate([hb[2 * C :], first], axis=0)
        g = jnp.dot(jnp.concatenate([early, hb, late], axis=1), band[...], preferred_element_type=F32)
        g = jnp.maximum(g + bias[1:2, :], 0.0).astype(BF16)
        total[...] += jnp.dot(g, o_here, preferred_element_type=F32)
        return carry

    lax.fori_loop(0, pick.shape[0], step, 0, unroll=2)
    y = total[...].reshape(planes, C, 2 * lanes)
    a, b = y[:, :, :lanes], y[:, :, lanes:]
    return a + jnp.where(even_lanes(b.shape), behind(b, 1), ahead(b, 1))


def shot_step(x, weights, member, out_ref, part_ref, total, band):
    y = (x + net(x, *weights, total, band)).astype(BF16)
    out_ref[...] = y
    y = y.astype(F32)
    energy = jnp.sum(jnp.sum(y * y, axis=0), axis=0, keepdims=True)
    sums = jnp.sum(member[...] * energy, axis=1, keepdims=True)
    part_ref[...] = jnp.broadcast_to(sums, part_ref.shape)


def shifted(buf, lag_ref, shots, forward):
    planes, lanes = buf.shape[1] // 2, buf.shape[3]
    shape = (planes, C, lanes)
    even = even_lanes(shape)
    per = lanes // 2 // shots
    lane_shot = lax.rem(lax.broadcasted_iota(jnp.int32, shape, 2), lanes // 2) // per
    out = jnp.zeros(shape, F32)
    for s in range(shots):
        lag = lag_ref[s]
        half, odd = lag // 2, lax.rem(lag, 2)
        at_even = half if forward else planes - half - odd
        at_odd = half + odd if forward else planes - half
        one = jnp.where(even, buf[odd, pl.ds(at_even, planes)], buf[odd, pl.ds(at_odd, planes)])
        out = jnp.where(lane_shot == s, one, out)
    return out


def station_step(shots, sp, tot_ref, spread, weights, lags, join, mix, take, pace, buf, total, band):
    planes, _, lanes = sp.shape
    rows = planes * C
    mean = jnp.sum(tot_ref[:, 0:1] * spread[...], axis=0, keepdims=True)
    rms = jnp.sqrt(mean + EPSILON).reshape(1, 1, lanes)
    normed = (sp / rms).astype(BF16).astype(F32)
    settled = (sp + rms * net(normed, *weights, total, band)).astype(BF16).astype(F32)

    def fill(x, forward):
        far = ahead(x, planes) if forward else behind(x, planes)
        near_at, far_at = (0, planes) if forward else (planes, 0)
        for v, at in ((x, near_at), (far, far_at)):
            buf[0, at : at + planes] = v
            h = lanes // 2
            buf[1, at : at + planes] = jnp.concatenate([v[:, :, h:], v[:, :, :h]], axis=2)

    fill(settled, False)
    fired = shifted(buf, lags, shots, False).astype(BF16).reshape(rows, lanes)
    misfit = jnp.dot(fired, join[...], preferred_element_type=F32)
    misfit -= jnp.dot(mix[...], take[...], preferred_element_type=F32)
    fill(misfit.reshape(planes, C, lanes), True)
    return (settled - pace * shifted(buf, lags, shots, True)).astype(BF16)


def by_phase(width):
    row = lax.broadcasted_iota(jnp.int32, (width, width), 0)
    col = lax.broadcasted_iota(jnp.int32, (width, width), 1)
    half = width // 2
    return jnp.where(col == 2 * lax.rem(row, half) + row // half, 1.0, 0.0).astype(BF16)


def unfold(read, into, sort):
    planes = into.shape[0]
    for c in range(C):
        v = lax.dot_general(sort, read(c), (((1,), (1,)), ((), ())), preferred_element_type=F32)
        into[:, c, :] = jnp.concatenate([v[:planes], v[planes:]], axis=1)


def entry_kernel(
    dims, x, wi, wp, wm, wo, wq, bi, member, out, part, mix, total, band, cube, side
):
    shots, blocks, halves = dims
    width = 2 * cube.shape[0]
    sort, each = by_phase(width), C // halves

    def traces(c):
        at, t = slice(c % each * width, (c % each + 1) * width), c // each
        rows = [x[(s * blocks + b) * halves + t, :, at].astype(F32) for s in range(shots) for b in range(blocks)]
        return jnp.concatenate(rows, axis=0).astype(BF16)

    tl = each * width

    def records(c):
        s, t = c // halves, c % halves
        rows = [
            x[(s * blocks + b) * halves + t, :, tl + g * width : tl + (g + 1) * width].astype(F32)
            for g in range((x.shape[2] - tl) // width)
            for b in range(blocks)
        ]
        return jnp.concatenate(rows, axis=0).astype(BF16)

    unfold(records, side, sort)
    mix[...] = side[...].astype(BF16).reshape(mix.shape)
    unfold(traces, cube, sort)
    shot_step(cube[...], (wi, wp, wm, wo, wq, bi), member, out, part, total, band)


def exit_kernel(
    it, dims, lags, pace, sp, tot, spread, wi, wp, wm, wo, wq, bi, join, mix, take, out, buf, total, band, cube
):
    shots, blocks, halves = dims
    width = 2 * cube.shape[0]
    sort, each = by_phase(width), C // halves
    x = station_step(
        shots, sp[...].astype(F32), tot, spread, (wi, wp, wm, wo, wq, bi), lags, join, mix, take, pace[it], buf, total, band
    )
    cube[...] = x.astype(F32)
    n, lh = cube.shape[2] // 2, out.shape[1]
    for c in range(C):
        v = cube[:, c, :]
        v = jnp.concatenate([v[:, :n], v[:, n:]], axis=0).T.astype(BF16)
        v = jnp.dot(v, sort, preferred_element_type=F32)
        at, t = slice(c % each * width, (c % each + 1) * width), c // each
        for j in range(shots * blocks):
            out[j * halves + t, :, at] = v[j * lh : (j + 1) * lh].astype(BF16)


def first_kernel(x, wi, wp, wm, wo, wq, bi, member, out, part, total, band):
    shot_step(x[...].astype(F32), (wi, wp, wm, wo, wq, bi), member, out, part, total, band)


def station_kernel(it, shots, lags, pace, sp, tot, spread, wi, wp, wm, wo, wq, bi, join, mix, take, out, buf, total, band):
    out[...] = station_step(
        shots, sp[...].astype(F32), tot, spread, (wi, wp, wm, wo, wq, bi), lags, join, mix, take, pace[it], buf, total, band
    )


def both_kernel(
    it, shots, lags, pace, sp, tot, spread, wi, wp, wm, wo, wq, bi, join, mix, take, vi, vp, vm, vo, vq, ci, member, out, part, buf, total, band
):
    x = station_step(
        shots, sp[...].astype(F32), tot, spread, (wi, wp, wm, wo, wq, bi), lags, join, mix, take, pace[it], buf, total, band
    )
    shot_step(x.astype(F32), (vi, vp, vm, vo, vq, ci), member, out, part, total, band)


def call(body, outs, ins, smem, scratch):
    v, s = pl.BlockSpec(memory_space=pltpu.VMEM), pl.BlockSpec(memory_space=pltpu.SMEM)
    return pl.pallas_call(
        body,
        out_shape=outs,
        in_specs=[s] * smem + [v] * (len(ins) - smem),
        out_specs=jax.tree.map(lambda _: v, outs),
        scratch_shapes=scratch,
        compiler_params=pltpu.CompilerParams(vmem_limit_bytes=48 * 2**20),
    )(*ins)


def prepared(w_in, w_mid, w_out, bias, near):
    n, feat = near.shape[1], w_in.shape[2]
    tiles = n // PACK
    cols = near.reshape(3, n, tiles, PACK).transpose(2, 1, 0, 3)
    pick = np.einsum("jk,tnci->tjnkci", np.eye(4)[list(TAPS)], cols).reshape(tiles, 4 * n, 12 * PACK)
    place = np.einsum("kj,tin->tjikn", np.eye(4)[list(TAPS)], np.eye(n).reshape(tiles, PACK, n)).reshape(tiles, 4 * PACK, 4 * n)
    w1 = w_in.reshape(12, 1, 1, feat)
    eye = jnp.eye(PACK, dtype=BF16)
    rows = (w1 * eye[None, :, :, None]).reshape(12 * PACK, PACK * feat)
    w2 = w_out.T.reshape(1, feat, 4, 1)
    ends = (w2 * eye[:, None, None, :]).reshape(PACK * feat, 4 * PACK)
    return rows, jnp.asarray(pick, BF16), w_mid, ends, jnp.asarray(place, BF16), jnp.tile(bias, (1, PACK))


def exchange_kernel(sizes, x, out, slots, send, recv):
    count = math.prod(sizes)
    me = (lax.axis_index("shot") * sizes[1] + lax.axis_index("line")) * sizes[2] + lax.axis_index("tm")

    def peer(off):
        at = lax.rem(me + off, count)
        return {
            "shot": at // (sizes[1] * sizes[2]),
            "line": lax.rem(at // sizes[2], sizes[1]),
            "tm": lax.rem(at, sizes[2]),
        }

    barrier = pltpu.get_barrier_semaphore()
    for off in range(1, count):
        pl.semaphore_signal(barrier, inc=1, device_id=peer(off), device_id_type=pl.DeviceIdType.MESH)
    pl.semaphore_wait(barrier, count - 1)
    copies = []
    for off in range(1, count):
        copy = pltpu.make_async_remote_copy(
            src_ref=x,
            dst_ref=slots.at[off],
            send_sem=send.at[off],
            recv_sem=recv.at[off],
            device_id=peer(off),
            device_id_type=pl.DeviceIdType.MESH,
        )
        copy.start()
        copies.append(copy)
    total = x[...]
    for off, copy in enumerate(copies, 1):
        copy.wait()
        total += slots[off]
    out[...] = total


def summed(x, sizes):
    count, v = math.prod(sizes), pl.BlockSpec(memory_space=pltpu.VMEM)
    return pl.pallas_call(
        functools.partial(exchange_kernel, sizes),
        out_shape=jax.ShapeDtypeStruct(x.shape, x.dtype),
        in_specs=[v],
        out_specs=v,
        scratch_shapes=[
            pltpu.VMEM((count, *x.shape), x.dtype),
            pltpu.SemaphoreType.DMA((count,)),
            pltpu.SemaphoreType.DMA((count,)),
        ],
        compiler_params=pltpu.CompilerParams(collective_id=0, has_side_effects=True),
    )(x)


SLOT = (0, 3, 1, 2)
HALF = 64
GROUPS = 4


def iota(shape, dim):
    return lax.broadcasted_iota(jnp.int32, shape, dim)


def weave(w_in, w_mid, w_out, bias, we, wm, wo, bi):
    feat = w_in.shape[2]
    wide = feat * len(SLOT)
    row, lane = iota((wide, wide), 0), iota((wide, wide), 1)
    at, ch = lax.rem(row, HALF), row // HALF
    slot = lane // feat
    pos = jnp.where(slot == 1, 3, jnp.where(slot == 0, 0, slot - 1))
    taps = w_in[...].astype(F32)
    for par in range(2):
        turned = lax.rem(at + (1 if par == 0 else HALF - 1), HALF)
        tap = lax.rem(turned, 4)
        base = jnp.zeros((wide, wide), F32)
        for c in range(3):
            for t in range(4):
                line = jnp.concatenate([taps[t, c : c + 1, :]] * len(SLOT), axis=1)
                base = jnp.where((ch == c) & (tap == t), line, base)
        for g in range(GROUPS):
            we[par * GROUPS + g] = jnp.where(turned // 4 == 4 * g + pos, base, 0.0).astype(BF16)
    zero = jnp.zeros((feat, feat), F32)
    mid = [w_mid[j].astype(F32) for j in range(3)]

    def block(came, goes):
        j = came - goes + 1
        return mid[j] if came is not None and 0 <= j < 3 else zero

    for n, came in enumerate(SLOT + (4, None, None, -1)):
        blocks = [zero if came is None else block(came, goes) for goes in SLOT]
        wm[n * feat : (n + 1) * feat, :] = jnp.concatenate(blocks, axis=1).astype(BF16)

    def sample(shape):
        col = iota(shape, 1)
        m = lax.rem(col, HALF)
        edge = jnp.where(m == HALF - 1, -1, jnp.where(m == 0, HALF, -4 * HALF))
        return jnp.where(col >= 2 * HALF, edge, m)

    near, far = sample((4, wide)), sample((feat, wide))
    for par in range(2):
        pick = jnp.where(lax.rem(near - 2 * par + 1 + 8 * HALF, 4) == iota((4, wide), 0), 1.0, 0.0).astype(BF16)
        base = lax.dot_general(w_out[...], pick, (((0,), (0,)), ((), ())), preferred_element_type=F32)
        for g in range(GROUPS):
            for n, i in enumerate(SLOT):
                d = far - 4 * (4 * g + i) - 2 * par + 1
                at = ((par * GROUPS + g) * len(SLOT) + n) * feat
                wo[at : at + feat, :] = jnp.where((d >= 0) & (d < 4), base, 0.0).astype(BF16)
    bi[...] = jnp.concatenate([bias[...]] * len(SLOT), axis=1)


def layers(zs, hs, gs, ys, we, wm, wo, bi):
    b0, b1 = bi[0:1, :], bi[1:2, :]
    rows, wide = zs.shape[1:]
    blocks = ys.shape[0] - 2
    per = rows // blocks
    for par in range(2):
        for g in range(GROUPS):
            h = jnp.dot(zs[par], we[par * GROUPS + g], preferred_element_type=F32)
            h = jnp.maximum(h + b0, 0.0).astype(BF16)
            for b in range(blocks):
                at = per + (b * GROUPS + g) * per
                hs[par, at : at + per, :] = h[b * per : (b + 1) * per]
    for par in range(2):
        for r in range(0, GROUPS * rows, rows):
            at = per + r
            x = [hs[par, at : at + rows, :]]
            x += [hs[par, at + d : at + d + rows, : wide // 2] for d in (per, -per)]
            g = jnp.dot(jnp.concatenate(x, axis=1), wm[...], preferred_element_type=F32)
            g = jnp.maximum(g + b1, 0.0).astype(BF16)
            for n in range(rows // per):
                b, q = divmod(r // per + n, GROUPS)
                col = (par * GROUPS + q) * wide
                gs[b * per : (b + 1) * per, col : col + wide] = g[n * per : (n + 1) * per]
    y = jnp.dot(gs[...], wo[...], preferred_element_type=F32)
    ys[1 : 1 + blocks] = y.reshape(blocks, per, wide)


def widen(pn, zs):
    blocks, per, wide = pn.shape
    lane = lax.rem(iota((per, wide), 1), HALF)

    def step(b, carry):
        here = pn[b + 1]
        at = pl.ds(pl.multiple_of(b * per, per), per)
        zs[0, at, :] = jnp.where(lane == HALF - 1, pn[b], here).astype(BF16)
        zs[1, at, :] = jnp.where(lane == 0, pn[b + 2], here).astype(BF16)
        return carry

    lax.fori_loop(0, blocks - 2, step, 0)


def patch_kernel(sizes, lags, order, tallies, pace, guess, mixtures, *refs):
    wa, wb, out = refs[:4], refs[4:8], refs[8]
    (gbuf, mbuf, sendx, recvx, sendm, recvm, backs, backr, sende, recve) = refs[9:19]
    (xs, mx, rolled, mf, member, pn, zs, hs, gs, ys) = refs[19:29]
    ta, tb = refs[29:33], refs[33:37]
    load_sem, ssem, rsem = refs[37:]
    n_shot, n_line, n_tm = sizes
    count = math.prod(sizes)
    at_shot, at_line, at_tm = (lax.axis_index(a) for a in AXES)
    me = (at_shot * n_line + at_line) * n_tm + at_tm
    shots = n_shot
    n_mix = mixtures.shape[0]
    run = shots // n_mix
    lc = guess.shape[1] // count
    tl = guess.shape[2]
    tile = 2 * HALF
    blocks = tl * n_tm // HALF
    each = tl // HALF

    def device(at):
        return {"shot": at // (n_line * n_tm), "line": lax.rem(at // n_tm, n_line), "tm": lax.rem(at, n_tm)}

    barrier = pltpu.get_barrier_semaphore()
    for off in range(1, count):
        pl.semaphore_signal(barrier, inc=1, device_id=device(lax.rem(me + off, count)), device_id_type=pl.DeviceIdType.MESH)
    loads = [
        pltpu.make_async_copy(guess.at[0], gbuf, load_sem.at[0]),
        pltpu.make_async_copy(mixtures, mbuf, load_sem.at[1]),
    ]
    for copy in loads:
        copy.start()
    for ref in (hs, ys, pn, rolled, mf):
        ref[...] = jnp.zeros_like(ref)

    def send(which, src, dst, to):
        return pltpu.make_async_remote_copy(
            src_ref=src,
            dst_ref=dst,
            send_sem=ssem.at[which, to],
            recv_sem=rsem.at[which, me],
            device_id=device(to),
            device_id_type=pl.DeviceIdType.MESH,
        )

    def arrival(which, src, dst, came):
        return pltpu.make_async_remote_copy(
            src_ref=src,
            dst_ref=dst,
            send_sem=ssem.at[which, came],
            recv_sem=rsem.at[which, came],
            device_id=device(came),
            device_id_type=pl.DeviceIdType.MESH,
        )

    recv_n = guess.shape[1]
    row, col = iota((recv_n, recv_n), 0), iota((recv_n, recv_n), 1)
    perm = jnp.where(col == lax.rem(row, lc) * count + row // lc, 1.0, 0.0).astype(BF16)
    loads[0].wait()
    v = jnp.dot(perm, gbuf[...], preferred_element_type=F32)
    for k in range(count):
        part = v[k * lc : (k + 1) * lc]
        sendx[k] = jnp.concatenate([part[:, : tl // 2], part[:, tl // 2 :]], axis=0).astype(BF16)
    loads[1].wait()
    other = (at_shot * n_line + (n_line - 1 - at_line)) * n_tm + at_tm
    row, col = iota((2 * lc, recv_n), 0), iota((2 * lc, recv_n), 1)
    wanted = jnp.where(row < lc, me, other)
    pick = jnp.where(col == lax.rem(row, lc) * count + wanted, 1.0, 0.0).astype(BF16)
    picked = [jnp.dot(pick, mbuf[g], preferred_element_type=F32) for g in range(n_mix)]
    recvm[at_line] = jnp.concatenate([p[:lc] for p in picked], axis=0).astype(BF16)
    sendm[...] = jnp.concatenate([p[lc:] for p in picked], axis=0).astype(BF16)
    recvx[me] = sendx[me]

    pl.semaphore_wait(barrier, count - 1)
    for off in range(1, count):
        to = lax.rem(me + off, count)
        send(0, sendx.at[to], recvx.at[me], to).start()
    send(1, sendm, recvm.at[at_line], other).start()

    weave(*wa, *ta)
    weave(*wb, *tb)
    sec = []
    for rows in ((lc, tile), (count, tile)):
        if rows[0] == lc:
            q = iota(rows, 0) * count + me
        else:
            q = lax.rem(iota(rows, 1), lc) * count + iota(rows, 0)
        edge, at, size = jnp.int32(0), jnp.zeros(rows, jnp.int32), jnp.zeros(rows, jnp.int32)
        for p in range(tallies.shape[0]):
            at = jnp.where(q >= edge, p, at)
            size = jnp.where(q >= edge, tallies[p], size)
            edge = edge + tallies[p]
        sec.append((at, size))
    for k in range(count):
        member[k] = jnp.where(sec[0][0] == sec[1][0][k : k + 1, :], 1.0, 0.0)
    scale = 1.0 / (sec[0][1] * (shots * tl * n_tm)).astype(F32)

    lane = iota((lc, tile), 1)
    low = lane < HALF
    inner = lax.rem(lane, HALF)

    def wait_all(which, src, dst, ids):
        for came in ids:
            arrival(which, src(came), dst(came), came).wait_recv()

    def sent_all(which, src, dst, ids):
        for to in ids:
            send(which, src(to), dst(to), to).wait_send()

    peers = [lax.rem(me + off, count) for off in range(1, count)]
    wait_all(0, lambda p: sendx.at[p], lambda p: recvx.at[p], peers)

    def unfold(v):
        turned = pltpu.roll(v, HALF, 1)
        return jnp.where(low, v, turned), jnp.where(low, turned, v)

    for p in range(count):
        s, l, t = p // (n_line * n_tm), p // n_tm % n_line, p % n_tm
        v = recvx[p].astype(F32)
        top = (l * shots + s) * lc
        for j in range(tl // tile):
            h, c = divmod(j * tile, tl // 2)
            two = unfold(v[h * lc : (h + 1) * lc, c : c + tile])
            for n in range(2):
                xs[t * each + 2 * j + n, top : top + lc, :] = two[n]
    arrival(1, sendm, recvm.at[n_line - 1 - at_line], other).wait_recv()
    for l in range(n_line):
        v = recvm[l].astype(F32)
        for g in range(n_mix):
            for j in range(blocks // 2):
                two = unfold(v[g * lc : (g + 1) * lc, j * tile : (j + 1) * tile])
                for n in range(2):
                    mx[2 * j + n, g * n_line + l] = two[n]

    per = n_line * shots * lc
    cube = (n_line * shots, lc, tile)
    clow = lax.rem(iota(cube, 2), 2 * HALF) < HALF
    line_of = iota(cube, 1)
    early = lax.rem(iota((per, tile), 1), HALF) < HALF // 2

    def beside(before, here, after):
        both = jnp.where(clow, before, here)
        return jnp.concatenate([both.reshape(per, tile), after.reshape(per, tile)], axis=1)

    def change(b):
        return ys[b + 1, :, :tile] + jnp.where(early, ys[b, :, tile:], ys[b + 2, :, tile:])

    none = jnp.zeros((shots, lc, tile), F32)
    one = none[:1]
    group = []
    for s in range(shots):
        found = jnp.int32(0)
        for k in range(shots):
            found = jnp.where(order[k] == s, k // run, found)
        group.append(found)
    rest = [lax.rem(lags[s], HALF) for s in range(shots)]

    def iterate(it, carry):
        def lines(b, carry):
            x = xs[b].reshape(cube)
            down, up = pltpu.roll(x, 1, 1), pltpu.roll(x, lc - 1, 1)
            before = jnp.where(line_of == 0, jnp.concatenate([none, down[: per // lc - shots]], axis=0), down)
            after = jnp.where(line_of == lc - 1, jnp.concatenate([up[shots:], none], axis=0), up)
            pn[b + 1] = beside(before, x, after)
            return carry

        lax.fori_loop(0, blocks, lines, 0)
        widen(pn, zs)
        layers(zs, hs, gs, ys, *ta)

        def passed(b, energy):
            x = (xs[b] + change(b)).astype(BF16).astype(F32)
            xs[b] = x
            return energy + jnp.sum((x * x).reshape(n_line, shots, lc, tile), axis=1)

        energy = lax.fori_loop(0, blocks, passed, jnp.zeros((n_line, lc, tile), F32))
        mine = jnp.zeros((lc, tile), F32)
        for l in range(n_line):
            e = 0.5 * jnp.sum(energy[l], axis=1, keepdims=True)
            mine = mine + jnp.where(lane == iota((lc, tile), 0) + l * lc, e, 0.0)
        mine = jnp.sum(mine, axis=0, keepdims=True)
        sende[it] = mine
        recve[it, me] = mine
        for to in peers:
            send(2 + it, sende.at[it], recve.at[it, me], to).start()
        wait_all(2 + it, lambda p: sende.at[it], lambda p: recve.at[it, p], peers)
        sent_all(2 + it, lambda p: sende.at[it], lambda p: recve.at[it, me], peers)
        total = jnp.zeros((lc, tile), F32)
        for k in range(count):
            total = total + member[k] * recve[it, k]
        total = total * scale
        rms, inv = [], []
        for l in range(n_line):
            mean = jnp.sum(jnp.where(lane // lc == l, total, 0.0), axis=1, keepdims=True)
            root = jnp.broadcast_to(jnp.sqrt(mean + EPSILON), (lc, tile)).reshape(1, lc, tile)
            rms += [root] * shots
            inv += [1.0 / root] * shots
        rms, inv = jnp.concatenate(rms, axis=0), jnp.concatenate(inv, axis=0)

        def stations(b, carry):
            x = (xs[b].reshape(cube) * inv).astype(BF16).astype(F32)
            before, after = [], []
            for l in range(n_line):
                at = x[l * shots : (l + 1) * shots]
                before += [one, at[: shots - 1]]
                after += [at[1:], one]
            pn[b + 1] = beside(jnp.concatenate(before, axis=0), x, jnp.concatenate(after, axis=0))
            return carry

        lax.fori_loop(0, blocks, stations, 0)
        widen(pn, zs)
        layers(zs, hs, gs, ys, *tb)

        def settle(b, carry):
            x = xs[b].reshape(cube) + rms * change(b).reshape(cube)
            x = x.astype(BF16).astype(F32)
            xs[b] = x.reshape(per, tile)
            for n in range(n_line * shots):
                rolled[b + 2, n] = pltpu.roll(x[n], rest[n % shots], 1)
            return carry

        lax.fori_loop(0, blocks, settle, 0)
        for g in range(n_mix):
            for l in range(n_line):
                acc = -mx[:, g * n_line + l]
                for i in range(run):
                    s = order[g * run + i]
                    lag = lags[s]
                    a = 2 - lag // HALF
                    near = rolled[pl.ds(a, blocks), l * shots + s]
                    far = rolled[pl.ds(a - 1, blocks), l * shots + s]
                    acc = acc + jnp.where((inner >= lax.rem(lag, HALF))[None], near, far)
                mf[:blocks, g * n_line + l] = acc
        for s in range(shots):
            for l in range(n_line):
                m = mf[:, group[s] * n_line + l]
                m = pltpu.roll(m, lax.rem(tile - rest[s], tile), 2)
                rolled[: blocks + 2, l * shots + s] = m
        for s in range(shots):
            for l in range(n_line):
                a = lags[s] // HALF
                near = rolled[pl.ds(a, blocks), l * shots + s]
                far = rolled[pl.ds(a + 1, blocks), l * shots + s]
                back = jnp.where((inner < HALF - rest[s])[None], near, far)
                top = (l * shots + s) * lc
                xs[:, top : top + lc, :] = (xs[:, top : top + lc, :] - pace[it] * back).astype(BF16).astype(F32)
        rolled[:2] = jnp.zeros_like(rolled[:2])
        return carry

    lax.fori_loop(0, ITERS, iterate, 0)

    for p in range(count):
        s, l, t = p // (n_line * n_tm), p // n_tm % n_line, p % n_tm
        top = (l * shots + s) * lc
        halves = []
        for j in range(tl // tile):
            b = t * each + 2 * j
            halves.append(jnp.where(low, xs[b, top : top + lc, :], xs[b + 1, top : top + lc, :]))
        n = len(halves) // 2
        halves = [jnp.concatenate(halves[:n], axis=1), jnp.concatenate(halves[n:], axis=1)]
        backs[p] = jnp.concatenate(halves, axis=0).astype(BF16)
    for to in peers:
        send(2 + ITERS, backs.at[to], backr.at[me], to).start()
    backr[me] = backs[me]
    wait_all(2 + ITERS, lambda p: backs.at[p], lambda p: backr.at[p], peers)
    v = []
    for k in range(count):
        part = backr[k].astype(F32)
        v.append(jnp.concatenate([part[:lc], part[lc:]], axis=1))
    v = jnp.concatenate(v, axis=0).astype(BF16)
    row, col = iota((recv_n, recv_n), 0), iota((recv_n, recv_n), 1)
    perm = jnp.where(row == lax.rem(col, lc) * count + col // lc, 1.0, 0.0).astype(BF16)
    out[0] = jnp.dot(perm, v, preferred_element_type=F32).astype(BF16)
    sent_all(0, lambda p: sendx.at[p], lambda p: recvx.at[me], peers)
    send(1, sendm, recvm.at[at_line], other).wait_send()
    sent_all(2 + ITERS, lambda p: backs.at[p], lambda p: backr.at[me], peers)


def patch(guess, mixtures, lags, order, tallies, wa, wb, pace, sizes):
    count = math.prod(sizes)
    n_shot, n_line, n_tm = sizes
    recv, tl = guess.shape[1:]
    n_mix, nt = mixtures.shape[0], mixtures.shape[2]
    lc, tile = recv // count, 2 * HALF
    blocks, traces = nt // HALF, n_line * n_shot
    per, feat = traces * lc, wa[0].shape[2]
    wide = feat * len(SLOT)
    rows = blocks * per
    v, s, h = (pl.BlockSpec(memory_space=m) for m in (pltpu.VMEM, pltpu.SMEM, pl.ANY))
    slab = pltpu.VMEM((count, 2 * lc, tl // 2), BF16)
    woven = [
        pltpu.VMEM((2 * GROUPS, wide, wide), BF16),
        pltpu.VMEM((2 * wide, wide), BF16),
        pltpu.VMEM((2 * GROUPS * wide, wide), BF16),
        pltpu.VMEM((2, wide), F32),
    ]
    kinds = 3 + ITERS
    return pl.pallas_call(
        functools.partial(patch_kernel, sizes),
        out_shape=jax.ShapeDtypeStruct(guess.shape, BF16),
        in_specs=[s] * 4 + [h] * 2 + [v] * 8,
        out_specs=v,
        scratch_shapes=[
            pltpu.VMEM((recv, tl), BF16),
            pltpu.VMEM(mixtures.shape, BF16),
            slab,
            slab,
            pltpu.VMEM((n_mix * lc, nt), BF16),
            pltpu.VMEM((n_line, n_mix * lc, nt), BF16),
            slab,
            slab,
            pltpu.VMEM((ITERS, 1, tile), F32),
            pltpu.VMEM((ITERS, count, 1, tile), F32),
            pltpu.VMEM((blocks, per, tile), F32),
            pltpu.VMEM((blocks, n_mix * n_line, lc, tile), F32),
            pltpu.VMEM((blocks + 2, traces, lc, tile), F32),
            pltpu.VMEM((blocks + 2, n_mix * n_line, lc, tile), F32),
            pltpu.VMEM((count, lc, tile), F32),
            pltpu.VMEM((blocks + 2, per, wide), F32),
            pltpu.VMEM((2, rows, wide), BF16),
            pltpu.VMEM((2, GROUPS * rows + 2 * per, wide), BF16),
            pltpu.VMEM((rows, 2 * GROUPS * wide), BF16),
            pltpu.VMEM((blocks + 2, per, wide), F32),
            *woven,
            *woven,
            pltpu.SemaphoreType.DMA((2,)),
            pltpu.SemaphoreType.DMA((kinds, count)),
            pltpu.SemaphoreType.DMA((kinds, count)),
        ],
        compiler_params=pltpu.CompilerParams(vmem_limit_bytes=56 * 2**20, collective_id=1, has_side_effects=True),
    )(lags, order, tallies, pace, guess, mixtures, *wa, *wb)


def per_device(guess, mixtures, lags, order, tallies, e1, m1, x1, b1, e2, m2, x2, b2, pace):
    sh, recv, tl = guess.shape
    n_shot, n_line, n_tm = (lax.axis_size(a) for a in AXES)
    whole = RPL % (n_shot * n_line * n_tm) == 0
    where = AXES if whole else AXES[1:]
    parts = math.prod(lax.axis_size(a) for a in where)
    kp, lh = RPL // parts, recv // RPL
    lines, shots, nt = lh * n_line, sh * n_shot, tl * n_tm
    planes, s1 = nt // 2 // C, shots if whole else sh
    r1 = lines * kp
    r2 = r1 if whole else r1 // n_shot
    lanes1, lanes2 = 2 * s1 * r1, 2 * shots * r2
    sources = n_shot if whole else 1
    i32 = functools.partial(jnp.arange, dtype=jnp.int32)
    n_mix, feat = mixtures.shape[0], e1.shape[2]
    square = sh == 1 and kp == 1 and n_line == 2 and shots % n_mix == 0 and feat == HALF
    square = square and lh == C and tl % (4 * HALF) == 0 and n_mix * lh % 16 == 0
    square = square and lines == parts and 2 * (n_mix // n_line) == n_line
    if square:
        sizes = (n_shot, n_line, n_tm)
        return patch(guess, mixtures, lags, order, tallies, (e1, m1, x1, b1), (e2, m2, x2, b2), pace, sizes)

    at_shot = lax.axis_index("shot")
    n_mix, run = mixtures.shape[0], nt // C
    fused = whole and sh == 1 and kp == 1 and C % n_tm == 0 and n_shot * n_tm == C
    x = guess.reshape(sh, lh, parts, kp, tl).transpose(2, 0, 1, 3, 4)
    if fused:
        share = (at_shot * n_tm + lax.axis_index("tm")) * run
        mine = lax.dynamic_slice_in_dim(mixtures, share, run, axis=2).reshape(n_mix, lh, parts, run)
        mine = mine.transpose(2, 1, 0, 3).reshape(parts, lh, n_mix * run)
        x = jnp.concatenate([x.reshape(parts, lh, tl), mine], axis=2)
    x = lax.all_to_all(x, where, split_axis=0, concat_axis=0, tiled=False)
    if not fused:
        x = x.reshape(sources, n_line, n_tm, sh, lh, kp, tl).transpose(0, 3, 1, 4, 5, 2, 6)
        x = x.reshape(s1, r1, C, planes, 2).transpose(3, 2, 4, 0, 1).reshape(planes, C, lanes1)


    def first_k(line):
        block = line * n_tm + lax.axis_index("tm")
        return (at_shot * n_line * n_tm + block if whole else block) * kp

    if not fused:
        grid = mixtures.reshape(n_mix, lh, RPL, nt)
        sent = jnp.stack([lax.dynamic_slice_in_dim(grid, first_k(d), kp, axis=2) for d in range(n_line)])
        m = lax.all_to_all(sent, "line", split_axis=0, concat_axis=0)
        m = m.transpose(1, 0, 2, 3, 4).reshape(n_mix, r1, nt)
        if not whole:
            m = lax.dynamic_slice_in_dim(m, at_shot * r2, r2, axis=1)
        m = m.reshape(n_mix, r2, C, planes, 2).transpose(3, 2, 4, 0, 1).reshape(planes * C, 2 * n_mix * r2)

    np_ = tallies.shape[0]
    here = i32(np_)
    offsets = jnp.sum(jnp.where(here[None, :] < here[:, None], tallies[None, :], 0), axis=1)
    mine = first_k(lax.axis_index("line"))

    def one_hot(r):
        line, k = r // kp, mine + lax.rem(r, kp)
        q = lax.rem(line, lh) * RPL + k
        inside = (offsets[:, None] <= q[None, :]) & (q[None, :] < (offsets + tallies)[:, None])
        block = (line // lh)[None, :] == i32(n_line)[:, None]
        return (block[:, None, :] & inside[None, :, :]).reshape(n_line * np_, r.shape[0]).astype(F32)

    member = jnp.tile(one_hot(i32(r1)), (1, 2 * s1))
    r_own = i32(r2) if whole else at_shot * r2 + i32(r2)
    count = jnp.tile((tallies * (shots * nt)).astype(F32), n_line)
    spread = jnp.tile(one_hot(r_own) / count[:, None], (1, 2 * shots))

    sid = i32(shots)
    place = jnp.sum(jnp.where(order[None, :] == sid[:, None], sid[None, :], 0), axis=1)
    group = place // (shots // n_mix)
    same = (group[:, None] == group[None, :]).astype(BF16)
    chosen = (i32(n_mix)[:, None] == group[None, :]).astype(BF16)
    rest, two = jnp.eye(r2, dtype=BF16), jnp.eye(2, dtype=BF16)
    join = jnp.kron(two, jnp.kron(same, rest))
    take = jnp.kron(two, jnp.kron(chosen, rest))

    n1, n2 = s1 * r1, shots * r2
    a, b = np.arange(n1)[:, None], np.arange(n1)[None, :]
    near1 = np.stack([(a == b + (c - 1) * kp) & (a // r1 == b // r1) for c in range(3)])
    a, b = np.arange(n2)[:, None], np.arange(n2)[None, :]
    near2 = np.stack([a == b + (c - 1) * r2 for c in range(3)])
    wa = prepared(e1, m1, x1, b1, near1)
    wb = prepared(e2, m2, x2, b2, near2)

    rows = planes * C
    tot1, tot2 = pltpu.VMEM((rows, 2 * lanes1), F32), pltpu.VMEM((rows, 2 * lanes2), F32)
    feat = e1.shape[2]
    band = pltpu.VMEM((3 * PACK * feat, PACK * feat), BF16)
    buf = pltpu.VMEM((2, 2 * planes, C, lanes2), F32)
    spass = jax.ShapeDtypeStruct((planes, C, lanes1), BF16)
    part = jax.ShapeDtypeStruct((n_line * np_, 128), F32)
    moved = jax.ShapeDtypeStruct((planes, C, lanes2), BF16)

    def to_stations(y):
        y = y.reshape(rows, 2, sh, n_shot, r2)
        y = lax.all_to_all(y, "shot", split_axis=3, concat_axis=2, tiled=True)
        return y.reshape(planes, C, lanes2)

    def to_shots(y):
        y = y.reshape(rows, 2, shots, 1, r2)
        y = lax.all_to_all(y, "shot", split_axis=2, concat_axis=3, tiled=True)
        return y.reshape(planes, C, lanes1)

    dims = (n_shot, n_line, n_tm)
    cube = pltpu.VMEM((planes, C, lanes1), F32)
    if fused:
        mixed = jax.ShapeDtypeStruct((rows, 2 * n_mix * r2), BF16)
        side = pltpu.VMEM((planes, C, 2 * n_mix * r2), F32)
        sp, energy, m = call(
            functools.partial(entry_kernel, dims),
            (spass, part, mixed),
            (x, *wa, member),
            0,
            [tot1, band, cube, side],
        )
    else:
        sp, energy = call(first_kernel, (spass, part), (x, *wa, member), 0, [tot1, band])
    for it in range(ITERS):
        tot = summed(energy, (n_shot, n_line, n_tm)) if whole else lax.psum(energy, AXES)
        if not whole:
            sp = to_stations(sp)
        ins = (lags, pace, sp, tot, spread, *wb, join, m, take)
        if whole and it < ITERS - 1:
            sp, energy = call(
                functools.partial(both_kernel, it, shots), (spass, part), (*ins, *wa, member), 2, [buf, tot2, band]
            )
            continue
        if fused:
            back = jax.ShapeDtypeStruct((parts, lh, tl), BF16)
            x = call(functools.partial(exit_kernel, it, dims), back, ins, 2, [buf, tot2, band, cube])
            continue
        x = call(functools.partial(station_kernel, it, shots), moved, ins, 2, [buf, tot2, band])
        if not whole:
            x = to_shots(x)
            if it < ITERS - 1:
                sp, energy = call(first_kernel, (spass, part), (x, *wa, member), 0, [tot1, band])

    if not fused:
        x = x.reshape(planes, C, 2, s1, r1).transpose(3, 4, 1, 0, 2)
        x = x.reshape(sources, sh, n_line, lh, kp, n_tm, tl).transpose(0, 2, 5, 1, 3, 4, 6)
    x = lax.all_to_all(x.reshape(parts, sh, lh, kp, tl), where, split_axis=0, concat_axis=0)
    return x.transpose(1, 2, 0, 3, 4).reshape(sh, recv, tl)


def solution(mesh):
    spec = P(("group", "shot"), "line", "tm")
    placed = (spec, P("group", "line", None), P("group"), P("group"), P("group")) + (P(),) * 9
    return jax.shard_map(per_device, mesh=mesh, in_specs=placed, out_specs=spec, check_vma=False)
```

```python
import functools
import math

import jax
import jax.numpy as jnp
import numpy as np
from jax import lax
from jax.experimental import pallas as pl
from jax.experimental.pallas import tpu as pltpu
from jax.sharding import PartitionSpec as P

RPL = 16
ITERS = 2
EPSILON = 1e-05
C = 8
PACK = 4
TAPS = (1, 2, 3, 0)
F32, BF16 = jnp.float32, jnp.bfloat16
AXES = ("shot", "line", "tm")


def ahead(x, k):
    edge = pltpu.roll(x[:k], C - 1, 1)
    edge = jnp.where(lax.broadcasted_iota(jnp.int32, edge.shape, 1) == C - 1, 0.0, edge)
    return edge if k == x.shape[0] else jnp.concatenate([x[k:], edge], axis=0)


def behind(x, k):
    edge = pltpu.roll(x[x.shape[0] - k :], 1, 1)
    edge = jnp.where(lax.broadcasted_iota(jnp.int32, edge.shape, 1) == 0, 0.0, edge)
    return edge if k == x.shape[0] else jnp.concatenate([edge, x[: x.shape[0] - k]], axis=0)


def even_lanes(shape):
    return lax.broadcasted_iota(jnp.int32, shape, len(shape) - 1) < shape[-1] // 2


def net(x, w_in, pick, w_mid, w_out, place, bias, total, band):
    planes, _, lanes = x.shape
    rows = planes * C
    side = jnp.where(even_lanes(x.shape), ahead(x, 1), behind(x, 1))
    z = jnp.concatenate([x, side], axis=2).astype(BF16).reshape(rows, 2 * lanes)
    total[...] = jnp.zeros_like(total)
    wide = w_in.shape[1]
    feat = wide // PACK
    for j in range(3):
        tap = w_mid[j].astype(F32)
        for i in range(PACK):
            row = [tap if p == i else jnp.zeros_like(tap) for p in range(PACK)]
            at = (j * PACK + i) * feat
            band[at : at + feat, :] = jnp.concatenate(row, axis=1).astype(BF16)

    def step(q, carry):
        w_here = jnp.dot(pick[q], w_in[...], preferred_element_type=F32).astype(BF16)
        o_here = jnp.dot(w_out[...], place[q], preferred_element_type=F32).astype(BF16)
        h = jnp.dot(z, w_here, preferred_element_type=F32)
        h = jnp.maximum(h + bias[0:1, :], 0.0)
        cube = h.reshape(planes, C, wide)
        first = ahead(cube[:2], 2).reshape(2 * C, wide).astype(BF16)
        last = behind(cube[planes - 2 :], 2).reshape(2 * C, wide).astype(BF16)
        hb = h.astype(BF16)
        early = jnp.concatenate([last, hb[: rows - 2 * C]], axis=0)
        late = jnp.concatenate([hb[2 * C :], first], axis=0)
        g = jnp.dot(jnp.concatenate([early, hb, late], axis=1), band[...], preferred_element_type=F32)
        g = jnp.maximum(g + bias[1:2, :], 0.0).astype(BF16)
        total[...] += jnp.dot(g, o_here, preferred_element_type=F32)
        return carry

    lax.fori_loop(0, pick.shape[0], step, 0, unroll=2)
    y = total[...].reshape(planes, C, 2 * lanes)
    a, b = y[:, :, :lanes], y[:, :, lanes:]
    return a + jnp.where(even_lanes(b.shape), behind(b, 1), ahead(b, 1))


def shot_step(x, weights, member, out_ref, part_ref, total, band):
    y = (x + net(x, *weights, total, band)).astype(BF16)
    out_ref[...] = y
    y = y.astype(F32)
    energy = jnp.sum(jnp.sum(y * y, axis=0), axis=0, keepdims=True)
    sums = jnp.sum(member[...] * energy, axis=1, keepdims=True)
    part_ref[...] = jnp.broadcast_to(sums, part_ref.shape)


def shifted(buf, lag_ref, shots, forward):
    planes, lanes = buf.shape[1] // 2, buf.shape[3]
    shape = (planes, C, lanes)
    even = even_lanes(shape)
    per = lanes // 2 // shots
    lane_shot = lax.rem(lax.broadcasted_iota(jnp.int32, shape, 2), lanes // 2) // per
    out = jnp.zeros(shape, F32)
    for s in range(shots):
        lag = lag_ref[s]
        half, odd = lag // 2, lax.rem(lag, 2)
        at_even = half if forward else planes - half - odd
        at_odd = half + odd if forward else planes - half
        one = jnp.where(even, buf[odd, pl.ds(at_even, planes)], buf[odd, pl.ds(at_odd, planes)])
        out = jnp.where(lane_shot == s, one, out)
    return out


def station_step(shots, sp, tot_ref, spread, weights, lags, join, mix, take, pace, buf, total, band):
    planes, _, lanes = sp.shape
    rows = planes * C
    mean = jnp.sum(tot_ref[:, 0:1] * spread[...], axis=0, keepdims=True)
    rms = jnp.sqrt(mean + EPSILON).reshape(1, 1, lanes)
    normed = (sp / rms).astype(BF16).astype(F32)
    settled = (sp + rms * net(normed, *weights, total, band)).astype(BF16).astype(F32)

    def fill(x, forward):
        far = ahead(x, planes) if forward else behind(x, planes)
        near_at, far_at = (0, planes) if forward else (planes, 0)
        for v, at in ((x, near_at), (far, far_at)):
            buf[0, at : at + planes] = v
            h = lanes // 2
            buf[1, at : at + planes] = jnp.concatenate([v[:, :, h:], v[:, :, :h]], axis=2)

    fill(settled, False)
    fired = shifted(buf, lags, shots, False).astype(BF16).reshape(rows, lanes)
    misfit = jnp.dot(fired, join[...], preferred_element_type=F32)
    misfit -= jnp.dot(mix[...], take[...], preferred_element_type=F32)
    fill(misfit.reshape(planes, C, lanes), True)
    return (settled - pace * shifted(buf, lags, shots, True)).astype(BF16)


def by_phase(width):
    row = lax.broadcasted_iota(jnp.int32, (width, width), 0)
    col = lax.broadcasted_iota(jnp.int32, (width, width), 1)
    half = width // 2
    return jnp.where(col == 2 * lax.rem(row, half) + row // half, 1.0, 0.0).astype(BF16)


def unfold(read, into, sort):
    planes = into.shape[0]
    for c in range(C):
        v = lax.dot_general(sort, read(c), (((1,), (1,)), ((), ())), preferred_element_type=F32)
        into[:, c, :] = jnp.concatenate([v[:planes], v[planes:]], axis=1)


def entry_kernel(
    dims, x, wi, wp, wm, wo, wq, bi, member, out, part, mix, total, band, cube, side
):
    shots, blocks, halves = dims
    width = 2 * cube.shape[0]
    sort, each = by_phase(width), C // halves

    def traces(c):
        at, t = slice(c % each * width, (c % each + 1) * width), c // each
        rows = [x[(s * blocks + b) * halves + t, :, at].astype(F32) for s in range(shots) for b in range(blocks)]
        return jnp.concatenate(rows, axis=0).astype(BF16)

    tl = each * width

    def records(c):
        s, t = c // halves, c % halves
        rows = [
            x[(s * blocks + b) * halves + t, :, tl + g * width : tl + (g + 1) * width].astype(F32)
            for g in range((x.shape[2] - tl) // width)
            for b in range(blocks)
        ]
        return jnp.concatenate(rows, axis=0).astype(BF16)

    unfold(records, side, sort)
    mix[...] = side[...].astype(BF16).reshape(mix.shape)
    unfold(traces, cube, sort)
    shot_step(cube[...], (wi, wp, wm, wo, wq, bi), member, out, part, total, band)


def exit_kernel(
    it, dims, lags, pace, sp, tot, spread, wi, wp, wm, wo, wq, bi, join, mix, take, out, buf, total, band, cube
):
    shots, blocks, halves = dims
    width = 2 * cube.shape[0]
    sort, each = by_phase(width), C // halves
    x = station_step(
        shots, sp[...].astype(F32), tot, spread, (wi, wp, wm, wo, wq, bi), lags, join, mix, take, pace[it], buf, total, band
    )
    cube[...] = x.astype(F32)
    n, lh = cube.shape[2] // 2, out.shape[1]
    for c in range(C):
        v = cube[:, c, :]
        v = jnp.concatenate([v[:, :n], v[:, n:]], axis=0).T.astype(BF16)
        v = jnp.dot(v, sort, preferred_element_type=F32)
        at, t = slice(c % each * width, (c % each + 1) * width), c // each
        for j in range(shots * blocks):
            out[j * halves + t, :, at] = v[j * lh : (j + 1) * lh].astype(BF16)


def first_kernel(x, wi, wp, wm, wo, wq, bi, member, out, part, total, band):
    shot_step(x[...].astype(F32), (wi, wp, wm, wo, wq, bi), member, out, part, total, band)


def station_kernel(it, shots, lags, pace, sp, tot, spread, wi, wp, wm, wo, wq, bi, join, mix, take, out, buf, total, band):
    out[...] = station_step(
        shots, sp[...].astype(F32), tot, spread, (wi, wp, wm, wo, wq, bi), lags, join, mix, take, pace[it], buf, total, band
    )


def both_kernel(
    it, shots, lags, pace, sp, tot, spread, wi, wp, wm, wo, wq, bi, join, mix, take, vi, vp, vm, vo, vq, ci, member, out, part, buf, total, band
):
    x = station_step(
        shots, sp[...].astype(F32), tot, spread, (wi, wp, wm, wo, wq, bi), lags, join, mix, take, pace[it], buf, total, band
    )
    shot_step(x.astype(F32), (vi, vp, vm, vo, vq, ci), member, out, part, total, band)


def call(body, outs, ins, smem, scratch):
    v, s = pl.BlockSpec(memory_space=pltpu.VMEM), pl.BlockSpec(memory_space=pltpu.SMEM)
    return pl.pallas_call(
        body,
        out_shape=outs,
        in_specs=[s] * smem + [v] * (len(ins) - smem),
        out_specs=jax.tree.map(lambda _: v, outs),
        scratch_shapes=scratch,
        compiler_params=pltpu.CompilerParams(vmem_limit_bytes=48 * 2**20),
    )(*ins)


def prepared(w_in, w_mid, w_out, bias, near):
    n, feat = near.shape[1], w_in.shape[2]
    tiles = n // PACK
    cols = near.reshape(3, n, tiles, PACK).transpose(2, 1, 0, 3)
    pick = np.einsum("jk,tnci->tjnkci", np.eye(4)[list(TAPS)], cols).reshape(tiles, 4 * n, 12 * PACK)
    place = np.einsum("kj,tin->tjikn", np.eye(4)[list(TAPS)], np.eye(n).reshape(tiles, PACK, n)).reshape(tiles, 4 * PACK, 4 * n)
    w1 = w_in.reshape(12, 1, 1, feat)
    eye = jnp.eye(PACK, dtype=BF16)
    rows = (w1 * eye[None, :, :, None]).reshape(12 * PACK, PACK * feat)
    w2 = w_out.T.reshape(1, feat, 4, 1)
    ends = (w2 * eye[:, None, None, :]).reshape(PACK * feat, 4 * PACK)
    return rows, jnp.asarray(pick, BF16), w_mid, ends, jnp.asarray(place, BF16), jnp.tile(bias, (1, PACK))


def exchange_kernel(sizes, x, out, slots, send, recv):
    count = math.prod(sizes)
    me = (lax.axis_index("shot") * sizes[1] + lax.axis_index("line")) * sizes[2] + lax.axis_index("tm")

    def peer(off):
        at = lax.rem(me + off, count)
        return {
            "shot": at // (sizes[1] * sizes[2]),
            "line": lax.rem(at // sizes[2], sizes[1]),
            "tm": lax.rem(at, sizes[2]),
        }

    barrier = pltpu.get_barrier_semaphore()
    for off in range(1, count):
        pl.semaphore_signal(barrier, inc=1, device_id=peer(off), device_id_type=pl.DeviceIdType.MESH)
    pl.semaphore_wait(barrier, count - 1)
    copies = []
    for off in range(1, count):
        copy = pltpu.make_async_remote_copy(
            src_ref=x,
            dst_ref=slots.at[off],
            send_sem=send.at[off],
            recv_sem=recv.at[off],
            device_id=peer(off),
            device_id_type=pl.DeviceIdType.MESH,
        )
        copy.start()
        copies.append(copy)
    total = x[...]
    for off, copy in enumerate(copies, 1):
        copy.wait()
        total += slots[off]
    out[...] = total


def summed(x, sizes):
    count, v = math.prod(sizes), pl.BlockSpec(memory_space=pltpu.VMEM)
    return pl.pallas_call(
        functools.partial(exchange_kernel, sizes),
        out_shape=jax.ShapeDtypeStruct(x.shape, x.dtype),
        in_specs=[v],
        out_specs=v,
        scratch_shapes=[
            pltpu.VMEM((count, *x.shape), x.dtype),
            pltpu.SemaphoreType.DMA((count,)),
            pltpu.SemaphoreType.DMA((count,)),
        ],
        compiler_params=pltpu.CompilerParams(collective_id=0, has_side_effects=True),
    )(x)


SLOT = (0, 3, 1, 2)
HALF = 64
GROUPS = 4


def iota(shape, dim):
    return lax.broadcasted_iota(jnp.int32, shape, dim)


def weave(w_in, w_mid, w_out, bias, we, wm, wo, bi):
    feat = w_in.shape[2]
    wide = feat * len(SLOT)
    row, lane = iota((wide, wide), 0), iota((wide, wide), 1)
    at, ch = lax.rem(row, HALF), row // HALF
    slot = lane // feat
    pos = jnp.where(slot == 1, 3, jnp.where(slot == 0, 0, slot - 1))
    taps = w_in[...].astype(F32)
    for par in range(2):
        turned = lax.rem(at + (1 if par == 0 else HALF - 1), HALF)
        tap = lax.rem(turned, 4)
        base = jnp.zeros((wide, wide), F32)
        for c in range(3):
            for t in range(4):
                line = jnp.concatenate([taps[c, t : t + 1, :]] * len(SLOT), axis=1)
                base = jnp.where((ch == c) & (tap == t), line, base)
        for g in range(GROUPS):
            we[par * GROUPS + g] = jnp.where(turned // 4 == 4 * g + pos, base, 0.0).astype(BF16)
    zero = jnp.zeros((feat, feat), F32)
    mid = [w_mid[j].astype(F32) for j in range(3)]

    def block(came, goes):
        j = came - goes + 1
        return mid[j] if 0 <= j < 3 else zero

    for n, came in enumerate(SLOT):
        blocks = [block(came, goes) for goes in SLOT]
        wm[0, n * feat : (n + 1) * feat, :] = jnp.concatenate(blocks, axis=1).astype(BF16)
    for n in range(4):
        blocks = [zero] * 4
        blocks[n ^ 1] = mid[2 if n % 2 == 0 else 0]
        wm[1, n * feat : (n + 1) * feat, :] = jnp.concatenate(blocks, axis=1).astype(BF16)

    def sample(shape):
        col = iota(shape, 1)
        m = lax.rem(col, HALF)
        edge = jnp.where(m == HALF - 1, -1, jnp.where(m == 0, HALF, -4 * HALF))
        return jnp.where(col >= 2 * HALF, edge, m)

    near, far = sample((4, wide)), sample((feat, wide))
    for par in range(2):
        pick = jnp.where(lax.rem(near - 2 * par + 1 + 8 * HALF, 4) == iota((4, wide), 0), 1.0, 0.0).astype(BF16)
        base = lax.dot_general(w_out[...], pick, (((0,), (0,)), ((), ())), preferred_element_type=F32)
        for g in range(GROUPS):
            for n, i in enumerate(SLOT):
                d = far - 4 * (4 * g + i) - 2 * par + 1
                at = ((par * GROUPS + g) * len(SLOT) + n) * feat
                wo[at : at + feat, :] = jnp.where((d >= 0) & (d < 4), base, 0.0).astype(BF16)
    bi[...] = jnp.concatenate([bias[...]] * len(SLOT), axis=1)


def layers(zs, hs, gs, ys, we, wm, wo, bi):
    b0, b1 = bi[0:1, :], bi[1:2, :]
    rows, wide = zs.shape[1:]
    blocks = ys.shape[0] - 2
    per, half = rows // blocks, wide // 2
    for par in range(2):
        for g in range(GROUPS):
            h = jnp.dot(zs[par], we[par * GROUPS + g], preferred_element_type=F32)
            h = jnp.maximum(h + b0, 0.0).astype(BF16)
            for b in range(blocks):
                at = per + (b * GROUPS + g) * per
                hs[par, at : at + per, :] = h[b * per : (b + 1) * per]
    low = iota((rows, half), 1) < half // 2
    for r in range(per, per + GROUPS * rows, rows):
        edge = [jnp.where(low, hs[par, r + per : r + per + rows, :half], hs[par, r - per : r - per + rows, :half]) for par in range(2)]
        edge = jnp.dot(jnp.concatenate(edge, axis=1), wm[1], preferred_element_type=F32)
        for par in range(2):
            g = jnp.dot(hs[par, r : r + rows, :], wm[0], preferred_element_type=F32)
            ends = g[:, :half] + edge[:, par * half : (par + 1) * half]
            g = [jnp.maximum(ends + b1[:, :half], 0.0), jnp.maximum(g[:, half:] + b1[:, half:], 0.0)]
            for n in range(rows // per):
                b, q = divmod(r // per - 1 + n, GROUPS)
                for i in range(2):
                    col = (par * GROUPS + q) * wide + i * half
                    gs[b * per : (b + 1) * per, col : col + half] = g[i][n * per : (n + 1) * per].astype(BF16)
    y = jnp.dot(gs[...], wo[...], preferred_element_type=F32)
    ys[1 : 1 + blocks] = y.reshape(blocks, per, wide)


def patch_kernel(sizes, lags, order, tallies, pace, guess, mixtures, *refs):
    given, out = refs[:8], refs[8]
    (gbuf, mbuf, sendx, recvx, sendm, recvm, backs, backr, sende, recve) = refs[9:19]
    (xs, ps, mx, rolled, mf, member, zs, hs, gs, ys) = refs[19:29]
    ta, tb, held = refs[29:33], refs[33:37], refs[37:45]
    load_sem, ssem, rsem = refs[45:]
    n_shot, n_line, n_tm = sizes
    count = math.prod(sizes)
    axes = [lax.axis_index(a) for a in AXES]
    turns = [[axes[i]] + [lax.rem(axes[i] + d, n) for d in range(1, n)] for i, n in enumerate(sizes)]
    at_shot, at_line, at_tm = axes

    def number(s, l, t):
        return (s * n_line + l) * n_tm + t

    def device(s, l, t):
        return {"shot": s, "line": l, "tm": t}

    me = number(*axes)
    peers = [(s, l, t) for s in turns[0] for l in turns[1] for t in turns[2]][1:]
    shots = n_shot
    n_mix = mixtures.shape[0]
    run = shots // n_mix
    recv_n, tl = guess.shape[1:]
    lc = recv_n // count
    tile = 2 * HALF
    blocks = tl * n_tm // HALF
    each = tl // HALF
    back_kind = 2 + ITERS * n_line

    barrier = pltpu.get_barrier_semaphore()
    for p in peers:
        pl.semaphore_signal(barrier, inc=1, device_id=device(*p), device_id_type=pl.DeviceIdType.MESH)
    pairs = [(guess.at[0], gbuf), (mixtures, mbuf)] + list(zip(given, held))
    loads = [pltpu.make_async_copy(a, b, load_sem.at[i]) for i, (a, b) in enumerate(pairs)]
    for copy in loads:
        copy.start()

    def link(which, src, dst, to, came):
        return pltpu.make_async_remote_copy(
            src_ref=src,
            dst_ref=dst,
            send_sem=ssem.at[which, number(*to)],
            recv_sem=rsem.at[which, came],
            device_id=device(*to),
            device_id_type=pl.DeviceIdType.MESH,
        )

    row, col = iota((recv_n, recv_n), 0), iota((recv_n, recv_n), 1)
    perm = jnp.where(col == lax.rem(row, lc) * count + row // lc, 1.0, 0.0).astype(BF16)
    loads[0].wait()
    v = jnp.dot(perm, gbuf[...], preferred_element_type=F32)
    for k in range(count):
        part = v[k * lc : (k + 1) * lc]
        sendx[k] = jnp.concatenate([part[:, : tl // 2], part[:, tl // 2 :]], axis=0).astype(BF16)
    pl.semaphore_wait(barrier, count - 1)
    for p in peers:
        link(0, sendx.at[number(*p)], recvx.at[me], p, me).start()

    loads[1].wait()
    other = (at_shot, n_line - 1 - at_line, at_tm)
    row, col = iota((2 * lc, recv_n), 0), iota((2 * lc, recv_n), 1)
    wanted = jnp.where(row < lc, me, number(*other))
    pick = jnp.where(col == lax.rem(row, lc) * count + wanted, 1.0, 0.0).astype(BF16)
    picked = [jnp.dot(pick, mbuf[g], preferred_element_type=F32) for g in range(n_mix)]
    sendm[...] = jnp.concatenate([p[lc:] for p in picked], axis=0).astype(BF16)
    link(1, sendm, recvm.at[at_line], other, me).start()
    recvm[at_line] = jnp.concatenate([p[:lc] for p in picked], axis=0).astype(BF16)
    recvx[me] = sendx[me]

    for copy in loads[2:]:
        copy.wait()
    weave(*held[:4], *ta)
    weave(*held[4:], *tb)
    edges = hs.shape[1] - (GROUPS * blocks + 1) * (hs.shape[1] // (GROUPS * blocks + 2))
    hs[:, :edges] = jnp.zeros_like(hs[:, :edges])
    hs[:, hs.shape[1] - edges :] = jnp.zeros_like(hs[:, :edges])
    for ref in (ys, rolled, mf, xs):
        ref[0] = jnp.zeros_like(ref[0])
        ref[ref.shape[0] - 1] = jnp.zeros_like(ref[0])
    for ref, at in ((rolled, 1), (mf, blocks)):
        ref[at] = jnp.zeros_like(ref[at])
    sec = []
    for rows in ((lc, tile), (count, tile)):
        if rows[0] == lc:
            q = iota(rows, 0) * count + me
        else:
            q = lax.rem(iota(rows, 1), lc) * count + iota(rows, 0)
        edge, at, size = jnp.int32(0), jnp.zeros(rows, jnp.int32), jnp.zeros(rows, jnp.int32)
        for p in range(tallies.shape[0]):
            at = jnp.where(q >= edge, p, at)
            size = jnp.where(q >= edge, tallies[p], size)
            edge = edge + tallies[p]
        sec.append((at, size))
    scale = 1.0 / (sec[0][1] * (shots * tl * n_tm)).astype(F32)
    for k in range(count):
        member[k] = jnp.where(sec[0][0] == sec[1][0][k : k + 1, :], scale, 0.0)

    lane = iota((lc, tile), 1)
    low = lane < HALF
    inner = lax.rem(lane, HALF)

    def unfold(v):
        turned = pltpu.roll(v, HALF, 1)
        return jnp.where(low, v, turned), jnp.where(low, turned, v)

    for p in peers:
        link(0, sendx.at[number(*p)], recvx.at[number(*p)], p, number(*p)).wait_recv()
    for p in range(count):
        s, l, t = p // (n_line * n_tm), p // n_tm % n_line, p % n_tm
        v = recvx[p].astype(F32)
        for j in range(tl // tile):
            h, c = divmod(j * tile, tl // 2)
            two = unfold(v[h * lc : (h + 1) * lc, c : c + tile])
            for n in range(2):
                xs[1 + l, t * each + 2 * j + n, s] = two[n]
    link(1, sendm, recvm.at[n_line - 1 - at_line], other, number(*other)).wait_recv()
    for l in range(n_line):
        v = recvm[l].astype(F32)
        for g in range(n_mix):
            for j in range(blocks // 2):
                two = unfold(v[g * lc : (g + 1) * lc, j * tile : (j + 1) * tile])
                for n in range(2):
                    mx[2 * j + n, g * n_line + l] = two[n]

    cube = (shots, lc, tile)
    per = shots * lc
    clow = iota(cube, 2) < HALF
    line_of = iota(cube, 1)
    spot = lax.rem(iota((per, tile), 1), HALF)
    wide_spot = lax.rem(iota((per, 2 * tile), 1), HALF)
    early = spot < HALF // 2
    one = jnp.zeros((1, lc, tile), F32)
    nothing = jnp.zeros((per, 2 * tile), F32)

    def widen(make):
        ahead_of = [nothing, make(0)]
        for b in range(blocks):
            ahead_of.append(make(b + 1) if b + 1 < blocks else nothing)
            before, here, after = ahead_of[b : b + 3]
            zs[0, b * per : (b + 1) * per, :] = jnp.where(wide_spot == HALF - 1, before, here).astype(BF16)
            zs[1, b * per : (b + 1) * per, :] = jnp.where(wide_spot == 0, after, here).astype(BF16)

    def beside(before, here, after):
        both = jnp.where(clow, before, here)
        return jnp.concatenate([both.reshape(per, tile), after.reshape(per, tile)], axis=1)

    def change(b):
        return ys[b + 1, :, :tile] + jnp.where(early, ys[b, :, tile:], ys[b + 2, :, tile:])

    group = []
    for s in range(shots):
        found = jnp.int32(0)
        for k in range(shots):
            found = jnp.where(order[k] == s, k // run, found)
        group.append(found)
    rest = [lax.rem(lags[s], HALF) for s in range(shots)]
    far = [lags[s] // HALF for s in range(shots)]

    def over_lines(it, l):
        def make(b):
            x = xs[1 + l, b]
            before = jnp.where(line_of == lc - 1, xs[l, b], x)
            after = jnp.where(line_of == 0, xs[2 + l, b], x)
            return beside(pltpu.roll(before, 1, 1), x, pltpu.roll(after, lc - 1, 1))

        widen(make)
        layers(zs, hs, gs, ys, *ta)
        energy = jnp.zeros((lc, tile), F32)
        for b in range(blocks):
            x = (xs[1 + l, b] + change(b).reshape(cube)).astype(BF16).astype(F32)
            ps[l, b] = x
            energy = energy + jnp.sum(x * x, axis=0)
        energy = 0.5 * jnp.sum(energy, axis=1, keepdims=True)
        mine = jnp.sum(jnp.where(lane == iota((lc, tile), 0), energy, 0.0), axis=0, keepdims=True)
        at = it * n_line + l
        sende[at] = mine
        recve[at, me] = mine
        for p in peers:
            link(2 + at, sende.at[at], recve.at[at, me], p, me).start()

    def over_shots(it, l):
        at = it * n_line + l
        for p in peers:
            link(2 + at, sende.at[at], recve.at[at, number(*p)], p, number(*p)).wait_recv()
        total = jnp.zeros((lc, tile), F32)
        for k in range(count):
            total = total + member[k] * recve[at, k]
        mean = jnp.sum(total, axis=1, keepdims=True)
        rms = jnp.broadcast_to(jnp.sqrt(mean + EPSILON), (lc, tile)).reshape(1, lc, tile)
        inv = 1.0 / rms

        def make(b):
            x = (ps[l, b] * inv).astype(BF16).astype(F32)
            return beside(jnp.concatenate([one, x[: shots - 1]], axis=0), x, jnp.concatenate([x[1:], one], axis=0))

        widen(make)
        layers(zs, hs, gs, ys, *tb)
        for b in range(blocks):
            x = (ps[l, b] + rms * change(b).reshape(cube)).astype(BF16).astype(F32)
            ps[l, b] = x
            for s in range(shots):
                rolled[b + 2, s] = pltpu.roll(x[s], rest[s], 1)
        for g in range(n_mix):
            acc = -mx[:, g * n_line + l]
            for i in range(run):
                s = order[g * run + i]
                lag = lags[s]
                a = 2 - lag // HALF
                near, late = rolled[pl.ds(a, blocks), s], rolled[pl.ds(a - 1, blocks), s]
                acc = acc + jnp.where((inner >= lax.rem(lag, HALF))[None], near, late)
            mf[:blocks, g] = acc
        for s in range(shots):
            m = mf[:, group[s]]
            rolled[: blocks + 2, s] = pltpu.roll(m, lax.rem(tile - rest[s], tile), 2)
        for s in range(shots):
            near, late = rolled[pl.ds(far[s], blocks), s], rolled[pl.ds(far[s] + 1, blocks), s]
            back = jnp.where((inner < HALF - rest[s])[None], near, late)
            xs[1 + l, :, s] = (ps[l, :, s] - pace[it] * back).astype(BF16).astype(F32)
        rolled[:2] = jnp.zeros_like(rolled[:2])

        @pl.when(it == ITERS - 1)
        def _():
            for s in range(n_shot):
                for t in range(n_tm):
                    tiles = []
                    for j in range(tl // tile):
                        b = t * each + 2 * j
                        tiles.append(jnp.where(low, xs[1 + l, b, s], xs[1 + l, b + 1, s]))
                    n = len(tiles) // 2
                    halves = [jnp.concatenate(tiles[:n], axis=1), jnp.concatenate(tiles[n:], axis=1)]
                    backs[number(s, l, t)] = jnp.concatenate(halves, axis=0).astype(BF16)
            own = (at_shot, l, at_tm)
            for s in turns[0]:
                for t in turns[2]:
                    if s is at_shot and t is at_tm:
                        continue
                    link(back_kind, backs.at[number(s, l, t)], backr.at[me], (s, l, t), me).start()

            @pl.when(l != at_line)
            def _():
                link(back_kind, backs.at[number(*own)], backr.at[me], own, me).start()

    def iterate(it, carry):
        def lines(l, carry):
            over_lines(it, l)
            return carry

        def stations(l, carry):
            over_shots(it, l)
            return carry

        lax.fori_loop(0, n_line, lines, 0)
        lax.fori_loop(0, n_line, stations, 0)
        return carry

    lax.fori_loop(0, ITERS, iterate, 0)

    backr[me] = backs[me]
    row, col = iota((recv_n, recv_n), 0), iota((recv_n, recv_n), 1)
    perm = jnp.where(row == lax.rem(col, lc) * count + col // lc, 1.0, 0.0).astype(BF16)
    for p in peers:
        link(back_kind, backs.at[number(*p)], backr.at[number(*p)], p, number(*p)).wait_recv()
    v = []
    for k in range(count):
        part = backr[k].astype(F32)
        v.append(jnp.concatenate([part[:lc], part[lc:]], axis=1))
    v = jnp.concatenate(v, axis=0).astype(BF16)
    out[0] = jnp.dot(perm, v, preferred_element_type=F32).astype(BF16)
    link(1, sendm, recvm.at[at_line], other, me).wait_send()
    for p in peers:
        link(0, sendx.at[number(*p)], recvx.at[me], p, me).wait_send()
        for at in range(ITERS * n_line):
            link(2 + at, sende.at[at], recve.at[at, me], p, me).wait_send()
        link(back_kind, backs.at[number(*p)], backr.at[me], p, me).wait_send()


def patch(guess, mixtures, lags, order, tallies, wa, wb, pace, sizes):
    count = math.prod(sizes)
    n_shot, n_line, n_tm = sizes
    recv, tl = guess.shape[1:]
    n_mix, nt = mixtures.shape[0], mixtures.shape[2]
    lc, tile = recv // count, 2 * HALF
    blocks = nt // HALF
    per, feat = n_shot * lc, wa[0].shape[2]
    wide = feat * len(SLOT)
    rows = blocks * per
    weights = [w.transpose(1, 0, 2) if i == 0 else w for part in (wa, wb) for i, w in enumerate(part)]
    v, s, h = (pl.BlockSpec(memory_space=m) for m in (pltpu.VMEM, pltpu.SMEM, pl.ANY))
    slab = pltpu.VMEM((count, 2 * lc, tl // 2), BF16)
    woven = [
        pltpu.VMEM((2 * GROUPS, wide, wide), BF16),
        pltpu.VMEM((2, wide, wide), BF16),
        pltpu.VMEM((2 * GROUPS * wide, wide), BF16),
        pltpu.VMEM((2, wide), F32),
    ]
    kinds = 3 + ITERS * n_line
    return pl.pallas_call(
        functools.partial(patch_kernel, sizes),
        out_shape=jax.ShapeDtypeStruct(guess.shape, BF16),
        in_specs=[s] * 4 + [h] * 10,
        out_specs=v,
        scratch_shapes=[
            pltpu.VMEM((recv, tl), BF16),
            pltpu.VMEM(mixtures.shape, BF16),
            slab,
            slab,
            pltpu.VMEM((n_mix * lc, nt), BF16),
            pltpu.VMEM((n_line, n_mix * lc, nt), BF16),
            slab,
            slab,
            pltpu.VMEM((ITERS * n_line, 1, tile), F32),
            pltpu.VMEM((ITERS * n_line, count, 1, tile), F32),
            pltpu.VMEM((n_line + 2, blocks, n_shot, lc, tile), F32),
            pltpu.VMEM((n_line, blocks, n_shot, lc, tile), F32),
            pltpu.VMEM((blocks, n_mix * n_line, lc, tile), F32),
            pltpu.VMEM((blocks + 2, n_shot, lc, tile), F32),
            pltpu.VMEM((blocks + 2, n_mix, lc, tile), F32),
            pltpu.VMEM((count, lc, tile), F32),
            pltpu.VMEM((2, rows, wide), BF16),
            pltpu.VMEM((2, GROUPS * rows + 2 * per, wide), BF16),
            pltpu.VMEM((rows, 2 * GROUPS * wide), BF16),
            pltpu.VMEM((blocks + 2, per, wide), F32),
            *woven,
            *woven,
            *[pltpu.VMEM(w.shape, w.dtype) for w in weights],
            pltpu.SemaphoreType.DMA((2 + len(weights),)),
            pltpu.SemaphoreType.DMA((kinds, count)),
            pltpu.SemaphoreType.DMA((kinds, count)),
        ],
        compiler_params=pltpu.CompilerParams(vmem_limit_bytes=56 * 2**20, collective_id=1, has_side_effects=True),
    )(lags, order, tallies, pace, guess, mixtures, *weights)


def per_device(guess, mixtures, lags, order, tallies, e1, m1, x1, b1, e2, m2, x2, b2, pace):
    sh, recv, tl = guess.shape
    n_shot, n_line, n_tm = (lax.axis_size(a) for a in AXES)
    whole = RPL % (n_shot * n_line * n_tm) == 0
    where = AXES if whole else AXES[1:]
    parts = math.prod(lax.axis_size(a) for a in where)
    kp, lh = RPL // parts, recv // RPL
    lines, shots, nt = lh * n_line, sh * n_shot, tl * n_tm
    planes, s1 = nt // 2 // C, shots if whole else sh
    r1 = lines * kp
    r2 = r1 if whole else r1 // n_shot
    lanes1, lanes2 = 2 * s1 * r1, 2 * shots * r2
    sources = n_shot if whole else 1
    i32 = functools.partial(jnp.arange, dtype=jnp.int32)
    n_mix, feat = mixtures.shape[0], e1.shape[2]
    square = sh == 1 and kp == 1 and n_line == 2 and shots % n_mix == 0 and feat == HALF
    square = square and lh == C and tl % (4 * HALF) == 0 and n_mix * lh % 16 == 0
    square = square and lines == parts and 2 * (n_mix // n_line) == n_line
    if square:
        sizes = (n_shot, n_line, n_tm)
        return patch(guess, mixtures, lags, order, tallies, (e1, m1, x1, b1), (e2, m2, x2, b2), pace, sizes)

    at_shot = lax.axis_index("shot")
    n_mix, run = mixtures.shape[0], nt // C
    fused = whole and sh == 1 and kp == 1 and C % n_tm == 0 and n_shot * n_tm == C
    x = guess.reshape(sh, lh, parts, kp, tl).transpose(2, 0, 1, 3, 4)
    if fused:
        share = (at_shot * n_tm + lax.axis_index("tm")) * run
        mine = lax.dynamic_slice_in_dim(mixtures, share, run, axis=2).reshape(n_mix, lh, parts, run)
        mine = mine.transpose(2, 1, 0, 3).reshape(parts, lh, n_mix * run)
        x = jnp.concatenate([x.reshape(parts, lh, tl), mine], axis=2)
    x = lax.all_to_all(x, where, split_axis=0, concat_axis=0, tiled=False)
    if not fused:
        x = x.reshape(sources, n_line, n_tm, sh, lh, kp, tl).transpose(0, 3, 1, 4, 5, 2, 6)
        x = x.reshape(s1, r1, C, planes, 2).transpose(3, 2, 4, 0, 1).reshape(planes, C, lanes1)


    def first_k(line):
        block = line * n_tm + lax.axis_index("tm")
        return (at_shot * n_line * n_tm + block if whole else block) * kp

    if not fused:
        grid = mixtures.reshape(n_mix, lh, RPL, nt)
        sent = jnp.stack([lax.dynamic_slice_in_dim(grid, first_k(d), kp, axis=2) for d in range(n_line)])
        m = lax.all_to_all(sent, "line", split_axis=0, concat_axis=0)
        m = m.transpose(1, 0, 2, 3, 4).reshape(n_mix, r1, nt)
        if not whole:
            m = lax.dynamic_slice_in_dim(m, at_shot * r2, r2, axis=1)
        m = m.reshape(n_mix, r2, C, planes, 2).transpose(3, 2, 4, 0, 1).reshape(planes * C, 2 * n_mix * r2)

    np_ = tallies.shape[0]
    here = i32(np_)
    offsets = jnp.sum(jnp.where(here[None, :] < here[:, None], tallies[None, :], 0), axis=1)
    mine = first_k(lax.axis_index("line"))

    def one_hot(r):
        line, k = r // kp, mine + lax.rem(r, kp)
        q = lax.rem(line, lh) * RPL + k
        inside = (offsets[:, None] <= q[None, :]) & (q[None, :] < (offsets + tallies)[:, None])
        block = (line // lh)[None, :] == i32(n_line)[:, None]
        return (block[:, None, :] & inside[None, :, :]).reshape(n_line * np_, r.shape[0]).astype(F32)

    member = jnp.tile(one_hot(i32(r1)), (1, 2 * s1))
    r_own = i32(r2) if whole else at_shot * r2 + i32(r2)
    count = jnp.tile((tallies * (shots * nt)).astype(F32), n_line)
    spread = jnp.tile(one_hot(r_own) / count[:, None], (1, 2 * shots))

    sid = i32(shots)
    place = jnp.sum(jnp.where(order[None, :] == sid[:, None], sid[None, :], 0), axis=1)
    group = place // (shots // n_mix)
    same = (group[:, None] == group[None, :]).astype(BF16)
    chosen = (i32(n_mix)[:, None] == group[None, :]).astype(BF16)
    rest, two = jnp.eye(r2, dtype=BF16), jnp.eye(2, dtype=BF16)
    join = jnp.kron(two, jnp.kron(same, rest))
    take = jnp.kron(two, jnp.kron(chosen, rest))

    n1, n2 = s1 * r1, shots * r2
    a, b = np.arange(n1)[:, None], np.arange(n1)[None, :]
    near1 = np.stack([(a == b + (c - 1) * kp) & (a // r1 == b // r1) for c in range(3)])
    a, b = np.arange(n2)[:, None], np.arange(n2)[None, :]
    near2 = np.stack([a == b + (c - 1) * r2 for c in range(3)])
    wa = prepared(e1, m1, x1, b1, near1)
    wb = prepared(e2, m2, x2, b2, near2)

    rows = planes * C
    tot1, tot2 = pltpu.VMEM((rows, 2 * lanes1), F32), pltpu.VMEM((rows, 2 * lanes2), F32)
    feat = e1.shape[2]
    band = pltpu.VMEM((3 * PACK * feat, PACK * feat), BF16)
    buf = pltpu.VMEM((2, 2 * planes, C, lanes2), F32)
    spass = jax.ShapeDtypeStruct((planes, C, lanes1), BF16)
    part = jax.ShapeDtypeStruct((n_line * np_, 128), F32)
    moved = jax.ShapeDtypeStruct((planes, C, lanes2), BF16)

    def to_stations(y):
        y = y.reshape(rows, 2, sh, n_shot, r2)
        y = lax.all_to_all(y, "shot", split_axis=3, concat_axis=2, tiled=True)
        return y.reshape(planes, C, lanes2)

    def to_shots(y):
        y = y.reshape(rows, 2, shots, 1, r2)
        y = lax.all_to_all(y, "shot", split_axis=2, concat_axis=3, tiled=True)
        return y.reshape(planes, C, lanes1)

    dims = (n_shot, n_line, n_tm)
    cube = pltpu.VMEM((planes, C, lanes1), F32)
    if fused:
        mixed = jax.ShapeDtypeStruct((rows, 2 * n_mix * r2), BF16)
        side = pltpu.VMEM((planes, C, 2 * n_mix * r2), F32)
        sp, energy, m = call(
            functools.partial(entry_kernel, dims),
            (spass, part, mixed),
            (x, *wa, member),
            0,
            [tot1, band, cube, side],
        )
    else:
        sp, energy = call(first_kernel, (spass, part), (x, *wa, member), 0, [tot1, band])
    for it in range(ITERS):
        tot = summed(energy, (n_shot, n_line, n_tm)) if whole else lax.psum(energy, AXES)
        if not whole:
            sp = to_stations(sp)
        ins = (lags, pace, sp, tot, spread, *wb, join, m, take)
        if whole and it < ITERS - 1:
            sp, energy = call(
                functools.partial(both_kernel, it, shots), (spass, part), (*ins, *wa, member), 2, [buf, tot2, band]
            )
            continue
        if fused:
            back = jax.ShapeDtypeStruct((parts, lh, tl), BF16)
            x = call(functools.partial(exit_kernel, it, dims), back, ins, 2, [buf, tot2, band, cube])
            continue
        x = call(functools.partial(station_kernel, it, shots), moved, ins, 2, [buf, tot2, band])
        if not whole:
            x = to_shots(x)
            if it < ITERS - 1:
                sp, energy = call(first_kernel, (spass, part), (x, *wa, member), 0, [tot1, band])

    if not fused:
        x = x.reshape(planes, C, 2, s1, r1).transpose(3, 4, 1, 0, 2)
        x = x.reshape(sources, sh, n_line, lh, kp, n_tm, tl).transpose(0, 2, 5, 1, 3, 4, 6)
    x = lax.all_to_all(x.reshape(parts, sh, lh, kp, tl), where, split_axis=0, concat_axis=0)
    return x.transpose(1, 2, 0, 3, 4).reshape(sh, recv, tl)


def solution(mesh):
    spec = P(("group", "shot"), "line", "tm")
    placed = (spec, P("group", "line", None), P("group"), P("group"), P("group")) + (P(),) * 9
    return jax.shard_map(per_device, mesh=mesh, in_specs=placed, out_specs=spec, check_vma=False)
```

```python
import functools
import math

import jax
import jax.numpy as jnp
import numpy as np
from jax import lax
from jax.experimental import pallas as pl
from jax.experimental.pallas import tpu as pltpu
from jax.sharding import PartitionSpec as P

RPL = 16
ITERS = 2
EPSILON = 1e-05
C = 8
PACK = 4
TAPS = (1, 2, 3, 0)
F32, BF16 = jnp.float32, jnp.bfloat16
AXES = ("shot", "line", "tm")


def ahead(x, k):
    edge = pltpu.roll(x[:k], C - 1, 1)
    edge = jnp.where(lax.broadcasted_iota(jnp.int32, edge.shape, 1) == C - 1, 0.0, edge)
    return edge if k == x.shape[0] else jnp.concatenate([x[k:], edge], axis=0)


def behind(x, k):
    edge = pltpu.roll(x[x.shape[0] - k :], 1, 1)
    edge = jnp.where(lax.broadcasted_iota(jnp.int32, edge.shape, 1) == 0, 0.0, edge)
    return edge if k == x.shape[0] else jnp.concatenate([edge, x[: x.shape[0] - k]], axis=0)


def even_lanes(shape):
    return lax.broadcasted_iota(jnp.int32, shape, len(shape) - 1) < shape[-1] // 2


def net(x, w_in, pick, w_mid, w_out, place, bias, total, band):
    planes, _, lanes = x.shape
    rows = planes * C
    side = jnp.where(even_lanes(x.shape), ahead(x, 1), behind(x, 1))
    z = jnp.concatenate([x, side], axis=2).astype(BF16).reshape(rows, 2 * lanes)
    total[...] = jnp.zeros_like(total)
    wide = w_in.shape[1]
    feat = wide // PACK
    for j in range(3):
        tap = w_mid[j].astype(F32)
        for i in range(PACK):
            row = [tap if p == i else jnp.zeros_like(tap) for p in range(PACK)]
            at = (j * PACK + i) * feat
            band[at : at + feat, :] = jnp.concatenate(row, axis=1).astype(BF16)

    def step(q, carry):
        w_here = jnp.dot(pick[q], w_in[...], preferred_element_type=F32).astype(BF16)
        o_here = jnp.dot(w_out[...], place[q], preferred_element_type=F32).astype(BF16)
        h = jnp.dot(z, w_here, preferred_element_type=F32)
        h = jnp.maximum(h + bias[0:1, :], 0.0)
        cube = h.reshape(planes, C, wide)
        first = ahead(cube[:2], 2).reshape(2 * C, wide).astype(BF16)
        last = behind(cube[planes - 2 :], 2).reshape(2 * C, wide).astype(BF16)
        hb = h.astype(BF16)
        early = jnp.concatenate([last, hb[: rows - 2 * C]], axis=0)
        late = jnp.concatenate([hb[2 * C :], first], axis=0)
        g = jnp.dot(jnp.concatenate([early, hb, late], axis=1), band[...], preferred_element_type=F32)
        g = jnp.maximum(g + bias[1:2, :], 0.0).astype(BF16)
        total[...] += jnp.dot(g, o_here, preferred_element_type=F32)
        return carry

    lax.fori_loop(0, pick.shape[0], step, 0, unroll=2)
    y = total[...].reshape(planes, C, 2 * lanes)
    a, b = y[:, :, :lanes], y[:, :, lanes:]
    return a + jnp.where(even_lanes(b.shape), behind(b, 1), ahead(b, 1))


def shot_step(x, weights, member, out_ref, part_ref, total, band):
    y = (x + net(x, *weights, total, band)).astype(BF16)
    out_ref[...] = y
    y = y.astype(F32)
    energy = jnp.sum(jnp.sum(y * y, axis=0), axis=0, keepdims=True)
    sums = jnp.sum(member[...] * energy, axis=1, keepdims=True)
    part_ref[...] = jnp.broadcast_to(sums, part_ref.shape)


def shifted(buf, lag_ref, shots, forward):
    planes, lanes = buf.shape[1] // 2, buf.shape[3]
    shape = (planes, C, lanes)
    even = even_lanes(shape)
    per = lanes // 2 // shots
    lane_shot = lax.rem(lax.broadcasted_iota(jnp.int32, shape, 2), lanes // 2) // per
    out = jnp.zeros(shape, F32)
    for s in range(shots):
        lag = lag_ref[s]
        half, odd = lag // 2, lax.rem(lag, 2)
        at_even = half if forward else planes - half - odd
        at_odd = half + odd if forward else planes - half
        one = jnp.where(even, buf[odd, pl.ds(at_even, planes)], buf[odd, pl.ds(at_odd, planes)])
        out = jnp.where(lane_shot == s, one, out)
    return out


def station_step(shots, sp, tot_ref, spread, weights, lags, join, mix, take, pace, buf, total, band):
    planes, _, lanes = sp.shape
    rows = planes * C
    mean = jnp.sum(tot_ref[:, 0:1] * spread[...], axis=0, keepdims=True)
    rms = jnp.sqrt(mean + EPSILON).reshape(1, 1, lanes)
    normed = (sp / rms).astype(BF16).astype(F32)
    settled = (sp + rms * net(normed, *weights, total, band)).astype(BF16).astype(F32)

    def fill(x, forward):
        far = ahead(x, planes) if forward else behind(x, planes)
        near_at, far_at = (0, planes) if forward else (planes, 0)
        for v, at in ((x, near_at), (far, far_at)):
            buf[0, at : at + planes] = v
            h = lanes // 2
            buf[1, at : at + planes] = jnp.concatenate([v[:, :, h:], v[:, :, :h]], axis=2)

    fill(settled, False)
    fired = shifted(buf, lags, shots, False).astype(BF16).reshape(rows, lanes)
    misfit = jnp.dot(fired, join[...], preferred_element_type=F32)
    misfit -= jnp.dot(mix[...], take[...], preferred_element_type=F32)
    fill(misfit.reshape(planes, C, lanes), True)
    return (settled - pace * shifted(buf, lags, shots, True)).astype(BF16)


def by_phase(width):
    row = lax.broadcasted_iota(jnp.int32, (width, width), 0)
    col = lax.broadcasted_iota(jnp.int32, (width, width), 1)
    half = width // 2
    return jnp.where(col == 2 * lax.rem(row, half) + row // half, 1.0, 0.0).astype(BF16)


def unfold(read, into, sort):
    planes = into.shape[0]
    for c in range(C):
        v = lax.dot_general(sort, read(c), (((1,), (1,)), ((), ())), preferred_element_type=F32)
        into[:, c, :] = jnp.concatenate([v[:planes], v[planes:]], axis=1)


def entry_kernel(
    dims, x, wi, wp, wm, wo, wq, bi, member, out, part, mix, total, band, cube, side
):
    shots, blocks, halves = dims
    width = 2 * cube.shape[0]
    sort, each = by_phase(width), C // halves

    def traces(c):
        at, t = slice(c % each * width, (c % each + 1) * width), c // each
        rows = [x[(s * blocks + b) * halves + t, :, at].astype(F32) for s in range(shots) for b in range(blocks)]
        return jnp.concatenate(rows, axis=0).astype(BF16)

    tl = each * width

    def records(c):
        s, t = c // halves, c % halves
        rows = [
            x[(s * blocks + b) * halves + t, :, tl + g * width : tl + (g + 1) * width].astype(F32)
            for g in range((x.shape[2] - tl) // width)
            for b in range(blocks)
        ]
        return jnp.concatenate(rows, axis=0).astype(BF16)

    unfold(records, side, sort)
    mix[...] = side[...].astype(BF16).reshape(mix.shape)
    unfold(traces, cube, sort)
    shot_step(cube[...], (wi, wp, wm, wo, wq, bi), member, out, part, total, band)


def exit_kernel(
    it, dims, lags, pace, sp, tot, spread, wi, wp, wm, wo, wq, bi, join, mix, take, out, buf, total, band, cube
):
    shots, blocks, halves = dims
    width = 2 * cube.shape[0]
    sort, each = by_phase(width), C // halves
    x = station_step(
        shots, sp[...].astype(F32), tot, spread, (wi, wp, wm, wo, wq, bi), lags, join, mix, take, pace[it], buf, total, band
    )
    cube[...] = x.astype(F32)
    n, lh = cube.shape[2] // 2, out.shape[1]
    for c in range(C):
        v = cube[:, c, :]
        v = jnp.concatenate([v[:, :n], v[:, n:]], axis=0).T.astype(BF16)
        v = jnp.dot(v, sort, preferred_element_type=F32)
        at, t = slice(c % each * width, (c % each + 1) * width), c // each
        for j in range(shots * blocks):
            out[j * halves + t, :, at] = v[j * lh : (j + 1) * lh].astype(BF16)


def first_kernel(x, wi, wp, wm, wo, wq, bi, member, out, part, total, band):
    shot_step(x[...].astype(F32), (wi, wp, wm, wo, wq, bi), member, out, part, total, band)


def station_kernel(it, shots, lags, pace, sp, tot, spread, wi, wp, wm, wo, wq, bi, join, mix, take, out, buf, total, band):
    out[...] = station_step(
        shots, sp[...].astype(F32), tot, spread, (wi, wp, wm, wo, wq, bi), lags, join, mix, take, pace[it], buf, total, band
    )


def both_kernel(
    it, shots, lags, pace, sp, tot, spread, wi, wp, wm, wo, wq, bi, join, mix, take, vi, vp, vm, vo, vq, ci, member, out, part, buf, total, band
):
    x = station_step(
        shots, sp[...].astype(F32), tot, spread, (wi, wp, wm, wo, wq, bi), lags, join, mix, take, pace[it], buf, total, band
    )
    shot_step(x.astype(F32), (vi, vp, vm, vo, vq, ci), member, out, part, total, band)


def call(body, outs, ins, smem, scratch):
    v, s = pl.BlockSpec(memory_space=pltpu.VMEM), pl.BlockSpec(memory_space=pltpu.SMEM)
    return pl.pallas_call(
        body,
        out_shape=outs,
        in_specs=[s] * smem + [v] * (len(ins) - smem),
        out_specs=jax.tree.map(lambda _: v, outs),
        scratch_shapes=scratch,
        compiler_params=pltpu.CompilerParams(vmem_limit_bytes=48 * 2**20),
    )(*ins)


def prepared(w_in, w_mid, w_out, bias, near):
    n, feat = near.shape[1], w_in.shape[2]
    tiles = n // PACK
    cols = near.reshape(3, n, tiles, PACK).transpose(2, 1, 0, 3)
    pick = np.einsum("jk,tnci->tjnkci", np.eye(4)[list(TAPS)], cols).reshape(tiles, 4 * n, 12 * PACK)
    place = np.einsum("kj,tin->tjikn", np.eye(4)[list(TAPS)], np.eye(n).reshape(tiles, PACK, n)).reshape(tiles, 4 * PACK, 4 * n)
    w1 = w_in.reshape(12, 1, 1, feat)
    eye = jnp.eye(PACK, dtype=BF16)
    rows = (w1 * eye[None, :, :, None]).reshape(12 * PACK, PACK * feat)
    w2 = w_out.T.reshape(1, feat, 4, 1)
    ends = (w2 * eye[:, None, None, :]).reshape(PACK * feat, 4 * PACK)
    return rows, jnp.asarray(pick, BF16), w_mid, ends, jnp.asarray(place, BF16), jnp.tile(bias, (1, PACK))


def exchange_kernel(sizes, x, out, slots, send, recv):
    count = math.prod(sizes)
    me = (lax.axis_index("shot") * sizes[1] + lax.axis_index("line")) * sizes[2] + lax.axis_index("tm")

    def peer(off):
        at = lax.rem(me + off, count)
        return {
            "shot": at // (sizes[1] * sizes[2]),
            "line": lax.rem(at // sizes[2], sizes[1]),
            "tm": lax.rem(at, sizes[2]),
        }

    barrier = pltpu.get_barrier_semaphore()
    for off in range(1, count):
        pl.semaphore_signal(barrier, inc=1, device_id=peer(off), device_id_type=pl.DeviceIdType.MESH)
    pl.semaphore_wait(barrier, count - 1)
    copies = []
    for off in range(1, count):
        copy = pltpu.make_async_remote_copy(
            src_ref=x,
            dst_ref=slots.at[off],
            send_sem=send.at[off],
            recv_sem=recv.at[off],
            device_id=peer(off),
            device_id_type=pl.DeviceIdType.MESH,
        )
        copy.start()
        copies.append(copy)
    total = x[...]
    for off, copy in enumerate(copies, 1):
        copy.wait()
        total += slots[off]
    out[...] = total


def summed(x, sizes):
    count, v = math.prod(sizes), pl.BlockSpec(memory_space=pltpu.VMEM)
    return pl.pallas_call(
        functools.partial(exchange_kernel, sizes),
        out_shape=jax.ShapeDtypeStruct(x.shape, x.dtype),
        in_specs=[v],
        out_specs=v,
        scratch_shapes=[
            pltpu.VMEM((count, *x.shape), x.dtype),
            pltpu.SemaphoreType.DMA((count,)),
            pltpu.SemaphoreType.DMA((count,)),
        ],
        compiler_params=pltpu.CompilerParams(collective_id=0, has_side_effects=True),
    )(x)


SLOT = (0, 3, 1, 2)
HALF = 64
GROUPS = 4


def iota(shape, dim):
    return lax.broadcasted_iota(jnp.int32, shape, dim)


def weave(w_in, w_mid, w_out, bias, we, wm, wo, bi):
    feat = w_in.shape[2]
    wide = feat * len(SLOT)
    row, lane = iota((wide, wide), 0), iota((wide, wide), 1)
    at, ch = lax.rem(row, HALF), row // HALF
    slot = lane // feat
    pos = jnp.where(slot == 1, 3, jnp.where(slot == 0, 0, slot - 1))
    taps = w_in[...].astype(F32)
    for par in range(2):
        turned = lax.rem(at + (1 if par == 0 else HALF - 1), HALF)
        tap = lax.rem(turned, 4)
        base = jnp.zeros((wide, wide), F32)
        for c in range(3):
            for t in range(4):
                line = jnp.concatenate([taps[c, t : t + 1, :]] * len(SLOT), axis=1)
                base = jnp.where((ch == c) & (tap == t), line, base)
        for g in range(GROUPS):
            we[par * GROUPS + g] = jnp.where(turned // 4 == 4 * g + pos, base, 0.0).astype(BF16)
    zero = jnp.zeros((feat, feat), F32)
    mid = [w_mid[j].astype(F32) for j in range(3)]

    def block(came, goes):
        j = came - goes + 1
        return mid[j] if 0 <= j < 3 else zero

    for n, came in enumerate(SLOT):
        blocks = [block(came, goes) for goes in SLOT]
        wm[0, n * feat : (n + 1) * feat, :] = jnp.concatenate(blocks, axis=1).astype(BF16)
    for n in range(4):
        blocks = [zero] * 4
        blocks[n ^ 1] = mid[2 if n % 2 == 0 else 0]
        wm[1, n * feat : (n + 1) * feat, :] = jnp.concatenate(blocks, axis=1).astype(BF16)

    def sample(shape):
        col = iota(shape, 1)
        m = lax.rem(col, HALF)
        edge = jnp.where(m == HALF - 1, -1, jnp.where(m == 0, HALF, -4 * HALF))
        return jnp.where(col >= 2 * HALF, edge, m)

    near, far = sample((4, wide)), sample((feat, wide))
    for par in range(2):
        pick = jnp.where(lax.rem(near - 2 * par + 1 + 8 * HALF, 4) == iota((4, wide), 0), 1.0, 0.0).astype(BF16)
        base = lax.dot_general(w_out[...], pick, (((0,), (0,)), ((), ())), preferred_element_type=F32)
        for g in range(GROUPS):
            for n, i in enumerate(SLOT):
                d = far - 4 * (4 * g + i) - 2 * par + 1
                at = ((par * GROUPS + g) * len(SLOT) + n) * feat
                wo[at : at + feat, :] = jnp.where((d >= 0) & (d < 4), base, 0.0).astype(BF16)
    bi[...] = jnp.concatenate([bias[...]] * len(SLOT), axis=1)


def layers(zs, hs, gs, ys, we, wm, wo, bi):
    b0, b1 = bi[0:1, :], bi[1:2, :]
    rows, wide = zs.shape[1:]
    blocks = ys.shape[0] - 2
    per, half = rows // blocks, wide // 2
    for par in range(2):
        for g in range(GROUPS):
            h = jnp.dot(zs[par], we[par * GROUPS + g], preferred_element_type=F32)
            h = jnp.maximum(h + b0, 0.0).astype(BF16)
            for b in range(blocks):
                at = per + (b * GROUPS + g) * per
                hs[par, at : at + per, :] = h[b * per : (b + 1) * per]
    low = iota((rows, half), 1) < half // 2
    for r in range(per, per + GROUPS * rows, rows):
        edge = [jnp.where(low, hs[par, r + per : r + per + rows, :half], hs[par, r - per : r - per + rows, :half]) for par in range(2)]
        edge = jnp.dot(jnp.concatenate(edge, axis=1), wm[1], preferred_element_type=F32)
        for par in range(2):
            g = jnp.dot(hs[par, r : r + rows, :], wm[0], preferred_element_type=F32)
            ends = g[:, :half] + edge[:, par * half : (par + 1) * half]
            g = [jnp.maximum(ends + b1[:, :half], 0.0), jnp.maximum(g[:, half:] + b1[:, half:], 0.0)]
            for n in range(rows // per):
                b, q = divmod(r // per - 1 + n, GROUPS)
                for i in range(2):
                    col = (par * GROUPS + q) * wide + i * half
                    gs[b * per : (b + 1) * per, col : col + half] = g[i][n * per : (n + 1) * per].astype(BF16)
    part = blocks // 4
    for b in range(0, blocks, part):
        y = jnp.dot(gs[b * per : (b + part) * per, :], wo[...], preferred_element_type=F32)
        ys[1 + b : 1 + b + part] = y.reshape(part, per, wide)


def patch_kernel(sizes, lags, order, tallies, pace, guess, mixtures, *refs):
    given, out = refs[:8], refs[8]
    (gbuf, mbuf, sendx, recvx, sendm, recvm, backs, backr, sende, recve) = refs[9:19]
    (xs, ps, mx, rolled, mf, member, zs, hs, gs, ys) = refs[19:29]
    ta, tb, held = refs[29:33], refs[33:37], refs[37:45]
    load_sem, ssem, rsem = refs[45:]
    n_shot, n_line, n_tm = sizes
    count = math.prod(sizes)
    axes = [lax.axis_index(a) for a in AXES]
    turns = [[axes[i]] + [lax.rem(axes[i] + d, n) for d in range(1, n)] for i, n in enumerate(sizes)]
    at_shot, at_line, at_tm = axes

    def number(s, l, t):
        return (s * n_line + l) * n_tm + t

    def device(s, l, t):
        return {"shot": s, "line": l, "tm": t}

    me = number(*axes)
    peers = [(s, l, t) for s in turns[0] for l in turns[1] for t in turns[2]][1:]
    shots = n_shot
    n_mix = mixtures.shape[0]
    run = shots // n_mix
    recv_n, tl = guess.shape[1:]
    lc = recv_n // count
    tile = 2 * HALF
    blocks = tl * n_tm // HALF
    each = tl // HALF
    back_kind = 2 + ITERS * n_line

    barrier = pltpu.get_barrier_semaphore()
    for p in peers:
        pl.semaphore_signal(barrier, inc=1, device_id=device(*p), device_id_type=pl.DeviceIdType.MESH)
    pairs = [(guess.at[0], gbuf), (mixtures, mbuf)] + list(zip(given, held))
    loads = [pltpu.make_async_copy(a, b, load_sem.at[i]) for i, (a, b) in enumerate(pairs)]
    for copy in loads:
        copy.start()

    def link(which, src, dst, to, came):
        return pltpu.make_async_remote_copy(
            src_ref=src,
            dst_ref=dst,
            send_sem=ssem.at[which, number(*to)],
            recv_sem=rsem.at[which, came],
            device_id=device(*to),
            device_id_type=pl.DeviceIdType.MESH,
        )

    row, col = iota((recv_n, recv_n), 0), iota((recv_n, recv_n), 1)
    perm = jnp.where(col == lax.rem(row, lc) * count + row // lc, 1.0, 0.0).astype(BF16)
    loads[0].wait()
    v = jnp.dot(perm, gbuf[...], preferred_element_type=F32)
    for k in range(count):
        part = v[k * lc : (k + 1) * lc]
        sendx[k] = jnp.concatenate([part[:, : tl // 2], part[:, tl // 2 :]], axis=0).astype(BF16)
    pl.semaphore_wait(barrier, count - 1)
    for p in peers:
        link(0, sendx.at[number(*p)], recvx.at[me], p, me).start()

    loads[1].wait()
    other = (at_shot, n_line - 1 - at_line, at_tm)
    row, col = iota((2 * lc, recv_n), 0), iota((2 * lc, recv_n), 1)
    wanted = jnp.where(row < lc, me, number(*other))
    pick = jnp.where(col == lax.rem(row, lc) * count + wanted, 1.0, 0.0).astype(BF16)
    picked = [jnp.dot(pick, mbuf[g], preferred_element_type=F32) for g in range(n_mix)]
    sendm[...] = jnp.concatenate([p[lc:] for p in picked], axis=0).astype(BF16)
    link(1, sendm, recvm.at[at_line], other, me).start()
    recvm[at_line] = jnp.concatenate([p[:lc] for p in picked], axis=0).astype(BF16)
    recvx[me] = sendx[me]

    for copy in loads[2:]:
        copy.wait()
    weave(*held[:4], *ta)
    weave(*held[4:], *tb)
    edges = hs.shape[1] - (GROUPS * blocks + 1) * (hs.shape[1] // (GROUPS * blocks + 2))
    hs[:, :edges] = jnp.zeros_like(hs[:, :edges])
    hs[:, hs.shape[1] - edges :] = jnp.zeros_like(hs[:, :edges])
    for ref in (ys, rolled, mf, xs):
        ref[0] = jnp.zeros_like(ref[0])
        ref[ref.shape[0] - 1] = jnp.zeros_like(ref[0])
    for ref, at in ((rolled, 1), (mf, blocks)):
        ref[at] = jnp.zeros_like(ref[at])
    sec = []
    for rows in ((lc, tile), (count, tile)):
        if rows[0] == lc:
            q = iota(rows, 0) * count + me
        else:
            q = lax.rem(iota(rows, 1), lc) * count + iota(rows, 0)
        edge, at, size = jnp.int32(0), jnp.zeros(rows, jnp.int32), jnp.zeros(rows, jnp.int32)
        for p in range(tallies.shape[0]):
            at = jnp.where(q >= edge, p, at)
            size = jnp.where(q >= edge, tallies[p], size)
            edge = edge + tallies[p]
        sec.append((at, size))
    scale = 1.0 / (sec[0][1] * (shots * tl * n_tm)).astype(F32)
    for k in range(count):
        member[k] = jnp.where(sec[0][0] == sec[1][0][k : k + 1, :], scale, 0.0)

    lane = iota((lc, tile), 1)
    low = lane < HALF
    inner = lax.rem(lane, HALF)

    def unfold(v):
        turned = pltpu.roll(v, HALF, 1)
        return jnp.where(low, v, turned), jnp.where(low, turned, v)

    for p in peers:
        link(0, sendx.at[number(*p)], recvx.at[number(*p)], p, number(*p)).wait_recv()
    for p in range(count):
        s, l, t = p // (n_line * n_tm), p // n_tm % n_line, p % n_tm
        v = recvx[p].astype(F32)
        for j in range(tl // tile):
            h, c = divmod(j * tile, tl // 2)
            two = unfold(v[h * lc : (h + 1) * lc, c : c + tile])
            for n in range(2):
                xs[1 + l, t * each + 2 * j + n, s] = two[n]
    link(1, sendm, recvm.at[n_line - 1 - at_line], other, number(*other)).wait_recv()
    for l in range(n_line):
        v = recvm[l].astype(F32)
        for g in range(n_mix):
            for j in range(blocks // 2):
                two = unfold(v[g * lc : (g + 1) * lc, j * tile : (j + 1) * tile])
                for n in range(2):
                    mx[2 * j + n, g * n_line + l] = two[n]

    cube = (shots, lc, tile)
    per = shots * lc
    clow = iota(cube, 2) < HALF
    line_of = iota(cube, 1)
    spot = lax.rem(iota((per, tile), 1), HALF)
    wide_spot = lax.rem(iota((per, 2 * tile), 1), HALF)
    early = spot < HALF // 2
    one = jnp.zeros((1, lc, tile), F32)
    nothing = jnp.zeros((per, 2 * tile), F32)

    def widen(make):
        ahead_of = [nothing, make(0)]
        for b in range(blocks):
            ahead_of.append(make(b + 1) if b + 1 < blocks else nothing)
            before, here, after = ahead_of[b : b + 3]
            zs[0, b * per : (b + 1) * per, :] = jnp.where(wide_spot == HALF - 1, before, here).astype(BF16)
            zs[1, b * per : (b + 1) * per, :] = jnp.where(wide_spot == 0, after, here).astype(BF16)

    def beside(before, here, after):
        both = jnp.where(clow, before, here)
        return jnp.concatenate([both.reshape(per, tile), after.reshape(per, tile)], axis=1)

    def change(b):
        return ys[b + 1, :, :tile] + jnp.where(early, ys[b, :, tile:], ys[b + 2, :, tile:])

    group = []
    for s in range(shots):
        found = jnp.int32(0)
        for k in range(shots):
            found = jnp.where(order[k] == s, k // run, found)
        group.append(found)
    rest = [lax.rem(lags[s], HALF) for s in range(shots)]
    far = [lags[s] // HALF for s in range(shots)]

    def over_lines(it, l):
        def make(b):
            x = xs[1 + l, b]
            before = jnp.where(line_of == lc - 1, xs[l, b], x)
            after = jnp.where(line_of == 0, xs[2 + l, b], x)
            return beside(pltpu.roll(before, 1, 1), x, pltpu.roll(after, lc - 1, 1))

        widen(make)
        layers(zs, hs, gs, ys, *ta)
        energy = jnp.zeros((lc, tile), F32)
        for b in range(blocks):
            x = (xs[1 + l, b] + change(b).reshape(cube)).astype(BF16).astype(F32)
            ps[l, b] = x
            energy = energy + jnp.sum(x * x, axis=0)
        energy = 0.5 * jnp.sum(energy, axis=1, keepdims=True)
        mine = jnp.sum(jnp.where(lane == iota((lc, tile), 0), energy, 0.0), axis=0, keepdims=True)
        at = it * n_line + l
        sende[at] = mine
        recve[at, me] = mine
        for p in peers:
            link(2 + at, sende.at[at], recve.at[at, me], p, me).start()

    def over_shots(it, l):
        at = it * n_line + l
        for p in peers:
            link(2 + at, sende.at[at], recve.at[at, number(*p)], p, number(*p)).wait_recv()
        total = jnp.zeros((lc, tile), F32)
        for k in range(count):
            total = total + member[k] * recve[at, k]
        mean = jnp.sum(total, axis=1, keepdims=True)
        rms = jnp.broadcast_to(jnp.sqrt(mean + EPSILON), (lc, tile)).reshape(1, lc, tile)
        inv = 1.0 / rms

        def make(b):
            x = (ps[l, b] * inv).astype(BF16).astype(F32)
            return beside(jnp.concatenate([one, x[: shots - 1]], axis=0), x, jnp.concatenate([x[1:], one], axis=0))

        widen(make)
        layers(zs, hs, gs, ys, *tb)
        for b in range(blocks):
            x = (ps[l, b] + rms * change(b).reshape(cube)).astype(BF16).astype(F32)
            ps[l, b] = x
            for s in range(shots):
                rolled[b + 2, s] = pltpu.roll(x[s], rest[s], 1)
        for g in range(n_mix):
            acc = -mx[:, g * n_line + l]
            for i in range(run):
                s = order[g * run + i]
                lag = lags[s]
                a = 2 - lag // HALF
                near, late = rolled[pl.ds(a, blocks), s], rolled[pl.ds(a - 1, blocks), s]
                acc = acc + jnp.where((inner >= lax.rem(lag, HALF))[None], near, late)
            mf[:blocks, g] = acc
        for s in range(shots):
            m = mf[:, group[s]]
            rolled[: blocks + 2, s] = pltpu.roll(m, lax.rem(tile - rest[s], tile), 2)
        for s in range(shots):
            near, late = rolled[pl.ds(far[s], blocks), s], rolled[pl.ds(far[s] + 1, blocks), s]
            back = jnp.where((inner < HALF - rest[s])[None], near, late)
            xs[1 + l, :, s] = (ps[l, :, s] - pace[it] * back).astype(BF16).astype(F32)
        rolled[:2] = jnp.zeros_like(rolled[:2])

        @pl.when(it == ITERS - 1)
        def _():
            for s in range(n_shot):
                for t in range(n_tm):
                    tiles = []
                    for j in range(tl // tile):
                        b = t * each + 2 * j
                        tiles.append(jnp.where(low, xs[1 + l, b, s], xs[1 + l, b + 1, s]))
                    n = len(tiles) // 2
                    halves = [jnp.concatenate(tiles[:n], axis=1), jnp.concatenate(tiles[n:], axis=1)]
                    backs[number(s, l, t)] = jnp.concatenate(halves, axis=0).astype(BF16)
            own = (at_shot, l, at_tm)
            for s in turns[0]:
                for t in turns[2]:
                    if s is at_shot and t is at_tm:
                        continue
                    link(back_kind, backs.at[number(s, l, t)], backr.at[me], (s, l, t), me).start()

            @pl.when(l != at_line)
            def _():
                link(back_kind, backs.at[number(*own)], backr.at[me], own, me).start()

    def iterate(it, carry):
        def lines(l, carry):
            over_lines(it, l)
            return carry

        def stations(l, carry):
            over_shots(it, l)
            return carry

        lax.fori_loop(0, n_line, lines, 0)
        lax.fori_loop(0, n_line, stations, 0)
        return carry

    lax.fori_loop(0, ITERS, iterate, 0)

    backr[me] = backs[me]
    row, col = iota((recv_n, recv_n), 0), iota((recv_n, recv_n), 1)
    perm = jnp.where(row == lax.rem(col, lc) * count + col // lc, 1.0, 0.0).astype(BF16)
    for p in peers:
        link(back_kind, backs.at[number(*p)], backr.at[number(*p)], p, number(*p)).wait_recv()
    v = []
    for k in range(count):
        part = backr[k].astype(F32)
        v.append(jnp.concatenate([part[:lc], part[lc:]], axis=1))
    v = jnp.concatenate(v, axis=0).astype(BF16)
    out[0] = jnp.dot(perm, v, preferred_element_type=F32).astype(BF16)
    link(1, sendm, recvm.at[at_line], other, me).wait_send()
    for p in peers:
        link(0, sendx.at[number(*p)], recvx.at[me], p, me).wait_send()
        for at in range(ITERS * n_line):
            link(2 + at, sende.at[at], recve.at[at, me], p, me).wait_send()
        link(back_kind, backs.at[number(*p)], backr.at[me], p, me).wait_send()


def patch(guess, mixtures, lags, order, tallies, wa, wb, pace, sizes):
    count = math.prod(sizes)
    n_shot, n_line, n_tm = sizes
    recv, tl = guess.shape[1:]
    n_mix, nt = mixtures.shape[0], mixtures.shape[2]
    lc, tile = recv // count, 2 * HALF
    blocks = nt // HALF
    per, feat = n_shot * lc, wa[0].shape[2]
    wide = feat * len(SLOT)
    rows = blocks * per
    weights = [w.transpose(1, 0, 2) if i == 0 else w for part in (wa, wb) for i, w in enumerate(part)]
    v, s, h = (pl.BlockSpec(memory_space=m) for m in (pltpu.VMEM, pltpu.SMEM, pl.ANY))
    slab = pltpu.VMEM((count, 2 * lc, tl // 2), BF16)
    woven = [
        pltpu.VMEM((2 * GROUPS, wide, wide), BF16),
        pltpu.VMEM((2, wide, wide), BF16),
        pltpu.VMEM((2 * GROUPS * wide, wide), BF16),
        pltpu.VMEM((2, wide), F32),
    ]
    kinds = 3 + ITERS * n_line
    return pl.pallas_call(
        functools.partial(patch_kernel, sizes),
        out_shape=jax.ShapeDtypeStruct(guess.shape, BF16),
        in_specs=[s] * 4 + [h] * 10,
        out_specs=v,
        scratch_shapes=[
            pltpu.VMEM((recv, tl), BF16),
            pltpu.VMEM(mixtures.shape, BF16),
            slab,
            slab,
            pltpu.VMEM((n_mix * lc, nt), BF16),
            pltpu.VMEM((n_line, n_mix * lc, nt), BF16),
            slab,
            slab,
            pltpu.VMEM((ITERS * n_line, 1, tile), F32),
            pltpu.VMEM((ITERS * n_line, count, 1, tile), F32),
            pltpu.VMEM((n_line + 2, blocks, n_shot, lc, tile), F32),
            pltpu.VMEM((n_line, blocks, n_shot, lc, tile), F32),
            pltpu.VMEM((blocks, n_mix * n_line, lc, tile), F32),
            pltpu.VMEM((blocks + 2, n_shot, lc, tile), F32),
            pltpu.VMEM((blocks + 2, n_mix, lc, tile), F32),
            pltpu.VMEM((count, lc, tile), F32),
            pltpu.VMEM((2, rows, wide), BF16),
            pltpu.VMEM((2, GROUPS * rows + 2 * per, wide), BF16),
            pltpu.VMEM((rows, 2 * GROUPS * wide), BF16),
            pltpu.VMEM((blocks + 2, per, wide), F32),
            *woven,
            *woven,
            *[pltpu.VMEM(w.shape, w.dtype) for w in weights],
            pltpu.SemaphoreType.DMA((2 + len(weights),)),
            pltpu.SemaphoreType.DMA((kinds, count)),
            pltpu.SemaphoreType.DMA((kinds, count)),
        ],
        compiler_params=pltpu.CompilerParams(vmem_limit_bytes=56 * 2**20, collective_id=1, has_side_effects=True),
    )(lags, order, tallies, pace, guess, mixtures, *weights)


def per_device(guess, mixtures, lags, order, tallies, e1, m1, x1, b1, e2, m2, x2, b2, pace):
    sh, recv, tl = guess.shape
    n_shot, n_line, n_tm = (lax.axis_size(a) for a in AXES)
    whole = RPL % (n_shot * n_line * n_tm) == 0
    where = AXES if whole else AXES[1:]
    parts = math.prod(lax.axis_size(a) for a in where)
    kp, lh = RPL // parts, recv // RPL
    lines, shots, nt = lh * n_line, sh * n_shot, tl * n_tm
    planes, s1 = nt // 2 // C, shots if whole else sh
    r1 = lines * kp
    r2 = r1 if whole else r1 // n_shot
    lanes1, lanes2 = 2 * s1 * r1, 2 * shots * r2
    sources = n_shot if whole else 1
    i32 = functools.partial(jnp.arange, dtype=jnp.int32)
    n_mix, feat = mixtures.shape[0], e1.shape[2]
    square = sh == 1 and kp == 1 and n_line == 2 and shots % n_mix == 0 and feat == HALF
    square = square and lh == C and tl % (4 * HALF) == 0 and n_mix * lh % 16 == 0
    square = square and lines == parts and 2 * (n_mix // n_line) == n_line
    if square:
        sizes = (n_shot, n_line, n_tm)
        return patch(guess, mixtures, lags, order, tallies, (e1, m1, x1, b1), (e2, m2, x2, b2), pace, sizes)

    at_shot = lax.axis_index("shot")
    n_mix, run = mixtures.shape[0], nt // C
    fused = whole and sh == 1 and kp == 1 and C % n_tm == 0 and n_shot * n_tm == C
    x = guess.reshape(sh, lh, parts, kp, tl).transpose(2, 0, 1, 3, 4)
    if fused:
        share = (at_shot * n_tm + lax.axis_index("tm")) * run
        mine = lax.dynamic_slice_in_dim(mixtures, share, run, axis=2).reshape(n_mix, lh, parts, run)
        mine = mine.transpose(2, 1, 0, 3).reshape(parts, lh, n_mix * run)
        x = jnp.concatenate([x.reshape(parts, lh, tl), mine], axis=2)
    x = lax.all_to_all(x, where, split_axis=0, concat_axis=0, tiled=False)
    if not fused:
        x = x.reshape(sources, n_line, n_tm, sh, lh, kp, tl).transpose(0, 3, 1, 4, 5, 2, 6)
        x = x.reshape(s1, r1, C, planes, 2).transpose(3, 2, 4, 0, 1).reshape(planes, C, lanes1)


    def first_k(line):
        block = line * n_tm + lax.axis_index("tm")
        return (at_shot * n_line * n_tm + block if whole else block) * kp

    if not fused:
        grid = mixtures.reshape(n_mix, lh, RPL, nt)
        sent = jnp.stack([lax.dynamic_slice_in_dim(grid, first_k(d), kp, axis=2) for d in range(n_line)])
        m = lax.all_to_all(sent, "line", split_axis=0, concat_axis=0)
        m = m.transpose(1, 0, 2, 3, 4).reshape(n_mix, r1, nt)
        if not whole:
            m = lax.dynamic_slice_in_dim(m, at_shot * r2, r2, axis=1)
        m = m.reshape(n_mix, r2, C, planes, 2).transpose(3, 2, 4, 0, 1).reshape(planes * C, 2 * n_mix * r2)

    np_ = tallies.shape[0]
    here = i32(np_)
    offsets = jnp.sum(jnp.where(here[None, :] < here[:, None], tallies[None, :], 0), axis=1)
    mine = first_k(lax.axis_index("line"))

    def one_hot(r):
        line, k = r // kp, mine + lax.rem(r, kp)
        q = lax.rem(line, lh) * RPL + k
        inside = (offsets[:, None] <= q[None, :]) & (q[None, :] < (offsets + tallies)[:, None])
        block = (line // lh)[None, :] == i32(n_line)[:, None]
        return (block[:, None, :] & inside[None, :, :]).reshape(n_line * np_, r.shape[0]).astype(F32)

    member = jnp.tile(one_hot(i32(r1)), (1, 2 * s1))
    r_own = i32(r2) if whole else at_shot * r2 + i32(r2)
    count = jnp.tile((tallies * (shots * nt)).astype(F32), n_line)
    spread = jnp.tile(one_hot(r_own) / count[:, None], (1, 2 * shots))

    sid = i32(shots)
    place = jnp.sum(jnp.where(order[None, :] == sid[:, None], sid[None, :], 0), axis=1)
    group = place // (shots // n_mix)
    same = (group[:, None] == group[None, :]).astype(BF16)
    chosen = (i32(n_mix)[:, None] == group[None, :]).astype(BF16)
    rest, two = jnp.eye(r2, dtype=BF16), jnp.eye(2, dtype=BF16)
    join = jnp.kron(two, jnp.kron(same, rest))
    take = jnp.kron(two, jnp.kron(chosen, rest))

    n1, n2 = s1 * r1, shots * r2
    a, b = np.arange(n1)[:, None], np.arange(n1)[None, :]
    near1 = np.stack([(a == b + (c - 1) * kp) & (a // r1 == b // r1) for c in range(3)])
    a, b = np.arange(n2)[:, None], np.arange(n2)[None, :]
    near2 = np.stack([a == b + (c - 1) * r2 for c in range(3)])
    wa = prepared(e1, m1, x1, b1, near1)
    wb = prepared(e2, m2, x2, b2, near2)

    rows = planes * C
    tot1, tot2 = pltpu.VMEM((rows, 2 * lanes1), F32), pltpu.VMEM((rows, 2 * lanes2), F32)
    feat = e1.shape[2]
    band = pltpu.VMEM((3 * PACK * feat, PACK * feat), BF16)
    buf = pltpu.VMEM((2, 2 * planes, C, lanes2), F32)
    spass = jax.ShapeDtypeStruct((planes, C, lanes1), BF16)
    part = jax.ShapeDtypeStruct((n_line * np_, 128), F32)
    moved = jax.ShapeDtypeStruct((planes, C, lanes2), BF16)

    def to_stations(y):
        y = y.reshape(rows, 2, sh, n_shot, r2)
        y = lax.all_to_all(y, "shot", split_axis=3, concat_axis=2, tiled=True)
        return y.reshape(planes, C, lanes2)

    def to_shots(y):
        y = y.reshape(rows, 2, shots, 1, r2)
        y = lax.all_to_all(y, "shot", split_axis=2, concat_axis=3, tiled=True)
        return y.reshape(planes, C, lanes1)

    dims = (n_shot, n_line, n_tm)
    cube = pltpu.VMEM((planes, C, lanes1), F32)
    if fused:
        mixed = jax.ShapeDtypeStruct((rows, 2 * n_mix * r2), BF16)
        side = pltpu.VMEM((planes, C, 2 * n_mix * r2), F32)
        sp, energy, m = call(
            functools.partial(entry_kernel, dims),
            (spass, part, mixed),
            (x, *wa, member),
            0,
            [tot1, band, cube, side],
        )
    else:
        sp, energy = call(first_kernel, (spass, part), (x, *wa, member), 0, [tot1, band])
    for it in range(ITERS):
        tot = summed(energy, (n_shot, n_line, n_tm)) if whole else lax.psum(energy, AXES)
        if not whole:
            sp = to_stations(sp)
        ins = (lags, pace, sp, tot, spread, *wb, join, m, take)
        if whole and it < ITERS - 1:
            sp, energy = call(
                functools.partial(both_kernel, it, shots), (spass, part), (*ins, *wa, member), 2, [buf, tot2, band]
            )
            continue
        if fused:
            back = jax.ShapeDtypeStruct((parts, lh, tl), BF16)
            x = call(functools.partial(exit_kernel, it, dims), back, ins, 2, [buf, tot2, band, cube])
            continue
        x = call(functools.partial(station_kernel, it, shots), moved, ins, 2, [buf, tot2, band])
        if not whole:
            x = to_shots(x)
            if it < ITERS - 1:
                sp, energy = call(first_kernel, (spass, part), (x, *wa, member), 0, [tot1, band])

    if not fused:
        x = x.reshape(planes, C, 2, s1, r1).transpose(3, 4, 1, 0, 2)
        x = x.reshape(sources, sh, n_line, lh, kp, n_tm, tl).transpose(0, 2, 5, 1, 3, 4, 6)
    x = lax.all_to_all(x.reshape(parts, sh, lh, kp, tl), where, split_axis=0, concat_axis=0)
    return x.transpose(1, 2, 0, 3, 4).reshape(sh, recv, tl)


def solution(mesh):
    spec = P(("group", "shot"), "line", "tm")
    placed = (spec, P("group", "line", None), P("group"), P("group"), P("group")) + (P(),) * 9
    return jax.shard_map(per_device, mesh=mesh, in_specs=placed, out_specs=spec, check_vma=False)
```

```python
import functools
import math

import jax
import jax.numpy as jnp
import numpy as np
from jax import lax
from jax.experimental import pallas as pl
from jax.experimental.pallas import tpu as pltpu
from jax.sharding import PartitionSpec as P

RPL = 16
ITERS = 2
EPSILON = 1e-05
C = 8
PACK = 4
TAPS = (1, 2, 3, 0)
F32, BF16 = jnp.float32, jnp.bfloat16
AXES = ("shot", "line", "tm")


def ahead(x, k):
    edge = pltpu.roll(x[:k], C - 1, 1)
    edge = jnp.where(lax.broadcasted_iota(jnp.int32, edge.shape, 1) == C - 1, 0.0, edge)
    return edge if k == x.shape[0] else jnp.concatenate([x[k:], edge], axis=0)


def behind(x, k):
    edge = pltpu.roll(x[x.shape[0] - k :], 1, 1)
    edge = jnp.where(lax.broadcasted_iota(jnp.int32, edge.shape, 1) == 0, 0.0, edge)
    return edge if k == x.shape[0] else jnp.concatenate([edge, x[: x.shape[0] - k]], axis=0)


def even_lanes(shape):
    return lax.broadcasted_iota(jnp.int32, shape, len(shape) - 1) < shape[-1] // 2


def net(x, w_in, pick, w_mid, w_out, place, bias, total, band):
    planes, _, lanes = x.shape
    rows = planes * C
    side = jnp.where(even_lanes(x.shape), ahead(x, 1), behind(x, 1))
    z = jnp.concatenate([x, side], axis=2).astype(BF16).reshape(rows, 2 * lanes)
    total[...] = jnp.zeros_like(total)
    wide = w_in.shape[1]
    feat = wide // PACK
    for j in range(3):
        tap = w_mid[j].astype(F32)
        for i in range(PACK):
            row = [tap if p == i else jnp.zeros_like(tap) for p in range(PACK)]
            at = (j * PACK + i) * feat
            band[at : at + feat, :] = jnp.concatenate(row, axis=1).astype(BF16)

    def step(q, carry):
        w_here = jnp.dot(pick[q], w_in[...], preferred_element_type=F32).astype(BF16)
        o_here = jnp.dot(w_out[...], place[q], preferred_element_type=F32).astype(BF16)
        h = jnp.dot(z, w_here, preferred_element_type=F32)
        h = jnp.maximum(h + bias[0:1, :], 0.0)
        cube = h.reshape(planes, C, wide)
        first = ahead(cube[:2], 2).reshape(2 * C, wide).astype(BF16)
        last = behind(cube[planes - 2 :], 2).reshape(2 * C, wide).astype(BF16)
        hb = h.astype(BF16)
        early = jnp.concatenate([last, hb[: rows - 2 * C]], axis=0)
        late = jnp.concatenate([hb[2 * C :], first], axis=0)
        g = jnp.dot(jnp.concatenate([early, hb, late], axis=1), band[...], preferred_element_type=F32)
        g = jnp.maximum(g + bias[1:2, :], 0.0).astype(BF16)
        total[...] += jnp.dot(g, o_here, preferred_element_type=F32)
        return carry

    lax.fori_loop(0, pick.shape[0], step, 0, unroll=2)
    y = total[...].reshape(planes, C, 2 * lanes)
    a, b = y[:, :, :lanes], y[:, :, lanes:]
    return a + jnp.where(even_lanes(b.shape), behind(b, 1), ahead(b, 1))


def shot_step(x, weights, member, out_ref, part_ref, total, band):
    y = (x + net(x, *weights, total, band)).astype(BF16)
    out_ref[...] = y
    y = y.astype(F32)
    energy = jnp.sum(jnp.sum(y * y, axis=0), axis=0, keepdims=True)
    sums = jnp.sum(member[...] * energy, axis=1, keepdims=True)
    part_ref[...] = jnp.broadcast_to(sums, part_ref.shape)


def shifted(buf, lag_ref, shots, forward):
    planes, lanes = buf.shape[1] // 2, buf.shape[3]
    shape = (planes, C, lanes)
    even = even_lanes(shape)
    per = lanes // 2 // shots
    lane_shot = lax.rem(lax.broadcasted_iota(jnp.int32, shape, 2), lanes // 2) // per
    out = jnp.zeros(shape, F32)
    for s in range(shots):
        lag = lag_ref[s]
        half, odd = lag // 2, lax.rem(lag, 2)
        at_even = half if forward else planes - half - odd
        at_odd = half + odd if forward else planes - half
        one = jnp.where(even, buf[odd, pl.ds(at_even, planes)], buf[odd, pl.ds(at_odd, planes)])
        out = jnp.where(lane_shot == s, one, out)
    return out


def station_step(shots, sp, tot_ref, spread, weights, lags, join, mix, take, pace, buf, total, band):
    planes, _, lanes = sp.shape
    rows = planes * C
    mean = jnp.sum(tot_ref[:, 0:1] * spread[...], axis=0, keepdims=True)
    rms = jnp.sqrt(mean + EPSILON).reshape(1, 1, lanes)
    normed = (sp / rms).astype(BF16).astype(F32)
    settled = (sp + rms * net(normed, *weights, total, band)).astype(BF16).astype(F32)

    def fill(x, forward):
        far = ahead(x, planes) if forward else behind(x, planes)
        near_at, far_at = (0, planes) if forward else (planes, 0)
        for v, at in ((x, near_at), (far, far_at)):
            buf[0, at : at + planes] = v
            h = lanes // 2
            buf[1, at : at + planes] = jnp.concatenate([v[:, :, h:], v[:, :, :h]], axis=2)

    fill(settled, False)
    fired = shifted(buf, lags, shots, False).astype(BF16).reshape(rows, lanes)
    misfit = jnp.dot(fired, join[...], preferred_element_type=F32)
    misfit -= jnp.dot(mix[...], take[...], preferred_element_type=F32)
    fill(misfit.reshape(planes, C, lanes), True)
    return (settled - pace * shifted(buf, lags, shots, True)).astype(BF16)


def by_phase(width):
    row = lax.broadcasted_iota(jnp.int32, (width, width), 0)
    col = lax.broadcasted_iota(jnp.int32, (width, width), 1)
    half = width // 2
    return jnp.where(col == 2 * lax.rem(row, half) + row // half, 1.0, 0.0).astype(BF16)


def unfold(read, into, sort):
    planes = into.shape[0]
    for c in range(C):
        v = lax.dot_general(sort, read(c), (((1,), (1,)), ((), ())), preferred_element_type=F32)
        into[:, c, :] = jnp.concatenate([v[:planes], v[planes:]], axis=1)


def entry_kernel(
    dims, x, wi, wp, wm, wo, wq, bi, member, out, part, mix, total, band, cube, side
):
    shots, blocks, halves = dims
    width = 2 * cube.shape[0]
    sort, each = by_phase(width), C // halves

    def traces(c):
        at, t = slice(c % each * width, (c % each + 1) * width), c // each
        rows = [x[(s * blocks + b) * halves + t, :, at].astype(F32) for s in range(shots) for b in range(blocks)]
        return jnp.concatenate(rows, axis=0).astype(BF16)

    tl = each * width

    def records(c):
        s, t = c // halves, c % halves
        rows = [
            x[(s * blocks + b) * halves + t, :, tl + g * width : tl + (g + 1) * width].astype(F32)
            for g in range((x.shape[2] - tl) // width)
            for b in range(blocks)
        ]
        return jnp.concatenate(rows, axis=0).astype(BF16)

    unfold(records, side, sort)
    mix[...] = side[...].astype(BF16).reshape(mix.shape)
    unfold(traces, cube, sort)
    shot_step(cube[...], (wi, wp, wm, wo, wq, bi), member, out, part, total, band)


def exit_kernel(
    it, dims, lags, pace, sp, tot, spread, wi, wp, wm, wo, wq, bi, join, mix, take, out, buf, total, band, cube
):
    shots, blocks, halves = dims
    width = 2 * cube.shape[0]
    sort, each = by_phase(width), C // halves
    x = station_step(
        shots, sp[...].astype(F32), tot, spread, (wi, wp, wm, wo, wq, bi), lags, join, mix, take, pace[it], buf, total, band
    )
    cube[...] = x.astype(F32)
    n, lh = cube.shape[2] // 2, out.shape[1]
    for c in range(C):
        v = cube[:, c, :]
        v = jnp.concatenate([v[:, :n], v[:, n:]], axis=0).T.astype(BF16)
        v = jnp.dot(v, sort, preferred_element_type=F32)
        at, t = slice(c % each * width, (c % each + 1) * width), c // each
        for j in range(shots * blocks):
            out[j * halves + t, :, at] = v[j * lh : (j + 1) * lh].astype(BF16)


def first_kernel(x, wi, wp, wm, wo, wq, bi, member, out, part, total, band):
    shot_step(x[...].astype(F32), (wi, wp, wm, wo, wq, bi), member, out, part, total, band)


def station_kernel(it, shots, lags, pace, sp, tot, spread, wi, wp, wm, wo, wq, bi, join, mix, take, out, buf, total, band):
    out[...] = station_step(
        shots, sp[...].astype(F32), tot, spread, (wi, wp, wm, wo, wq, bi), lags, join, mix, take, pace[it], buf, total, band
    )


def both_kernel(
    it, shots, lags, pace, sp, tot, spread, wi, wp, wm, wo, wq, bi, join, mix, take, vi, vp, vm, vo, vq, ci, member, out, part, buf, total, band
):
    x = station_step(
        shots, sp[...].astype(F32), tot, spread, (wi, wp, wm, wo, wq, bi), lags, join, mix, take, pace[it], buf, total, band
    )
    shot_step(x.astype(F32), (vi, vp, vm, vo, vq, ci), member, out, part, total, band)


def call(body, outs, ins, smem, scratch):
    v, s = pl.BlockSpec(memory_space=pltpu.VMEM), pl.BlockSpec(memory_space=pltpu.SMEM)
    return pl.pallas_call(
        body,
        out_shape=outs,
        in_specs=[s] * smem + [v] * (len(ins) - smem),
        out_specs=jax.tree.map(lambda _: v, outs),
        scratch_shapes=scratch,
        compiler_params=pltpu.CompilerParams(vmem_limit_bytes=48 * 2**20),
    )(*ins)


def prepared(w_in, w_mid, w_out, bias, near):
    n, feat = near.shape[1], w_in.shape[2]
    tiles = n // PACK
    cols = near.reshape(3, n, tiles, PACK).transpose(2, 1, 0, 3)
    pick = np.einsum("jk,tnci->tjnkci", np.eye(4)[list(TAPS)], cols).reshape(tiles, 4 * n, 12 * PACK)
    place = np.einsum("kj,tin->tjikn", np.eye(4)[list(TAPS)], np.eye(n).reshape(tiles, PACK, n)).reshape(tiles, 4 * PACK, 4 * n)
    w1 = w_in.reshape(12, 1, 1, feat)
    eye = jnp.eye(PACK, dtype=BF16)
    rows = (w1 * eye[None, :, :, None]).reshape(12 * PACK, PACK * feat)
    w2 = w_out.T.reshape(1, feat, 4, 1)
    ends = (w2 * eye[:, None, None, :]).reshape(PACK * feat, 4 * PACK)
    return rows, jnp.asarray(pick, BF16), w_mid, ends, jnp.asarray(place, BF16), jnp.tile(bias, (1, PACK))


def exchange_kernel(sizes, x, out, slots, send, recv):
    count = math.prod(sizes)
    me = (lax.axis_index("shot") * sizes[1] + lax.axis_index("line")) * sizes[2] + lax.axis_index("tm")

    def peer(off):
        at = lax.rem(me + off, count)
        return {
            "shot": at // (sizes[1] * sizes[2]),
            "line": lax.rem(at // sizes[2], sizes[1]),
            "tm": lax.rem(at, sizes[2]),
        }

    barrier = pltpu.get_barrier_semaphore()
    for off in range(1, count):
        pl.semaphore_signal(barrier, inc=1, device_id=peer(off), device_id_type=pl.DeviceIdType.MESH)
    pl.semaphore_wait(barrier, count - 1)
    copies = []
    for off in range(1, count):
        copy = pltpu.make_async_remote_copy(
            src_ref=x,
            dst_ref=slots.at[off],
            send_sem=send.at[off],
            recv_sem=recv.at[off],
            device_id=peer(off),
            device_id_type=pl.DeviceIdType.MESH,
        )
        copy.start()
        copies.append(copy)
    total = x[...]
    for off, copy in enumerate(copies, 1):
        copy.wait()
        total += slots[off]
    out[...] = total


def summed(x, sizes):
    count, v = math.prod(sizes), pl.BlockSpec(memory_space=pltpu.VMEM)
    return pl.pallas_call(
        functools.partial(exchange_kernel, sizes),
        out_shape=jax.ShapeDtypeStruct(x.shape, x.dtype),
        in_specs=[v],
        out_specs=v,
        scratch_shapes=[
            pltpu.VMEM((count, *x.shape), x.dtype),
            pltpu.SemaphoreType.DMA((count,)),
            pltpu.SemaphoreType.DMA((count,)),
        ],
        compiler_params=pltpu.CompilerParams(collective_id=0, has_side_effects=True),
    )(x)


SLOT = (0, 3, 1, 2)
HALF = 64
GROUPS = 4


def iota(shape, dim):
    return lax.broadcasted_iota(jnp.int32, shape, dim)


def weave(w_in, w_mid, w_out, bias, we, wm, wo, bi):
    feat = w_in.shape[2]
    wide = feat * len(SLOT)
    row, lane = iota((wide, wide), 0), iota((wide, wide), 1)
    at, ch = lax.rem(row, HALF), row // HALF
    slot = lane // feat
    pos = jnp.where(slot == 1, 3, jnp.where(slot == 0, 0, slot - 1))
    taps = w_in[...].astype(F32)
    for par in range(2):
        turned = lax.rem(at + (1 if par == 0 else HALF - 1), HALF)
        tap = lax.rem(turned, 4)
        base = jnp.zeros((wide, wide), F32)
        for c in range(3):
            for t in range(4):
                line = jnp.concatenate([taps[c, t : t + 1, :]] * len(SLOT), axis=1)
                base = jnp.where((ch == c) & (tap == t), line, base)
        for g in range(GROUPS):
            we[par * GROUPS + g] = jnp.where(turned // 4 == 4 * g + pos, base, 0.0).astype(BF16)
    zero = jnp.zeros((feat, feat), F32)
    mid = [w_mid[j].astype(F32) for j in range(3)]

    def block(came, goes):
        j = came - goes + 1
        return mid[j] if 0 <= j < 3 else zero

    for n, came in enumerate(SLOT):
        blocks = [block(came, goes) for goes in SLOT]
        wm[0, n * feat : (n + 1) * feat, :] = jnp.concatenate(blocks, axis=1).astype(BF16)
    for n in range(4):
        blocks = [zero] * 4
        blocks[n ^ 1] = mid[2 if n % 2 == 0 else 0]
        wm[1, n * feat : (n + 1) * feat, :] = jnp.concatenate(blocks, axis=1).astype(BF16)

    def sample(shape):
        col = iota(shape, 1)
        m = lax.rem(col, HALF)
        edge = jnp.where(m == HALF - 1, -1, jnp.where(m == 0, HALF, -4 * HALF))
        return jnp.where(col >= 2 * HALF, edge, m)

    near, far = sample((4, wide)), sample((feat, wide))
    for par in range(2):
        pick = jnp.where(lax.rem(near - 2 * par + 1 + 8 * HALF, 4) == iota((4, wide), 0), 1.0, 0.0).astype(BF16)
        base = lax.dot_general(w_out[...], pick, (((0,), (0,)), ((), ())), preferred_element_type=F32)
        for g in range(GROUPS):
            for n, i in enumerate(SLOT):
                d = far - 4 * (4 * g + i) - 2 * par + 1
                at = ((par * GROUPS + g) * len(SLOT) + n) * feat
                wo[at : at + feat, :] = jnp.where((d >= 0) & (d < 4), base, 0.0).astype(BF16)
    bi[...] = jnp.concatenate([bias[...]] * len(SLOT), axis=1)


def rectified(h, bias):
    cubes = h.reshape(h.shape[0] // bias.shape[0], bias.shape[0], h.shape[1])
    return jnp.maximum(cubes + bias[None], 0.0).reshape(h.shape)


def layers(zs, hs, gs, ys, we, wm, wo, b0, b1):
    rows, wide = zs.shape[1:]
    blocks = ys.shape[0] - 2
    per, half = rows // blocks, wide // 2
    for par in range(2):
        for g in range(GROUPS):
            h = jnp.dot(zs[par], we[par * GROUPS + g], preferred_element_type=F32)
            h = rectified(h, b0).astype(BF16)
            for b in range(blocks):
                at = per + (b * GROUPS + g) * per
                hs[par, at : at + per, :] = h[b * per : (b + 1) * per]
    low = iota((rows, half), 1) < half // 2
    for r in range(per, per + GROUPS * rows, rows):
        edge = [jnp.where(low, hs[par, r + per : r + per + rows, :half], hs[par, r - per : r - per + rows, :half]) for par in range(2)]
        edge = jnp.dot(jnp.concatenate(edge, axis=1), wm[1], preferred_element_type=F32)
        for par in range(2):
            g = jnp.dot(hs[par, r : r + rows, :], wm[0], preferred_element_type=F32)
            ends = g[:, :half] + edge[:, par * half : (par + 1) * half]
            g = [rectified(ends, b1[:, :half]), rectified(g[:, half:], b1[:, half:])]
            for n in range(rows // per):
                b, q = divmod(r // per - 1 + n, GROUPS)
                for i in range(2):
                    col = (par * GROUPS + q) * wide + i * half
                    gs[b * per : (b + 1) * per, col : col + half] = g[i][n * per : (n + 1) * per].astype(BF16)
    part = blocks // 4
    for b in range(0, blocks, part):
        y = jnp.dot(gs[b * per : (b + part) * per, :], wo[...], preferred_element_type=F32)
        ys[1 + b : 1 + b + part] = y.reshape(part, per, wide)


def patch_kernel(sizes, *refs):
    scalars, (guess, mixtures), refs = refs[:4], refs[4:6], refs[6:]
    lags, order, tallies, pace = refs[45:49]
    given, out = refs[:8], refs[8]
    (gbuf, mbuf, sendx, recvx, sendm, recvm, backs, backr, sende, recve) = refs[9:19]
    (xs, ps, mx, rolled, mf, member, zs, hs, gs, ys) = refs[19:29]
    ta, tb, held = refs[29:33], refs[33:37], refs[37:45]
    load_sem, ssem, rsem = refs[49:]
    n_shot, n_line, n_tm = sizes
    count = math.prod(sizes)
    axes = [lax.axis_index(a) for a in AXES]
    turns = [[axes[i]] + [lax.rem(axes[i] + d, n) for d in range(1, n)] for i, n in enumerate(sizes)]
    at_shot, at_line, at_tm = axes

    def number(s, l, t):
        return (s * n_line + l) * n_tm + t

    def device(s, l, t):
        return {"shot": s, "line": l, "tm": t}

    me = number(*axes)
    peers = [(s, l, t) for s in turns[0] for l in turns[1] for t in turns[2]][1:]
    shots = n_shot
    n_mix = mixtures.shape[0]
    run = shots // n_mix
    recv_n, tl = guess.shape[1:]
    lc = recv_n // count
    tile = 2 * HALF
    blocks = tl * n_tm // HALF
    each = tl // HALF
    back_kind = 2 + ITERS * n_line

    barrier = pltpu.get_barrier_semaphore()
    for p in peers:
        pl.semaphore_signal(barrier, inc=1, device_id=device(*p), device_id_type=pl.DeviceIdType.MESH)
    pairs = [(guess.at[0], gbuf), (mixtures, mbuf)] + list(zip(given, held)) + list(zip(scalars, refs[45:49]))
    loads = [pltpu.make_async_copy(a, b, load_sem.at[i]) for i, (a, b) in enumerate(pairs)]
    for copy in loads:
        copy.start()

    def link(which, src, dst, to, came):
        return pltpu.make_async_remote_copy(
            src_ref=src,
            dst_ref=dst,
            send_sem=ssem.at[which, number(*to)],
            recv_sem=rsem.at[which, came],
            device_id=device(*to),
            device_id_type=pl.DeviceIdType.MESH,
        )

    row, col = iota((recv_n, recv_n), 0), iota((recv_n, recv_n), 1)
    perm = jnp.where(col == lax.rem(row, lc) * count + row // lc, 1.0, 0.0).astype(BF16)
    loads[0].wait()
    v = jnp.dot(perm, gbuf[...], preferred_element_type=F32)
    for k in range(count):
        part = v[k * lc : (k + 1) * lc]
        sendx[k] = jnp.concatenate([part[:, : tl // 2], part[:, tl // 2 :]], axis=0).astype(BF16)
    pl.semaphore_wait(barrier, count - 1)
    for p in peers:
        link(0, sendx.at[number(*p)], recvx.at[me], p, me).start()

    loads[1].wait()
    other = (at_shot, n_line - 1 - at_line, at_tm)
    row, col = iota((2 * lc, recv_n), 0), iota((2 * lc, recv_n), 1)
    wanted = jnp.where(row < lc, me, number(*other))
    pick = jnp.where(col == lax.rem(row, lc) * count + wanted, 1.0, 0.0).astype(BF16)
    picked = [jnp.dot(pick, mbuf[g], preferred_element_type=F32) for g in range(n_mix)]
    sendm[...] = jnp.concatenate([p[lc:] for p in picked], axis=0).astype(BF16)
    link(1, sendm, recvm.at[at_line], other, me).start()
    recvm[at_line] = jnp.concatenate([p[:lc] for p in picked], axis=0).astype(BF16)
    recvx[me] = sendx[me]

    for copy in loads[2:]:
        copy.wait()
    weave(*held[:4], *ta)
    weave(*held[4:], *tb)
    edges = hs.shape[1] - (GROUPS * blocks + 1) * (hs.shape[1] // (GROUPS * blocks + 2))
    hs[:, :edges] = jnp.zeros_like(hs[:, :edges])
    hs[:, hs.shape[1] - edges :] = jnp.zeros_like(hs[:, :edges])
    for ref in (ys, rolled, mf, xs):
        ref[0] = jnp.zeros_like(ref[0])
        ref[ref.shape[0] - 1] = jnp.zeros_like(ref[0])
    for ref, at in ((rolled, 1), (mf, blocks)):
        ref[at] = jnp.zeros_like(ref[at])
    sec = []
    for rows in ((lc, tile), (count, tile)):
        if rows[0] == lc:
            q = iota(rows, 0) * count + me
        else:
            q = lax.rem(iota(rows, 1), lc) * count + iota(rows, 0)
        edge, at, size = jnp.int32(0), jnp.zeros(rows, jnp.int32), jnp.zeros(rows, jnp.int32)
        for p in range(tallies.shape[0]):
            at = jnp.where(q >= edge, p, at)
            size = jnp.where(q >= edge, tallies[p], size)
            edge = edge + tallies[p]
        sec.append((at, size))
    scale = 1.0 / (sec[0][1] * (shots * tl * n_tm)).astype(F32)
    for k in range(count):
        member[k] = jnp.where(sec[0][0] == sec[1][0][k : k + 1, :], scale, 0.0)

    lane = iota((lc, tile), 1)
    low = lane < HALF
    inner = lax.rem(lane, HALF)

    def unfold(v):
        turned = pltpu.roll(v, HALF, 1)
        return jnp.where(low, v, turned), jnp.where(low, turned, v)

    for p in peers:
        link(0, sendx.at[number(*p)], recvx.at[number(*p)], p, number(*p)).wait_recv()
    for p in range(count):
        s, l, t = p // (n_line * n_tm), p // n_tm % n_line, p % n_tm
        v = recvx[p].astype(F32)
        for j in range(tl // tile):
            h, c = divmod(j * tile, tl // 2)
            two = unfold(v[h * lc : (h + 1) * lc, c : c + tile])
            for n in range(2):
                xs[1 + l, t * each + 2 * j + n, s] = two[n]
    link(1, sendm, recvm.at[n_line - 1 - at_line], other, number(*other)).wait_recv()
    for l in range(n_line):
        v = recvm[l].astype(F32)
        for g in range(n_mix):
            for j in range(blocks // 2):
                two = unfold(v[g * lc : (g + 1) * lc, j * tile : (j + 1) * tile])
                for n in range(2):
                    mx[2 * j + n, g * n_line + l] = two[n]

    cube = (shots, lc, tile)
    per = shots * lc
    clow = iota(cube, 2) < HALF
    line_of = iota(cube, 1)
    spot = lax.rem(iota((per, tile), 1), HALF)
    wide_spot = lax.rem(iota((per, 2 * tile), 1), HALF)
    early = spot < HALF // 2
    one = jnp.zeros((1, lc, tile), F32)
    nothing = jnp.zeros((per, 2 * tile), F32)

    def widen(make):
        ahead_of = [nothing, make(0)]
        for b in range(blocks):
            ahead_of.append(make(b + 1) if b + 1 < blocks else nothing)
            before, here, after = ahead_of[b : b + 3]
            zs[0, b * per : (b + 1) * per, :] = jnp.where(wide_spot == HALF - 1, before, here).astype(BF16)
            zs[1, b * per : (b + 1) * per, :] = jnp.where(wide_spot == 0, after, here).astype(BF16)

    def beside(before, here, after):
        both = jnp.where(clow, before, here)
        return jnp.concatenate([both.reshape(per, tile), after.reshape(per, tile)], axis=1)

    def change(b):
        return ys[b + 1, :, :tile] + jnp.where(early, ys[b, :, tile:], ys[b + 2, :, tile:])

    group = []
    for s in range(shots):
        found = jnp.int32(0)
        for k in range(shots):
            found = jnp.where(order[k] == s, k // run, found)
        group.append(found)
    rest = [lax.rem(lags[s], HALF) for s in range(shots)]
    far = [lags[s] // HALF for s in range(shots)]

    def over_lines(it, l):
        def make(b):
            x = xs[1 + l, b]
            before = jnp.where(line_of == lc - 1, xs[l, b], x)
            after = jnp.where(line_of == 0, xs[2 + l, b], x)
            return beside(pltpu.roll(before, 1, 1), x, pltpu.roll(after, lc - 1, 1))

        widen(make)
        biases = [jnp.broadcast_to(ta[3][i : i + 1, :], (lc, 2 * tile)) for i in range(2)]
        layers(zs, hs, gs, ys, *ta[:3], *biases)
        energy = jnp.zeros((lc, tile), F32)
        for b in range(blocks):
            x = (xs[1 + l, b] + change(b).reshape(cube)).astype(BF16).astype(F32)
            ps[l, b] = x
            energy = energy + jnp.sum(x * x, axis=0)
        energy = 0.5 * jnp.sum(energy, axis=1, keepdims=True)
        mine = jnp.sum(jnp.where(lane == iota((lc, tile), 0), energy, 0.0), axis=0, keepdims=True)
        at = it * n_line + l
        sende[at] = mine
        recve[at, me] = mine
        for p in peers:
            link(2 + at, sende.at[at], recve.at[at, me], p, me).start()

    def over_shots(it, l):
        def make(b):
            x = ps[l, b]
            return beside(jnp.concatenate([one, x[: shots - 1]], axis=0), x, jnp.concatenate([x[1:], one], axis=0))

        widen(make)
        at = it * n_line + l
        for p in peers:
            link(2 + at, sende.at[at], recve.at[at, number(*p)], p, number(*p)).wait_recv()
        total = jnp.zeros((lc, tile), F32)
        for k in range(count):
            total = total + member[k] * recve[at, k]
        mean = jnp.sum(total, axis=1, keepdims=True)
        rms = jnp.broadcast_to(jnp.sqrt(mean + EPSILON), (lc, 2 * tile))
        biases = [rms * tb[3][i : i + 1, :] for i in range(2)]
        layers(zs, hs, gs, ys, *tb[:3], *biases)
        for b in range(blocks):
            x = (ps[l, b] + change(b).reshape(cube)).astype(BF16).astype(F32)
            ps[l, b] = x
            for s in range(shots):
                rolled[b + 2, s] = pltpu.roll(x[s], rest[s], 1)
        for g in range(n_mix):
            acc = -mx[:, g * n_line + l]
            for i in range(run):
                s = order[g * run + i]
                lag = lags[s]
                a = 2 - lag // HALF
                near, late = rolled[pl.ds(a, blocks), s], rolled[pl.ds(a - 1, blocks), s]
                acc = acc + jnp.where((inner >= lax.rem(lag, HALF))[None], near, late)
            mf[:blocks, g] = acc
        for s in range(shots):
            m = mf[:, group[s]]
            rolled[: blocks + 2, s] = pltpu.roll(m, lax.rem(tile - rest[s], tile), 2)
        for s in range(shots):
            near, late = rolled[pl.ds(far[s], blocks), s], rolled[pl.ds(far[s] + 1, blocks), s]
            back = jnp.where((inner < HALF - rest[s])[None], near, late)
            xs[1 + l, :, s] = (ps[l, :, s] - pace[it] * back).astype(BF16).astype(F32)
        rolled[:2] = jnp.zeros_like(rolled[:2])

        @pl.when(it == ITERS - 1)
        def _():
            for s in range(n_shot):
                for t in range(n_tm):
                    tiles = []
                    for j in range(tl // tile):
                        b = t * each + 2 * j
                        tiles.append(jnp.where(low, xs[1 + l, b, s], xs[1 + l, b + 1, s]))
                    n = len(tiles) // 2
                    halves = [jnp.concatenate(tiles[:n], axis=1), jnp.concatenate(tiles[n:], axis=1)]
                    backs[number(s, l, t)] = jnp.concatenate(halves, axis=0).astype(BF16)
            own = (at_shot, l, at_tm)
            for s in turns[0]:
                for t in turns[2]:
                    if s is at_shot and t is at_tm:
                        continue
                    link(back_kind, backs.at[number(s, l, t)], backr.at[me], (s, l, t), me).start()

            @pl.when(l != at_line)
            def _():
                link(back_kind, backs.at[number(*own)], backr.at[me], own, me).start()

    def iterate(it, carry):
        def lines(l, carry):
            over_lines(it, l)
            return carry

        def stations(l, carry):
            over_shots(it, l)
            return carry

        lax.fori_loop(0, n_line, lines, 0)
        lax.fori_loop(0, n_line, stations, 0)
        return carry

    lax.fori_loop(0, ITERS, iterate, 0)

    backr[me] = backs[me]
    row, col = iota((recv_n, recv_n), 0), iota((recv_n, recv_n), 1)
    perm = jnp.where(row == lax.rem(col, lc) * count + col // lc, 1.0, 0.0).astype(BF16)
    for p in peers:
        link(back_kind, backs.at[number(*p)], backr.at[number(*p)], p, number(*p)).wait_recv()
    v = []
    for k in range(count):
        part = backr[k].astype(F32)
        v.append(jnp.concatenate([part[:lc], part[lc:]], axis=1))
    v = jnp.concatenate(v, axis=0).astype(BF16)
    out[0] = jnp.dot(perm, v, preferred_element_type=F32).astype(BF16)
    link(1, sendm, recvm.at[at_line], other, me).wait_send()
    for p in peers:
        link(0, sendx.at[number(*p)], recvx.at[me], p, me).wait_send()
        for at in range(ITERS * n_line):
            link(2 + at, sende.at[at], recve.at[at, me], p, me).wait_send()
        link(back_kind, backs.at[number(*p)], backr.at[me], p, me).wait_send()


def patch(guess, mixtures, lags, order, tallies, wa, wb, pace, sizes):
    count = math.prod(sizes)
    n_shot, n_line, n_tm = sizes
    recv, tl = guess.shape[1:]
    n_mix, nt = mixtures.shape[0], mixtures.shape[2]
    lc, tile = recv // count, 2 * HALF
    blocks = nt // HALF
    per, feat = n_shot * lc, wa[0].shape[2]
    wide = feat * len(SLOT)
    rows = blocks * per
    weights = [w.transpose(1, 0, 2) if i == 0 else w for part in (wa, wb) for i, w in enumerate(part)]
    v, h = (pl.BlockSpec(memory_space=m) for m in (pltpu.VMEM, pl.ANY))
    slab = pltpu.VMEM((count, 2 * lc, tl // 2), BF16)
    woven = [
        pltpu.VMEM((2 * GROUPS, wide, wide), BF16),
        pltpu.VMEM((2, wide, wide), BF16),
        pltpu.VMEM((2 * GROUPS * wide, wide), BF16),
        pltpu.VMEM((2, wide), F32),
    ]
    kinds = 3 + ITERS * n_line
    return pl.pallas_call(
        functools.partial(patch_kernel, sizes),
        out_shape=pltpu.VMEM(guess.shape, BF16),
        in_specs=[h] * 14,
        out_specs=v,
        scratch_shapes=[
            pltpu.VMEM((recv, tl), BF16),
            pltpu.VMEM(mixtures.shape, BF16),
            slab,
            slab,
            pltpu.VMEM((n_mix * lc, nt), BF16),
            pltpu.VMEM((n_line, n_mix * lc, nt), BF16),
            slab,
            slab,
            pltpu.VMEM((ITERS * n_line, 1, tile), F32),
            pltpu.VMEM((ITERS * n_line, count, 1, tile), F32),
            pltpu.VMEM((n_line + 2, blocks, n_shot, lc, tile), F32),
            pltpu.VMEM((n_line, blocks, n_shot, lc, tile), F32),
            pltpu.VMEM((blocks, n_mix * n_line, lc, tile), F32),
            pltpu.VMEM((blocks + 2, n_shot, lc, tile), F32),
            pltpu.VMEM((blocks + 2, n_mix, lc, tile), F32),
            pltpu.VMEM((count, lc, tile), F32),
            pltpu.VMEM((2, rows, wide), BF16),
            pltpu.VMEM((2, GROUPS * rows + 2 * per, wide), BF16),
            pltpu.VMEM((rows, 2 * GROUPS * wide), BF16),
            pltpu.VMEM((blocks + 2, per, wide), F32),
            *woven,
            *woven,
            *[pltpu.VMEM(w.shape, w.dtype) for w in weights],
            *[pltpu.SMEM(w.shape, w.dtype) for w in (lags, order, tallies, pace)],
            pltpu.SemaphoreType.DMA((6 + len(weights),)),
            pltpu.SemaphoreType.DMA((kinds, count)),
            pltpu.SemaphoreType.DMA((kinds, count)),
        ],
        compiler_params=pltpu.CompilerParams(vmem_limit_bytes=56 * 2**20, collective_id=1, has_side_effects=True),
    )(lags, order, tallies, pace, guess, mixtures, *weights)


def per_device(guess, mixtures, lags, order, tallies, e1, m1, x1, b1, e2, m2, x2, b2, pace):
    sh, recv, tl = guess.shape
    n_shot, n_line, n_tm = (lax.axis_size(a) for a in AXES)
    whole = RPL % (n_shot * n_line * n_tm) == 0
    where = AXES if whole else AXES[1:]
    parts = math.prod(lax.axis_size(a) for a in where)
    kp, lh = RPL // parts, recv // RPL
    lines, shots, nt = lh * n_line, sh * n_shot, tl * n_tm
    planes, s1 = nt // 2 // C, shots if whole else sh
    r1 = lines * kp
    r2 = r1 if whole else r1 // n_shot
    lanes1, lanes2 = 2 * s1 * r1, 2 * shots * r2
    sources = n_shot if whole else 1
    i32 = functools.partial(jnp.arange, dtype=jnp.int32)
    n_mix, feat = mixtures.shape[0], e1.shape[2]
    square = sh == 1 and kp == 1 and n_line == 2 and shots % n_mix == 0 and feat == HALF
    square = square and lh == C and tl % (4 * HALF) == 0 and n_mix * lh % 16 == 0
    square = square and lines == parts and 2 * (n_mix // n_line) == n_line
    if square:
        sizes = (n_shot, n_line, n_tm)
        return patch(guess, mixtures, lags, order, tallies, (e1, m1, x1, b1), (e2, m2, x2, b2), pace, sizes)

    at_shot = lax.axis_index("shot")
    n_mix, run = mixtures.shape[0], nt // C
    fused = whole and sh == 1 and kp == 1 and C % n_tm == 0 and n_shot * n_tm == C
    x = guess.reshape(sh, lh, parts, kp, tl).transpose(2, 0, 1, 3, 4)
    if fused:
        share = (at_shot * n_tm + lax.axis_index("tm")) * run
        mine = lax.dynamic_slice_in_dim(mixtures, share, run, axis=2).reshape(n_mix, lh, parts, run)
        mine = mine.transpose(2, 1, 0, 3).reshape(parts, lh, n_mix * run)
        x = jnp.concatenate([x.reshape(parts, lh, tl), mine], axis=2)
    x = lax.all_to_all(x, where, split_axis=0, concat_axis=0, tiled=False)
    if not fused:
        x = x.reshape(sources, n_line, n_tm, sh, lh, kp, tl).transpose(0, 3, 1, 4, 5, 2, 6)
        x = x.reshape(s1, r1, C, planes, 2).transpose(3, 2, 4, 0, 1).reshape(planes, C, lanes1)


    def first_k(line):
        block = line * n_tm + lax.axis_index("tm")
        return (at_shot * n_line * n_tm + block if whole else block) * kp

    if not fused:
        grid = mixtures.reshape(n_mix, lh, RPL, nt)
        sent = jnp.stack([lax.dynamic_slice_in_dim(grid, first_k(d), kp, axis=2) for d in range(n_line)])
        m = lax.all_to_all(sent, "line", split_axis=0, concat_axis=0)
        m = m.transpose(1, 0, 2, 3, 4).reshape(n_mix, r1, nt)
        if not whole:
            m = lax.dynamic_slice_in_dim(m, at_shot * r2, r2, axis=1)
        m = m.reshape(n_mix, r2, C, planes, 2).transpose(3, 2, 4, 0, 1).reshape(planes * C, 2 * n_mix * r2)

    np_ = tallies.shape[0]
    here = i32(np_)
    offsets = jnp.sum(jnp.where(here[None, :] < here[:, None], tallies[None, :], 0), axis=1)
    mine = first_k(lax.axis_index("line"))

    def one_hot(r):
        line, k = r // kp, mine + lax.rem(r, kp)
        q = lax.rem(line, lh) * RPL + k
        inside = (offsets[:, None] <= q[None, :]) & (q[None, :] < (offsets + tallies)[:, None])
        block = (line // lh)[None, :] == i32(n_line)[:, None]
        return (block[:, None, :] & inside[None, :, :]).reshape(n_line * np_, r.shape[0]).astype(F32)

    member = jnp.tile(one_hot(i32(r1)), (1, 2 * s1))
    r_own = i32(r2) if whole else at_shot * r2 + i32(r2)
    count = jnp.tile((tallies * (shots * nt)).astype(F32), n_line)
    spread = jnp.tile(one_hot(r_own) / count[:, None], (1, 2 * shots))

    sid = i32(shots)
    place = jnp.sum(jnp.where(order[None, :] == sid[:, None], sid[None, :], 0), axis=1)
    group = place // (shots // n_mix)
    same = (group[:, None] == group[None, :]).astype(BF16)
    chosen = (i32(n_mix)[:, None] == group[None, :]).astype(BF16)
    rest, two = jnp.eye(r2, dtype=BF16), jnp.eye(2, dtype=BF16)
    join = jnp.kron(two, jnp.kron(same, rest))
    take = jnp.kron(two, jnp.kron(chosen, rest))

    n1, n2 = s1 * r1, shots * r2
    a, b = np.arange(n1)[:, None], np.arange(n1)[None, :]
    near1 = np.stack([(a == b + (c - 1) * kp) & (a // r1 == b // r1) for c in range(3)])
    a, b = np.arange(n2)[:, None], np.arange(n2)[None, :]
    near2 = np.stack([a == b + (c - 1) * r2 for c in range(3)])
    wa = prepared(e1, m1, x1, b1, near1)
    wb = prepared(e2, m2, x2, b2, near2)

    rows = planes * C
    tot1, tot2 = pltpu.VMEM((rows, 2 * lanes1), F32), pltpu.VMEM((rows, 2 * lanes2), F32)
    feat = e1.shape[2]
    band = pltpu.VMEM((3 * PACK * feat, PACK * feat), BF16)
    buf = pltpu.VMEM((2, 2 * planes, C, lanes2), F32)
    spass = jax.ShapeDtypeStruct((planes, C, lanes1), BF16)
    part = jax.ShapeDtypeStruct((n_line * np_, 128), F32)
    moved = jax.ShapeDtypeStruct((planes, C, lanes2), BF16)

    def to_stations(y):
        y = y.reshape(rows, 2, sh, n_shot, r2)
        y = lax.all_to_all(y, "shot", split_axis=3, concat_axis=2, tiled=True)
        return y.reshape(planes, C, lanes2)

    def to_shots(y):
        y = y.reshape(rows, 2, shots, 1, r2)
        y = lax.all_to_all(y, "shot", split_axis=2, concat_axis=3, tiled=True)
        return y.reshape(planes, C, lanes1)

    dims = (n_shot, n_line, n_tm)
    cube = pltpu.VMEM((planes, C, lanes1), F32)
    if fused:
        mixed = jax.ShapeDtypeStruct((rows, 2 * n_mix * r2), BF16)
        side = pltpu.VMEM((planes, C, 2 * n_mix * r2), F32)
        sp, energy, m = call(
            functools.partial(entry_kernel, dims),
            (spass, part, mixed),
            (x, *wa, member),
            0,
            [tot1, band, cube, side],
        )
    else:
        sp, energy = call(first_kernel, (spass, part), (x, *wa, member), 0, [tot1, band])
    for it in range(ITERS):
        tot = summed(energy, (n_shot, n_line, n_tm)) if whole else lax.psum(energy, AXES)
        if not whole:
            sp = to_stations(sp)
        ins = (lags, pace, sp, tot, spread, *wb, join, m, take)
        if whole and it < ITERS - 1:
            sp, energy = call(
                functools.partial(both_kernel, it, shots), (spass, part), (*ins, *wa, member), 2, [buf, tot2, band]
            )
            continue
        if fused:
            back = jax.ShapeDtypeStruct((parts, lh, tl), BF16)
            x = call(functools.partial(exit_kernel, it, dims), back, ins, 2, [buf, tot2, band, cube])
            continue
        x = call(functools.partial(station_kernel, it, shots), moved, ins, 2, [buf, tot2, band])
        if not whole:
            x = to_shots(x)
            if it < ITERS - 1:
                sp, energy = call(first_kernel, (spass, part), (x, *wa, member), 0, [tot1, band])

    if not fused:
        x = x.reshape(planes, C, 2, s1, r1).transpose(3, 4, 1, 0, 2)
        x = x.reshape(sources, sh, n_line, lh, kp, n_tm, tl).transpose(0, 2, 5, 1, 3, 4, 6)
    x = lax.all_to_all(x.reshape(parts, sh, lh, kp, tl), where, split_axis=0, concat_axis=0)
    return x.transpose(1, 2, 0, 3, 4).reshape(sh, recv, tl)


def solution(mesh):
    spec = P(("group", "shot"), "line", "tm")
    placed = (spec, P("group", "line", None), P("group"), P("group"), P("group")) + (P(),) * 9
    return jax.shard_map(per_device, mesh=mesh, in_specs=placed, out_specs=spec, check_vma=False)
```

```python
import functools
import math

import jax
import jax.numpy as jnp
import numpy as np
from jax import lax
from jax.experimental import pallas as pl
from jax.experimental.pallas import tpu as pltpu
from jax.sharding import PartitionSpec as P

RPL = 16
ITERS = 2
EPSILON = 1e-05
C = 8
PACK = 4
TAPS = (1, 2, 3, 0)
F32, BF16 = jnp.float32, jnp.bfloat16
AXES = ("shot", "line", "tm")


def ahead(x, k):
    edge = pltpu.roll(x[:k], C - 1, 1)
    edge = jnp.where(lax.broadcasted_iota(jnp.int32, edge.shape, 1) == C - 1, 0.0, edge)
    return edge if k == x.shape[0] else jnp.concatenate([x[k:], edge], axis=0)


def behind(x, k):
    edge = pltpu.roll(x[x.shape[0] - k :], 1, 1)
    edge = jnp.where(lax.broadcasted_iota(jnp.int32, edge.shape, 1) == 0, 0.0, edge)
    return edge if k == x.shape[0] else jnp.concatenate([edge, x[: x.shape[0] - k]], axis=0)


def even_lanes(shape):
    return lax.broadcasted_iota(jnp.int32, shape, len(shape) - 1) < shape[-1] // 2


def net(x, w_in, pick, w_mid, w_out, place, bias, total, band):
    planes, _, lanes = x.shape
    rows = planes * C
    side = jnp.where(even_lanes(x.shape), ahead(x, 1), behind(x, 1))
    z = jnp.concatenate([x, side], axis=2).astype(BF16).reshape(rows, 2 * lanes)
    total[...] = jnp.zeros_like(total)
    wide = w_in.shape[1]
    feat = wide // PACK
    for j in range(3):
        tap = w_mid[j].astype(F32)
        for i in range(PACK):
            row = [tap if p == i else jnp.zeros_like(tap) for p in range(PACK)]
            at = (j * PACK + i) * feat
            band[at : at + feat, :] = jnp.concatenate(row, axis=1).astype(BF16)

    def step(q, carry):
        w_here = jnp.dot(pick[q], w_in[...], preferred_element_type=F32).astype(BF16)
        o_here = jnp.dot(w_out[...], place[q], preferred_element_type=F32).astype(BF16)
        h = jnp.dot(z, w_here, preferred_element_type=F32)
        h = jnp.maximum(h + bias[0:1, :], 0.0)
        cube = h.reshape(planes, C, wide)
        first = ahead(cube[:2], 2).reshape(2 * C, wide).astype(BF16)
        last = behind(cube[planes - 2 :], 2).reshape(2 * C, wide).astype(BF16)
        hb = h.astype(BF16)
        early = jnp.concatenate([last, hb[: rows - 2 * C]], axis=0)
        late = jnp.concatenate([hb[2 * C :], first], axis=0)
        g = jnp.dot(jnp.concatenate([early, hb, late], axis=1), band[...], preferred_element_type=F32)
        g = jnp.maximum(g + bias[1:2, :], 0.0).astype(BF16)
        total[...] += jnp.dot(g, o_here, preferred_element_type=F32)
        return carry

    lax.fori_loop(0, pick.shape[0], step, 0, unroll=2)
    y = total[...].reshape(planes, C, 2 * lanes)
    a, b = y[:, :, :lanes], y[:, :, lanes:]
    return a + jnp.where(even_lanes(b.shape), behind(b, 1), ahead(b, 1))


def shot_step(x, weights, member, out_ref, part_ref, total, band):
    y = (x + net(x, *weights, total, band)).astype(BF16)
    out_ref[...] = y
    y = y.astype(F32)
    energy = jnp.sum(jnp.sum(y * y, axis=0), axis=0, keepdims=True)
    sums = jnp.sum(member[...] * energy, axis=1, keepdims=True)
    part_ref[...] = jnp.broadcast_to(sums, part_ref.shape)


def shifted(buf, lag_ref, shots, forward):
    planes, lanes = buf.shape[1] // 2, buf.shape[3]
    shape = (planes, C, lanes)
    even = even_lanes(shape)
    per = lanes // 2 // shots
    lane_shot = lax.rem(lax.broadcasted_iota(jnp.int32, shape, 2), lanes // 2) // per
    out = jnp.zeros(shape, F32)
    for s in range(shots):
        lag = lag_ref[s]
        half, odd = lag // 2, lax.rem(lag, 2)
        at_even = half if forward else planes - half - odd
        at_odd = half + odd if forward else planes - half
        one = jnp.where(even, buf[odd, pl.ds(at_even, planes)], buf[odd, pl.ds(at_odd, planes)])
        out = jnp.where(lane_shot == s, one, out)
    return out


def station_step(shots, sp, tot_ref, spread, weights, lags, join, mix, take, pace, buf, total, band):
    planes, _, lanes = sp.shape
    rows = planes * C
    mean = jnp.sum(tot_ref[:, 0:1] * spread[...], axis=0, keepdims=True)
    rms = jnp.sqrt(mean + EPSILON).reshape(1, 1, lanes)
    normed = (sp / rms).astype(BF16).astype(F32)
    settled = (sp + rms * net(normed, *weights, total, band)).astype(BF16).astype(F32)

    def fill(x, forward):
        far = ahead(x, planes) if forward else behind(x, planes)
        near_at, far_at = (0, planes) if forward else (planes, 0)
        for v, at in ((x, near_at), (far, far_at)):
            buf[0, at : at + planes] = v
            h = lanes // 2
            buf[1, at : at + planes] = jnp.concatenate([v[:, :, h:], v[:, :, :h]], axis=2)

    fill(settled, False)
    fired = shifted(buf, lags, shots, False).astype(BF16).reshape(rows, lanes)
    misfit = jnp.dot(fired, join[...], preferred_element_type=F32)
    misfit -= jnp.dot(mix[...], take[...], preferred_element_type=F32)
    fill(misfit.reshape(planes, C, lanes), True)
    return (settled - pace * shifted(buf, lags, shots, True)).astype(BF16)


def by_phase(width):
    row = lax.broadcasted_iota(jnp.int32, (width, width), 0)
    col = lax.broadcasted_iota(jnp.int32, (width, width), 1)
    half = width // 2
    return jnp.where(col == 2 * lax.rem(row, half) + row // half, 1.0, 0.0).astype(BF16)


def unfold(read, into, sort):
    planes = into.shape[0]
    for c in range(C):
        v = lax.dot_general(sort, read(c), (((1,), (1,)), ((), ())), preferred_element_type=F32)
        into[:, c, :] = jnp.concatenate([v[:planes], v[planes:]], axis=1)


def entry_kernel(
    dims, x, wi, wp, wm, wo, wq, bi, member, out, part, mix, total, band, cube, side
):
    shots, blocks, halves = dims
    width = 2 * cube.shape[0]
    sort, each = by_phase(width), C // halves

    def traces(c):
        at, t = slice(c % each * width, (c % each + 1) * width), c // each
        rows = [x[(s * blocks + b) * halves + t, :, at].astype(F32) for s in range(shots) for b in range(blocks)]
        return jnp.concatenate(rows, axis=0).astype(BF16)

    tl = each * width

    def records(c):
        s, t = c // halves, c % halves
        rows = [
            x[(s * blocks + b) * halves + t, :, tl + g * width : tl + (g + 1) * width].astype(F32)
            for g in range((x.shape[2] - tl) // width)
            for b in range(blocks)
        ]
        return jnp.concatenate(rows, axis=0).astype(BF16)

    unfold(records, side, sort)
    mix[...] = side[...].astype(BF16).reshape(mix.shape)
    unfold(traces, cube, sort)
    shot_step(cube[...], (wi, wp, wm, wo, wq, bi), member, out, part, total, band)


def exit_kernel(
    it, dims, lags, pace, sp, tot, spread, wi, wp, wm, wo, wq, bi, join, mix, take, out, buf, total, band, cube
):
    shots, blocks, halves = dims
    width = 2 * cube.shape[0]
    sort, each = by_phase(width), C // halves
    x = station_step(
        shots, sp[...].astype(F32), tot, spread, (wi, wp, wm, wo, wq, bi), lags, join, mix, take, pace[it], buf, total, band
    )
    cube[...] = x.astype(F32)
    n, lh = cube.shape[2] // 2, out.shape[1]
    for c in range(C):
        v = cube[:, c, :]
        v = jnp.concatenate([v[:, :n], v[:, n:]], axis=0).T.astype(BF16)
        v = jnp.dot(v, sort, preferred_element_type=F32)
        at, t = slice(c % each * width, (c % each + 1) * width), c // each
        for j in range(shots * blocks):
            out[j * halves + t, :, at] = v[j * lh : (j + 1) * lh].astype(BF16)


def first_kernel(x, wi, wp, wm, wo, wq, bi, member, out, part, total, band):
    shot_step(x[...].astype(F32), (wi, wp, wm, wo, wq, bi), member, out, part, total, band)


def station_kernel(it, shots, lags, pace, sp, tot, spread, wi, wp, wm, wo, wq, bi, join, mix, take, out, buf, total, band):
    out[...] = station_step(
        shots, sp[...].astype(F32), tot, spread, (wi, wp, wm, wo, wq, bi), lags, join, mix, take, pace[it], buf, total, band
    )


def both_kernel(
    it, shots, lags, pace, sp, tot, spread, wi, wp, wm, wo, wq, bi, join, mix, take, vi, vp, vm, vo, vq, ci, member, out, part, buf, total, band
):
    x = station_step(
        shots, sp[...].astype(F32), tot, spread, (wi, wp, wm, wo, wq, bi), lags, join, mix, take, pace[it], buf, total, band
    )
    shot_step(x.astype(F32), (vi, vp, vm, vo, vq, ci), member, out, part, total, band)


def call(body, outs, ins, smem, scratch):
    v, s = pl.BlockSpec(memory_space=pltpu.VMEM), pl.BlockSpec(memory_space=pltpu.SMEM)
    return pl.pallas_call(
        body,
        out_shape=outs,
        in_specs=[s] * smem + [v] * (len(ins) - smem),
        out_specs=jax.tree.map(lambda _: v, outs),
        scratch_shapes=scratch,
        compiler_params=pltpu.CompilerParams(vmem_limit_bytes=48 * 2**20),
    )(*ins)


def prepared(w_in, w_mid, w_out, bias, near):
    n, feat = near.shape[1], w_in.shape[2]
    tiles = n // PACK
    cols = near.reshape(3, n, tiles, PACK).transpose(2, 1, 0, 3)
    pick = np.einsum("jk,tnci->tjnkci", np.eye(4)[list(TAPS)], cols).reshape(tiles, 4 * n, 12 * PACK)
    place = np.einsum("kj,tin->tjikn", np.eye(4)[list(TAPS)], np.eye(n).reshape(tiles, PACK, n)).reshape(tiles, 4 * PACK, 4 * n)
    w1 = w_in.reshape(12, 1, 1, feat)
    eye = jnp.eye(PACK, dtype=BF16)
    rows = (w1 * eye[None, :, :, None]).reshape(12 * PACK, PACK * feat)
    w2 = w_out.T.reshape(1, feat, 4, 1)
    ends = (w2 * eye[:, None, None, :]).reshape(PACK * feat, 4 * PACK)
    return rows, jnp.asarray(pick, BF16), w_mid, ends, jnp.asarray(place, BF16), jnp.tile(bias, (1, PACK))


def exchange_kernel(sizes, x, out, slots, send, recv):
    count = math.prod(sizes)
    me = (lax.axis_index("shot") * sizes[1] + lax.axis_index("line")) * sizes[2] + lax.axis_index("tm")

    def peer(off):
        at = lax.rem(me + off, count)
        return {
            "shot": at // (sizes[1] * sizes[2]),
            "line": lax.rem(at // sizes[2], sizes[1]),
            "tm": lax.rem(at, sizes[2]),
        }

    barrier = pltpu.get_barrier_semaphore()
    for off in range(1, count):
        pl.semaphore_signal(barrier, inc=1, device_id=peer(off), device_id_type=pl.DeviceIdType.MESH)
    pl.semaphore_wait(barrier, count - 1)
    copies = []
    for off in range(1, count):
        copy = pltpu.make_async_remote_copy(
            src_ref=x,
            dst_ref=slots.at[off],
            send_sem=send.at[off],
            recv_sem=recv.at[off],
            device_id=peer(off),
            device_id_type=pl.DeviceIdType.MESH,
        )
        copy.start()
        copies.append(copy)
    total = x[...]
    for off, copy in enumerate(copies, 1):
        copy.wait()
        total += slots[off]
    out[...] = total


def summed(x, sizes):
    count, v = math.prod(sizes), pl.BlockSpec(memory_space=pltpu.VMEM)
    return pl.pallas_call(
        functools.partial(exchange_kernel, sizes),
        out_shape=jax.ShapeDtypeStruct(x.shape, x.dtype),
        in_specs=[v],
        out_specs=v,
        scratch_shapes=[
            pltpu.VMEM((count, *x.shape), x.dtype),
            pltpu.SemaphoreType.DMA((count,)),
            pltpu.SemaphoreType.DMA((count,)),
        ],
        compiler_params=pltpu.CompilerParams(collective_id=0, has_side_effects=True),
    )(x)


SLOT = (0, 3, 1, 2)
HALF = 64
GROUPS = 4


def iota(shape, dim):
    return lax.broadcasted_iota(jnp.int32, shape, dim)


def weave(w_in, w_mid, w_out, bias, we, wm, wo, bi):
    feat = w_in.shape[2]
    wide = feat * len(SLOT)
    row, lane = iota((wide, wide), 0), iota((wide, wide), 1)
    at, ch = lax.rem(row, HALF), row // HALF
    slot = lane // feat
    pos = jnp.where(slot == 1, 3, jnp.where(slot == 0, 0, slot - 1))
    taps = w_in[...].astype(F32)
    for par in range(2):
        turned = lax.rem(at + (1 if par == 0 else HALF - 1), HALF)
        tap = lax.rem(turned, 4)
        base = jnp.zeros((wide, wide), F32)
        for c in range(3):
            for t in range(4):
                line = jnp.concatenate([taps[c, t : t + 1, :]] * len(SLOT), axis=1)
                base = jnp.where((ch == c) & (tap == t), line, base)
        for g in range(GROUPS):
            we[par * GROUPS + g] = jnp.where(turned // 4 == 4 * g + pos, base, 0.0).astype(BF16)
    zero = jnp.zeros((feat, feat), F32)
    mid = [w_mid[j].astype(F32) for j in range(3)]

    def block(came, goes):
        j = came - goes + 1
        return mid[j] if 0 <= j < 3 else zero

    for n, came in enumerate(SLOT):
        blocks = [block(came, goes) for goes in SLOT]
        wm[0, n * feat : (n + 1) * feat, :] = jnp.concatenate(blocks, axis=1).astype(BF16)
    for n in range(4):
        blocks = [zero] * 4
        blocks[n ^ 1] = mid[2 if n % 2 == 0 else 0]
        wm[1, n * feat : (n + 1) * feat, :] = jnp.concatenate(blocks, axis=1).astype(BF16)

    def sample(shape):
        col = iota(shape, 1)
        m = lax.rem(col, HALF)
        edge = jnp.where(m == HALF - 1, -1, jnp.where(m == 0, HALF, -4 * HALF))
        return jnp.where(col >= 2 * HALF, edge, m)

    near, far = sample((4, wide)), sample((feat, wide))
    for par in range(2):
        pick = jnp.where(lax.rem(near - 2 * par + 1 + 8 * HALF, 4) == iota((4, wide), 0), 1.0, 0.0).astype(BF16)
        base = lax.dot_general(w_out[...], pick, (((0,), (0,)), ((), ())), preferred_element_type=F32)
        for g in range(GROUPS):
            for n, i in enumerate(SLOT):
                d = far - 4 * (4 * g + i) - 2 * par + 1
                at = ((par * GROUPS + g) * len(SLOT) + n) * feat
                wo[at : at + feat, :] = jnp.where((d >= 0) & (d < 4), base, 0.0).astype(BF16)
    bi[...] = jnp.concatenate([bias[...]] * len(SLOT), axis=1)


def rectified(h, bias):
    cubes = h.reshape(h.shape[0] // bias.shape[0], bias.shape[0], h.shape[1])
    return jnp.maximum(cubes + bias[None], 0.0).reshape(h.shape)


def enter(zs, hs, we, b0, blocks):
    per = zs.shape[1] // blocks
    for par in range(2):
        for g in range(GROUPS):
            h = jnp.dot(zs[par], we[par * GROUPS + g], preferred_element_type=F32)
            h = rectified(h, b0).astype(BF16)
            for b in range(blocks):
                at = per + (b * GROUPS + g) * per
                hs[par, at : at + per, :] = h[b * per : (b + 1) * per]


def prepare(zs, pre, we):
    for par in range(2):
        for g in range(GROUPS):
            pre[par * GROUPS + g] = jnp.dot(zs[par], we[par * GROUPS + g], preferred_element_type=F32)


def complete(pre, hs, b0, blocks):
    per = pre.shape[1] // blocks
    for b in range(blocks):
        for par in range(2):
            for g in range(GROUPS):
                at = per + (b * GROUPS + g) * per
                h = pre[par * GROUPS + g, b * per : (b + 1) * per, :]
                hs[par, at : at + per, :] = rectified(h, b0).astype(BF16)


def leave(hs, gs, ys, wm, wo, b1):
    rows, wide = gs.shape[0], hs.shape[2]
    blocks = ys.shape[0] - 2
    per, half = rows // blocks, wide // 2
    low = iota((rows, half), 1) < half // 2
    for r in range(per, per + GROUPS * rows, rows):
        edge = [jnp.where(low, hs[par, r + per : r + per + rows, :half], hs[par, r - per : r - per + rows, :half]) for par in range(2)]
        edge = jnp.dot(jnp.concatenate(edge, axis=1), wm[1], preferred_element_type=F32)
        for par in range(2):
            g = jnp.dot(hs[par, r : r + rows, :], wm[0], preferred_element_type=F32)
            ends = g[:, :half] + edge[:, par * half : (par + 1) * half]
            g = [rectified(ends, b1[:, :half]), rectified(g[:, half:], b1[:, half:])]
            for n in range(rows // per):
                b, q = divmod(r // per - 1 + n, GROUPS)
                for i in range(2):
                    col = (par * GROUPS + q) * wide + i * half
                    gs[b * per : (b + 1) * per, col : col + half] = g[i][n * per : (n + 1) * per].astype(BF16)
    part = blocks // 4
    for b in range(0, blocks, part):
        y = jnp.dot(gs[b * per : (b + part) * per, :], wo[...], preferred_element_type=F32)
        ys[1 + b : 1 + b + part] = y.reshape(part, per, wide)


def patch_kernel(sizes, *refs):
    scalars, (guess, mixtures), refs = refs[:4], refs[4:6], refs[6:]
    lags, order, tallies, pace = refs[45:49]
    given, out = refs[:8], refs[8]
    (gbuf, mbuf, sendx, recvx, sendm, recvm, backs, backr, sende, recve) = refs[9:19]
    (xs, ps, mx, rolled, mf, member, zs, hs, gs, ys) = refs[19:29]
    pre = refs[49]
    ta, tb, held = refs[29:33], refs[33:37], refs[37:45]
    load_sem, ssem, rsem = refs[50:]
    n_shot, n_line, n_tm = sizes
    count = math.prod(sizes)
    axes = [lax.axis_index(a) for a in AXES]
    turns = [[axes[i]] + [lax.rem(axes[i] + d, n) for d in range(1, n)] for i, n in enumerate(sizes)]
    at_shot, at_line, at_tm = axes

    def number(s, l, t):
        return (s * n_line + l) * n_tm + t

    def device(s, l, t):
        return {"shot": s, "line": l, "tm": t}

    me = number(*axes)
    peers = [(s, l, t) for s in turns[0] for l in turns[1] for t in turns[2]][1:]
    shots = n_shot
    n_mix = mixtures.shape[0]
    run = shots // n_mix
    recv_n, tl = guess.shape[1:]
    lc = recv_n // count
    tile = 2 * HALF
    blocks = tl * n_tm // HALF
    each = tl // HALF
    back_kind = 2 + ITERS * n_line

    barrier = pltpu.get_barrier_semaphore()
    for p in peers:
        pl.semaphore_signal(barrier, inc=1, device_id=device(*p), device_id_type=pl.DeviceIdType.MESH)
    pairs = [(guess.at[0], gbuf), (mixtures, mbuf)] + list(zip(given, held)) + list(zip(scalars, refs[45:49]))
    loads = [pltpu.make_async_copy(a, b, load_sem.at[i]) for i, (a, b) in enumerate(pairs)]
    for copy in loads:
        copy.start()

    def link(which, src, dst, to, came):
        return pltpu.make_async_remote_copy(
            src_ref=src,
            dst_ref=dst,
            send_sem=ssem.at[which, number(*to)],
            recv_sem=rsem.at[which, came],
            device_id=device(*to),
            device_id_type=pl.DeviceIdType.MESH,
        )

    row, col = iota((recv_n, recv_n), 0), iota((recv_n, recv_n), 1)
    perm = jnp.where(col == lax.rem(row, lc) * count + row // lc, 1.0, 0.0).astype(BF16)
    loads[0].wait()
    v = jnp.dot(perm, gbuf[...], preferred_element_type=F32)
    for k in range(count):
        part = v[k * lc : (k + 1) * lc]
        sendx[k] = jnp.concatenate([part[:, : tl // 2], part[:, tl // 2 :]], axis=0).astype(BF16)
    pl.semaphore_wait(barrier, count - 1)
    for p in peers:
        link(0, sendx.at[number(*p)], recvx.at[me], p, me).start()

    loads[1].wait()
    other = (at_shot, n_line - 1 - at_line, at_tm)
    row, col = iota((2 * lc, recv_n), 0), iota((2 * lc, recv_n), 1)
    wanted = jnp.where(row < lc, me, number(*other))
    pick = jnp.where(col == lax.rem(row, lc) * count + wanted, 1.0, 0.0).astype(BF16)
    picked = [jnp.dot(pick, mbuf[g], preferred_element_type=F32) for g in range(n_mix)]
    sendm[...] = jnp.concatenate([p[lc:] for p in picked], axis=0).astype(BF16)
    link(1, sendm, recvm.at[at_line], other, me).start()
    recvm[at_line] = jnp.concatenate([p[:lc] for p in picked], axis=0).astype(BF16)
    recvx[me] = sendx[me]

    for copy in loads[2:]:
        copy.wait()
    weave(*held[:4], *ta)
    weave(*held[4:], *tb)
    edges = hs.shape[1] - (GROUPS * blocks + 1) * (hs.shape[1] // (GROUPS * blocks + 2))
    hs[:, :edges] = jnp.zeros_like(hs[:, :edges])
    hs[:, hs.shape[1] - edges :] = jnp.zeros_like(hs[:, :edges])
    for ref in (ys, rolled, mf, xs):
        ref[0] = jnp.zeros_like(ref[0])
        ref[ref.shape[0] - 1] = jnp.zeros_like(ref[0])
    for ref, at in ((rolled, 1), (mf, blocks)):
        ref[at] = jnp.zeros_like(ref[at])
    sec = []
    for rows in ((lc, tile), (count, tile)):
        if rows[0] == lc:
            q = iota(rows, 0) * count + me
        else:
            q = lax.rem(iota(rows, 1), lc) * count + iota(rows, 0)
        edge, at, size = jnp.int32(0), jnp.zeros(rows, jnp.int32), jnp.zeros(rows, jnp.int32)
        for p in range(tallies.shape[0]):
            at = jnp.where(q >= edge, p, at)
            size = jnp.where(q >= edge, tallies[p], size)
            edge = edge + tallies[p]
        sec.append((at, size))
    scale = 1.0 / (sec[0][1] * (shots * tl * n_tm)).astype(F32)
    for k in range(count):
        member[k] = jnp.where(sec[0][0] == sec[1][0][k : k + 1, :], scale, 0.0)

    lane = iota((lc, tile), 1)
    low = lane < HALF
    inner = lax.rem(lane, HALF)

    def unfold(v):
        turned = pltpu.roll(v, HALF, 1)
        return jnp.where(low, v, turned), jnp.where(low, turned, v)

    for p in peers:
        link(0, sendx.at[number(*p)], recvx.at[number(*p)], p, number(*p)).wait_recv()
    for p in range(count):
        s, l, t = p // (n_line * n_tm), p // n_tm % n_line, p % n_tm
        v = recvx[p].astype(F32)
        for j in range(tl // tile):
            h, c = divmod(j * tile, tl // 2)
            two = unfold(v[h * lc : (h + 1) * lc, c : c + tile])
            for n in range(2):
                xs[1 + l, t * each + 2 * j + n, s] = two[n]

    def unfold_mixtures():
        link(1, sendm, recvm.at[n_line - 1 - at_line], other, number(*other)).wait_recv()
        for l in range(n_line):
            v = recvm[l].astype(F32)
            for g in range(n_mix):
                for j in range(blocks // 2):
                    two = unfold(v[g * lc : (g + 1) * lc, j * tile : (j + 1) * tile])
                    for n in range(2):
                        mx[2 * j + n, g * n_line + l] = two[n]

    cube = (shots, lc, tile)
    per = shots * lc
    clow = iota(cube, 2) < HALF
    line_of = iota(cube, 1)
    spot = lax.rem(iota((per, tile), 1), HALF)
    wide_spot = lax.rem(iota((per, 2 * tile), 1), HALF)
    early = spot < HALF // 2
    one = jnp.zeros((1, lc, tile), F32)
    nothing = jnp.zeros((per, 2 * tile), F32)

    def widen(make):
        ahead_of = [nothing, make(0)]
        for b in range(blocks):
            ahead_of.append(make(b + 1) if b + 1 < blocks else nothing)
            before, here, after = ahead_of[b : b + 3]
            zs[0, b * per : (b + 1) * per, :] = jnp.where(wide_spot == HALF - 1, before, here).astype(BF16)
            zs[1, b * per : (b + 1) * per, :] = jnp.where(wide_spot == 0, after, here).astype(BF16)

    def beside(before, here, after):
        both = jnp.where(clow, before, here)
        return jnp.concatenate([both.reshape(per, tile), after.reshape(per, tile)], axis=1)

    def change(b):
        return ys[b + 1, :, :tile] + jnp.where(early, ys[b, :, tile:], ys[b + 2, :, tile:])

    group = []
    for s in range(shots):
        found = jnp.int32(0)
        for k in range(shots):
            found = jnp.where(order[k] == s, k // run, found)
        group.append(found)
    rest = [lax.rem(lags[s], HALF) for s in range(shots)]
    far = [lags[s] // HALF for s in range(shots)]

    def over_lines(it, l):
        def make(b):
            x = xs[1 + l, b]
            before = jnp.where(line_of == lc - 1, xs[l, b], x)
            after = jnp.where(line_of == 0, xs[2 + l, b], x)
            return beside(pltpu.roll(before, 1, 1), x, pltpu.roll(after, lc - 1, 1))

        widen(make)
        biases = [jnp.broadcast_to(ta[3][i : i + 1, :], (lc, 2 * tile)) for i in range(2)]
        enter(zs, hs, ta[0], biases[0], blocks)
        leave(hs, gs, ys, *ta[1:3], biases[1])
        energy = jnp.zeros((lc, tile), F32)
        for b in range(blocks):
            x = (xs[1 + l, b] + change(b).reshape(cube)).astype(BF16).astype(F32)
            ps[l, b] = x
            energy = energy + jnp.sum(x * x, axis=0)
        energy = 0.5 * jnp.sum(energy, axis=1, keepdims=True)
        mine = jnp.sum(jnp.where(lane == iota((lc, tile), 0), energy, 0.0), axis=0, keepdims=True)
        at = it * n_line + l
        sende[at] = mine
        recve[at, me] = mine
        for p in peers:
            link(2 + at, sende.at[at], recve.at[at, me], p, me).start()

    def before_shots(l):
        def make(b):
            x = ps[l, b]
            return beside(jnp.concatenate([one, x[: shots - 1]], axis=0), x, jnp.concatenate([x[1:], one], axis=0))

        widen(make)
        prepare(zs, pre.at[l], tb[0])

    def over_shots(it, l):
        at = it * n_line + l
        for p in peers:
            link(2 + at, sende.at[at], recve.at[at, number(*p)], p, number(*p)).wait_recv()
        total = jnp.zeros((lc, tile), F32)
        for k in range(count):
            total = total + member[k] * recve[at, k]
        mean = jnp.sum(total, axis=1, keepdims=True)
        rms = jnp.broadcast_to(jnp.sqrt(mean + EPSILON), (lc, 2 * tile))
        biases = [rms * tb[3][i : i + 1, :] for i in range(2)]
        complete(pre.at[l], hs, biases[0], blocks)
        leave(hs, gs, ys, *tb[1:3], biases[1])
        for b in range(blocks):
            x = (ps[l, b] + change(b).reshape(cube)).astype(BF16).astype(F32)
            ps[l, b] = x
            for s in range(shots):
                rolled[b + 2, s] = pltpu.roll(x[s], rest[s], 1)
        for g in range(n_mix):
            acc = -mx[:, g * n_line + l]
            for i in range(run):
                s = order[g * run + i]
                lag = lags[s]
                a = 2 - lag // HALF
                near, late = rolled[pl.ds(a, blocks), s], rolled[pl.ds(a - 1, blocks), s]
                acc = acc + jnp.where((inner >= lax.rem(lag, HALF))[None], near, late)
            mf[:blocks, g] = acc
        for s in range(shots):
            m = mf[:, group[s]]
            rolled[: blocks + 2, s] = pltpu.roll(m, lax.rem(tile - rest[s], tile), 2)
        for s in range(shots):
            near, late = rolled[pl.ds(far[s], blocks), s], rolled[pl.ds(far[s] + 1, blocks), s]
            back = jnp.where((inner < HALF - rest[s])[None], near, late)
            xs[1 + l, :, s] = (ps[l, :, s] - pace[it] * back).astype(BF16).astype(F32)
        rolled[:2] = jnp.zeros_like(rolled[:2])

        @pl.when(it == ITERS - 1)
        def _():
            for s in range(n_shot):
                for t in range(n_tm):
                    tiles = []
                    for j in range(tl // tile):
                        b = t * each + 2 * j
                        tiles.append(jnp.where(low, xs[1 + l, b, s], xs[1 + l, b + 1, s]))
                    n = len(tiles) // 2
                    halves = [jnp.concatenate(tiles[:n], axis=1), jnp.concatenate(tiles[n:], axis=1)]
                    backs[number(s, l, t)] = jnp.concatenate(halves, axis=0).astype(BF16)
            own = (at_shot, l, at_tm)
            for s in turns[0]:
                for t in turns[2]:
                    if s is at_shot and t is at_tm:
                        continue
                    link(back_kind, backs.at[number(s, l, t)], backr.at[me], (s, l, t), me).start()

            @pl.when(l != at_line)
            def _():
                link(back_kind, backs.at[number(*own)], backr.at[me], own, me).start()

    def iterate(it, carry):
        def lines(l, carry):
            over_lines(it, l)
            return carry

        def stations(l, carry):
            over_shots(it, l)
            return carry

        def first(l, carry):
            before_shots(l)
            return carry

        lax.fori_loop(0, n_line, lines, 0)
        lax.fori_loop(0, n_line, first, 0)

        @pl.when(it == 0)
        def _():
            unfold_mixtures()

        lax.fori_loop(0, n_line, stations, 0)
        return carry

    lax.fori_loop(0, ITERS, iterate, 0)

    backr[me] = backs[me]
    row, col = iota((recv_n, recv_n), 0), iota((recv_n, recv_n), 1)
    perm = jnp.where(row == lax.rem(col, lc) * count + col // lc, 1.0, 0.0).astype(BF16)
    for p in peers:
        link(back_kind, backs.at[number(*p)], backr.at[number(*p)], p, number(*p)).wait_recv()
    v = []
    for k in range(count):
        part = backr[k].astype(F32)
        v.append(jnp.concatenate([part[:lc], part[lc:]], axis=1))
    v = jnp.concatenate(v, axis=0).astype(BF16)
    out[0] = jnp.dot(perm, v, preferred_element_type=F32).astype(BF16)
    link(1, sendm, recvm.at[at_line], other, me).wait_send()
    for p in peers:
        link(0, sendx.at[number(*p)], recvx.at[me], p, me).wait_send()
        for at in range(ITERS * n_line):
            link(2 + at, sende.at[at], recve.at[at, me], p, me).wait_send()
        link(back_kind, backs.at[number(*p)], backr.at[me], p, me).wait_send()


def patch(guess, mixtures, lags, order, tallies, wa, wb, pace, sizes):
    count = math.prod(sizes)
    n_shot, n_line, n_tm = sizes
    recv, tl = guess.shape[1:]
    n_mix, nt = mixtures.shape[0], mixtures.shape[2]
    lc, tile = recv // count, 2 * HALF
    blocks = nt // HALF
    per, feat = n_shot * lc, wa[0].shape[2]
    wide = feat * len(SLOT)
    rows = blocks * per
    weights = [w.transpose(1, 0, 2) if i == 0 else w for part in (wa, wb) for i, w in enumerate(part)]
    v, h = (pl.BlockSpec(memory_space=m) for m in (pltpu.VMEM, pl.ANY))
    slab = pltpu.VMEM((count, 2 * lc, tl // 2), BF16)
    woven = [
        pltpu.VMEM((2 * GROUPS, wide, wide), BF16),
        pltpu.VMEM((2, wide, wide), BF16),
        pltpu.VMEM((2 * GROUPS * wide, wide), BF16),
        pltpu.VMEM((2, wide), F32),
    ]
    kinds = 3 + ITERS * n_line
    return pl.pallas_call(
        functools.partial(patch_kernel, sizes),
        out_shape=pltpu.VMEM(guess.shape, BF16),
        in_specs=[h] * 14,
        out_specs=v,
        scratch_shapes=[
            pltpu.VMEM((recv, tl), BF16),
            pltpu.VMEM(mixtures.shape, BF16),
            slab,
            slab,
            pltpu.VMEM((n_mix * lc, nt), BF16),
            pltpu.VMEM((n_line, n_mix * lc, nt), BF16),
            slab,
            slab,
            pltpu.VMEM((ITERS * n_line, 1, tile), F32),
            pltpu.VMEM((ITERS * n_line, count, 1, tile), F32),
            pltpu.VMEM((n_line + 2, blocks, n_shot, lc, tile), F32),
            pltpu.VMEM((n_line, blocks, n_shot, lc, tile), F32),
            pltpu.VMEM((blocks, n_mix * n_line, lc, tile), F32),
            pltpu.VMEM((blocks + 2, n_shot, lc, tile), F32),
            pltpu.VMEM((blocks + 2, n_mix, lc, tile), F32),
            pltpu.VMEM((count, lc, tile), F32),
            pltpu.VMEM((2, rows, wide), BF16),
            pltpu.VMEM((2, GROUPS * rows + 2 * per, wide), BF16),
            pltpu.VMEM((rows, 2 * GROUPS * wide), BF16),
            pltpu.VMEM((blocks + 2, per, wide), F32),
            *woven,
            *woven,
            *[pltpu.VMEM(w.shape, w.dtype) for w in weights],
            *[pltpu.SMEM(w.shape, w.dtype) for w in (lags, order, tallies, pace)],
            pltpu.VMEM((n_line, 2 * GROUPS, rows, wide), F32),
            pltpu.SemaphoreType.DMA((6 + len(weights),)),
            pltpu.SemaphoreType.DMA((kinds, count)),
            pltpu.SemaphoreType.DMA((kinds, count)),
        ],
        compiler_params=pltpu.CompilerParams(vmem_limit_bytes=56 * 2**20, collective_id=1, has_side_effects=True),
    )(lags, order, tallies, pace, guess, mixtures, *weights)


def per_device(guess, mixtures, lags, order, tallies, e1, m1, x1, b1, e2, m2, x2, b2, pace):
    sh, recv, tl = guess.shape
    n_shot, n_line, n_tm = (lax.axis_size(a) for a in AXES)
    whole = RPL % (n_shot * n_line * n_tm) == 0
    where = AXES if whole else AXES[1:]
    parts = math.prod(lax.axis_size(a) for a in where)
    kp, lh = RPL // parts, recv // RPL
    lines, shots, nt = lh * n_line, sh * n_shot, tl * n_tm
    planes, s1 = nt // 2 // C, shots if whole else sh
    r1 = lines * kp
    r2 = r1 if whole else r1 // n_shot
    lanes1, lanes2 = 2 * s1 * r1, 2 * shots * r2
    sources = n_shot if whole else 1
    i32 = functools.partial(jnp.arange, dtype=jnp.int32)
    n_mix, feat = mixtures.shape[0], e1.shape[2]
    square = sh == 1 and kp == 1 and n_line == 2 and shots % n_mix == 0 and feat == HALF
    square = square and lh == C and tl % (4 * HALF) == 0 and n_mix * lh % 16 == 0
    square = square and lines == parts and 2 * (n_mix // n_line) == n_line
    if square:
        sizes = (n_shot, n_line, n_tm)
        return patch(guess, mixtures, lags, order, tallies, (e1, m1, x1, b1), (e2, m2, x2, b2), pace, sizes)

    at_shot = lax.axis_index("shot")
    n_mix, run = mixtures.shape[0], nt // C
    fused = whole and sh == 1 and kp == 1 and C % n_tm == 0 and n_shot * n_tm == C
    x = guess.reshape(sh, lh, parts, kp, tl).transpose(2, 0, 1, 3, 4)
    if fused:
        share = (at_shot * n_tm + lax.axis_index("tm")) * run
        mine = lax.dynamic_slice_in_dim(mixtures, share, run, axis=2).reshape(n_mix, lh, parts, run)
        mine = mine.transpose(2, 1, 0, 3).reshape(parts, lh, n_mix * run)
        x = jnp.concatenate([x.reshape(parts, lh, tl), mine], axis=2)
    x = lax.all_to_all(x, where, split_axis=0, concat_axis=0, tiled=False)
    if not fused:
        x = x.reshape(sources, n_line, n_tm, sh, lh, kp, tl).transpose(0, 3, 1, 4, 5, 2, 6)
        x = x.reshape(s1, r1, C, planes, 2).transpose(3, 2, 4, 0, 1).reshape(planes, C, lanes1)


    def first_k(line):
        block = line * n_tm + lax.axis_index("tm")
        return (at_shot * n_line * n_tm + block if whole else block) * kp

    if not fused:
        grid = mixtures.reshape(n_mix, lh, RPL, nt)
        sent = jnp.stack([lax.dynamic_slice_in_dim(grid, first_k(d), kp, axis=2) for d in range(n_line)])
        m = lax.all_to_all(sent, "line", split_axis=0, concat_axis=0)
        m = m.transpose(1, 0, 2, 3, 4).reshape(n_mix, r1, nt)
        if not whole:
            m = lax.dynamic_slice_in_dim(m, at_shot * r2, r2, axis=1)
        m = m.reshape(n_mix, r2, C, planes, 2).transpose(3, 2, 4, 0, 1).reshape(planes * C, 2 * n_mix * r2)

    np_ = tallies.shape[0]
    here = i32(np_)
    offsets = jnp.sum(jnp.where(here[None, :] < here[:, None], tallies[None, :], 0), axis=1)
    mine = first_k(lax.axis_index("line"))

    def one_hot(r):
        line, k = r // kp, mine + lax.rem(r, kp)
        q = lax.rem(line, lh) * RPL + k
        inside = (offsets[:, None] <= q[None, :]) & (q[None, :] < (offsets + tallies)[:, None])
        block = (line // lh)[None, :] == i32(n_line)[:, None]
        return (block[:, None, :] & inside[None, :, :]).reshape(n_line * np_, r.shape[0]).astype(F32)

    member = jnp.tile(one_hot(i32(r1)), (1, 2 * s1))
    r_own = i32(r2) if whole else at_shot * r2 + i32(r2)
    count = jnp.tile((tallies * (shots * nt)).astype(F32), n_line)
    spread = jnp.tile(one_hot(r_own) / count[:, None], (1, 2 * shots))

    sid = i32(shots)
    place = jnp.sum(jnp.where(order[None, :] == sid[:, None], sid[None, :], 0), axis=1)
    group = place // (shots // n_mix)
    same = (group[:, None] == group[None, :]).astype(BF16)
    chosen = (i32(n_mix)[:, None] == group[None, :]).astype(BF16)
    rest, two = jnp.eye(r2, dtype=BF16), jnp.eye(2, dtype=BF16)
    join = jnp.kron(two, jnp.kron(same, rest))
    take = jnp.kron(two, jnp.kron(chosen, rest))

    n1, n2 = s1 * r1, shots * r2
    a, b = np.arange(n1)[:, None], np.arange(n1)[None, :]
    near1 = np.stack([(a == b + (c - 1) * kp) & (a // r1 == b // r1) for c in range(3)])
    a, b = np.arange(n2)[:, None], np.arange(n2)[None, :]
    near2 = np.stack([a == b + (c - 1) * r2 for c in range(3)])
    wa = prepared(e1, m1, x1, b1, near1)
    wb = prepared(e2, m2, x2, b2, near2)

    rows = planes * C
    tot1, tot2 = pltpu.VMEM((rows, 2 * lanes1), F32), pltpu.VMEM((rows, 2 * lanes2), F32)
    feat = e1.shape[2]
    band = pltpu.VMEM((3 * PACK * feat, PACK * feat), BF16)
    buf = pltpu.VMEM((2, 2 * planes, C, lanes2), F32)
    spass = jax.ShapeDtypeStruct((planes, C, lanes1), BF16)
    part = jax.ShapeDtypeStruct((n_line * np_, 128), F32)
    moved = jax.ShapeDtypeStruct((planes, C, lanes2), BF16)

    def to_stations(y):
        y = y.reshape(rows, 2, sh, n_shot, r2)
        y = lax.all_to_all(y, "shot", split_axis=3, concat_axis=2, tiled=True)
        return y.reshape(planes, C, lanes2)

    def to_shots(y):
        y = y.reshape(rows, 2, shots, 1, r2)
        y = lax.all_to_all(y, "shot", split_axis=2, concat_axis=3, tiled=True)
        return y.reshape(planes, C, lanes1)

    dims = (n_shot, n_line, n_tm)
    cube = pltpu.VMEM((planes, C, lanes1), F32)
    if fused:
        mixed = jax.ShapeDtypeStruct((rows, 2 * n_mix * r2), BF16)
        side = pltpu.VMEM((planes, C, 2 * n_mix * r2), F32)
        sp, energy, m = call(
            functools.partial(entry_kernel, dims),
            (spass, part, mixed),
            (x, *wa, member),
            0,
            [tot1, band, cube, side],
        )
    else:
        sp, energy = call(first_kernel, (spass, part), (x, *wa, member), 0, [tot1, band])
    for it in range(ITERS):
        tot = summed(energy, (n_shot, n_line, n_tm)) if whole else lax.psum(energy, AXES)
        if not whole:
            sp = to_stations(sp)
        ins = (lags, pace, sp, tot, spread, *wb, join, m, take)
        if whole and it < ITERS - 1:
            sp, energy = call(
                functools.partial(both_kernel, it, shots), (spass, part), (*ins, *wa, member), 2, [buf, tot2, band]
            )
            continue
        if fused:
            back = jax.ShapeDtypeStruct((parts, lh, tl), BF16)
            x = call(functools.partial(exit_kernel, it, dims), back, ins, 2, [buf, tot2, band, cube])
            continue
        x = call(functools.partial(station_kernel, it, shots), moved, ins, 2, [buf, tot2, band])
        if not whole:
            x = to_shots(x)
            if it < ITERS - 1:
                sp, energy = call(first_kernel, (spass, part), (x, *wa, member), 0, [tot1, band])

    if not fused:
        x = x.reshape(planes, C, 2, s1, r1).transpose(3, 4, 1, 0, 2)
        x = x.reshape(sources, sh, n_line, lh, kp, n_tm, tl).transpose(0, 2, 5, 1, 3, 4, 6)
    x = lax.all_to_all(x.reshape(parts, sh, lh, kp, tl), where, split_axis=0, concat_axis=0)
    return x.transpose(1, 2, 0, 3, 4).reshape(sh, recv, tl)


def solution(mesh):
    spec = P(("group", "shot"), "line", "tm")
    placed = (spec, P("group", "line", None), P("group"), P("group"), P("group")) + (P(),) * 9
    return jax.shard_map(per_device, mesh=mesh, in_specs=placed, out_specs=spec, check_vma=False)
```

```python
import functools
import math

import jax
import jax.numpy as jnp
import numpy as np
from jax import lax
from jax.experimental import pallas as pl
from jax.experimental.pallas import tpu as pltpu
from jax.sharding import PartitionSpec as P

RPL = 16
ITERS = 2
EPSILON = 1e-05
C = 8
PACK = 4
TAPS = (1, 2, 3, 0)
F32, BF16 = jnp.float32, jnp.bfloat16
AXES = ("shot", "line", "tm")


def ahead(x, k):
    edge = pltpu.roll(x[:k], C - 1, 1)
    edge = jnp.where(lax.broadcasted_iota(jnp.int32, edge.shape, 1) == C - 1, 0.0, edge)
    return edge if k == x.shape[0] else jnp.concatenate([x[k:], edge], axis=0)


def behind(x, k):
    edge = pltpu.roll(x[x.shape[0] - k :], 1, 1)
    edge = jnp.where(lax.broadcasted_iota(jnp.int32, edge.shape, 1) == 0, 0.0, edge)
    return edge if k == x.shape[0] else jnp.concatenate([edge, x[: x.shape[0] - k]], axis=0)


def even_lanes(shape):
    return lax.broadcasted_iota(jnp.int32, shape, len(shape) - 1) < shape[-1] // 2


def net(x, w_in, pick, w_mid, w_out, place, bias, total, band):
    planes, _, lanes = x.shape
    rows = planes * C
    side = jnp.where(even_lanes(x.shape), ahead(x, 1), behind(x, 1))
    z = jnp.concatenate([x, side], axis=2).astype(BF16).reshape(rows, 2 * lanes)
    total[...] = jnp.zeros_like(total)
    wide = w_in.shape[1]
    feat = wide // PACK
    for j in range(3):
        tap = w_mid[j].astype(F32)
        for i in range(PACK):
            row = [tap if p == i else jnp.zeros_like(tap) for p in range(PACK)]
            at = (j * PACK + i) * feat
            band[at : at + feat, :] = jnp.concatenate(row, axis=1).astype(BF16)

    def step(q, carry):
        w_here = jnp.dot(pick[q], w_in[...], preferred_element_type=F32).astype(BF16)
        o_here = jnp.dot(w_out[...], place[q], preferred_element_type=F32).astype(BF16)
        h = jnp.dot(z, w_here, preferred_element_type=F32)
        h = jnp.maximum(h + bias[0:1, :], 0.0)
        cube = h.reshape(planes, C, wide)
        first = ahead(cube[:2], 2).reshape(2 * C, wide).astype(BF16)
        last = behind(cube[planes - 2 :], 2).reshape(2 * C, wide).astype(BF16)
        hb = h.astype(BF16)
        early = jnp.concatenate([last, hb[: rows - 2 * C]], axis=0)
        late = jnp.concatenate([hb[2 * C :], first], axis=0)
        g = jnp.dot(jnp.concatenate([early, hb, late], axis=1), band[...], preferred_element_type=F32)
        g = jnp.maximum(g + bias[1:2, :], 0.0).astype(BF16)
        total[...] += jnp.dot(g, o_here, preferred_element_type=F32)
        return carry

    lax.fori_loop(0, pick.shape[0], step, 0, unroll=2)
    y = total[...].reshape(planes, C, 2 * lanes)
    a, b = y[:, :, :lanes], y[:, :, lanes:]
    return a + jnp.where(even_lanes(b.shape), behind(b, 1), ahead(b, 1))


def shot_step(x, weights, member, out_ref, part_ref, total, band):
    y = (x + net(x, *weights, total, band)).astype(BF16)
    out_ref[...] = y
    y = y.astype(F32)
    energy = jnp.sum(jnp.sum(y * y, axis=0), axis=0, keepdims=True)
    sums = jnp.sum(member[...] * energy, axis=1, keepdims=True)
    part_ref[...] = jnp.broadcast_to(sums, part_ref.shape)


def shifted(buf, lag_ref, shots, forward):
    planes, lanes = buf.shape[1] // 2, buf.shape[3]
    shape = (planes, C, lanes)
    even = even_lanes(shape)
    per = lanes // 2 // shots
    lane_shot = lax.rem(lax.broadcasted_iota(jnp.int32, shape, 2), lanes // 2) // per
    out = jnp.zeros(shape, F32)
    for s in range(shots):
        lag = lag_ref[s]
        half, odd = lag // 2, lax.rem(lag, 2)
        at_even = half if forward else planes - half - odd
        at_odd = half + odd if forward else planes - half
        one = jnp.where(even, buf[odd, pl.ds(at_even, planes)], buf[odd, pl.ds(at_odd, planes)])
        out = jnp.where(lane_shot == s, one, out)
    return out


def station_step(shots, sp, tot_ref, spread, weights, lags, join, mix, take, pace, buf, total, band):
    planes, _, lanes = sp.shape
    rows = planes * C
    mean = jnp.sum(tot_ref[:, 0:1] * spread[...], axis=0, keepdims=True)
    rms = jnp.sqrt(mean + EPSILON).reshape(1, 1, lanes)
    normed = (sp / rms).astype(BF16).astype(F32)
    settled = (sp + rms * net(normed, *weights, total, band)).astype(BF16).astype(F32)

    def fill(x, forward):
        far = ahead(x, planes) if forward else behind(x, planes)
        near_at, far_at = (0, planes) if forward else (planes, 0)
        for v, at in ((x, near_at), (far, far_at)):
            buf[0, at : at + planes] = v
            h = lanes // 2
            buf[1, at : at + planes] = jnp.concatenate([v[:, :, h:], v[:, :, :h]], axis=2)

    fill(settled, False)
    fired = shifted(buf, lags, shots, False).astype(BF16).reshape(rows, lanes)
    misfit = jnp.dot(fired, join[...], preferred_element_type=F32)
    misfit -= jnp.dot(mix[...], take[...], preferred_element_type=F32)
    fill(misfit.reshape(planes, C, lanes), True)
    return (settled - pace * shifted(buf, lags, shots, True)).astype(BF16)


def by_phase(width):
    row = lax.broadcasted_iota(jnp.int32, (width, width), 0)
    col = lax.broadcasted_iota(jnp.int32, (width, width), 1)
    half = width // 2
    return jnp.where(col == 2 * lax.rem(row, half) + row // half, 1.0, 0.0).astype(BF16)


def unfold(read, into, sort):
    planes = into.shape[0]
    for c in range(C):
        v = lax.dot_general(sort, read(c), (((1,), (1,)), ((), ())), preferred_element_type=F32)
        into[:, c, :] = jnp.concatenate([v[:planes], v[planes:]], axis=1)


def entry_kernel(
    dims, x, wi, wp, wm, wo, wq, bi, member, out, part, mix, total, band, cube, side
):
    shots, blocks, halves = dims
    width = 2 * cube.shape[0]
    sort, each = by_phase(width), C // halves

    def traces(c):
        at, t = slice(c % each * width, (c % each + 1) * width), c // each
        rows = [x[(s * blocks + b) * halves + t, :, at].astype(F32) for s in range(shots) for b in range(blocks)]
        return jnp.concatenate(rows, axis=0).astype(BF16)

    tl = each * width

    def records(c):
        s, t = c // halves, c % halves
        rows = [
            x[(s * blocks + b) * halves + t, :, tl + g * width : tl + (g + 1) * width].astype(F32)
            for g in range((x.shape[2] - tl) // width)
            for b in range(blocks)
        ]
        return jnp.concatenate(rows, axis=0).astype(BF16)

    unfold(records, side, sort)
    mix[...] = side[...].astype(BF16).reshape(mix.shape)
    unfold(traces, cube, sort)
    shot_step(cube[...], (wi, wp, wm, wo, wq, bi), member, out, part, total, band)


def exit_kernel(
    it, dims, lags, pace, sp, tot, spread, wi, wp, wm, wo, wq, bi, join, mix, take, out, buf, total, band, cube
):
    shots, blocks, halves = dims
    width = 2 * cube.shape[0]
    sort, each = by_phase(width), C // halves
    x = station_step(
        shots, sp[...].astype(F32), tot, spread, (wi, wp, wm, wo, wq, bi), lags, join, mix, take, pace[it], buf, total, band
    )
    cube[...] = x.astype(F32)
    n, lh = cube.shape[2] // 2, out.shape[1]
    for c in range(C):
        v = cube[:, c, :]
        v = jnp.concatenate([v[:, :n], v[:, n:]], axis=0).T.astype(BF16)
        v = jnp.dot(v, sort, preferred_element_type=F32)
        at, t = slice(c % each * width, (c % each + 1) * width), c // each
        for j in range(shots * blocks):
            out[j * halves + t, :, at] = v[j * lh : (j + 1) * lh].astype(BF16)


def first_kernel(x, wi, wp, wm, wo, wq, bi, member, out, part, total, band):
    shot_step(x[...].astype(F32), (wi, wp, wm, wo, wq, bi), member, out, part, total, band)


def station_kernel(it, shots, lags, pace, sp, tot, spread, wi, wp, wm, wo, wq, bi, join, mix, take, out, buf, total, band):
    out[...] = station_step(
        shots, sp[...].astype(F32), tot, spread, (wi, wp, wm, wo, wq, bi), lags, join, mix, take, pace[it], buf, total, band
    )


def both_kernel(
    it, shots, lags, pace, sp, tot, spread, wi, wp, wm, wo, wq, bi, join, mix, take, vi, vp, vm, vo, vq, ci, member, out, part, buf, total, band
):
    x = station_step(
        shots, sp[...].astype(F32), tot, spread, (wi, wp, wm, wo, wq, bi), lags, join, mix, take, pace[it], buf, total, band
    )
    shot_step(x.astype(F32), (vi, vp, vm, vo, vq, ci), member, out, part, total, band)


def call(body, outs, ins, smem, scratch):
    v, s = pl.BlockSpec(memory_space=pltpu.VMEM), pl.BlockSpec(memory_space=pltpu.SMEM)
    return pl.pallas_call(
        body,
        out_shape=outs,
        in_specs=[s] * smem + [v] * (len(ins) - smem),
        out_specs=jax.tree.map(lambda _: v, outs),
        scratch_shapes=scratch,
        compiler_params=pltpu.CompilerParams(vmem_limit_bytes=48 * 2**20),
    )(*ins)


def prepared(w_in, w_mid, w_out, bias, near):
    n, feat = near.shape[1], w_in.shape[2]
    tiles = n // PACK
    cols = near.reshape(3, n, tiles, PACK).transpose(2, 1, 0, 3)
    pick = np.einsum("jk,tnci->tjnkci", np.eye(4)[list(TAPS)], cols).reshape(tiles, 4 * n, 12 * PACK)
    place = np.einsum("kj,tin->tjikn", np.eye(4)[list(TAPS)], np.eye(n).reshape(tiles, PACK, n)).reshape(tiles, 4 * PACK, 4 * n)
    w1 = w_in.reshape(12, 1, 1, feat)
    eye = jnp.eye(PACK, dtype=BF16)
    rows = (w1 * eye[None, :, :, None]).reshape(12 * PACK, PACK * feat)
    w2 = w_out.T.reshape(1, feat, 4, 1)
    ends = (w2 * eye[:, None, None, :]).reshape(PACK * feat, 4 * PACK)
    return rows, jnp.asarray(pick, BF16), w_mid, ends, jnp.asarray(place, BF16), jnp.tile(bias, (1, PACK))


def exchange_kernel(sizes, x, out, slots, send, recv):
    count = math.prod(sizes)
    me = (lax.axis_index("shot") * sizes[1] + lax.axis_index("line")) * sizes[2] + lax.axis_index("tm")

    def peer(off):
        at = lax.rem(me + off, count)
        return {
            "shot": at // (sizes[1] * sizes[2]),
            "line": lax.rem(at // sizes[2], sizes[1]),
            "tm": lax.rem(at, sizes[2]),
        }

    barrier = pltpu.get_barrier_semaphore()
    for off in range(1, count):
        pl.semaphore_signal(barrier, inc=1, device_id=peer(off), device_id_type=pl.DeviceIdType.MESH)
    pl.semaphore_wait(barrier, count - 1)
    copies = []
    for off in range(1, count):
        copy = pltpu.make_async_remote_copy(
            src_ref=x,
            dst_ref=slots.at[off],
            send_sem=send.at[off],
            recv_sem=recv.at[off],
            device_id=peer(off),
            device_id_type=pl.DeviceIdType.MESH,
        )
        copy.start()
        copies.append(copy)
    total = x[...]
    for off, copy in enumerate(copies, 1):
        copy.wait()
        total += slots[off]
    out[...] = total


def summed(x, sizes):
    count, v = math.prod(sizes), pl.BlockSpec(memory_space=pltpu.VMEM)
    return pl.pallas_call(
        functools.partial(exchange_kernel, sizes),
        out_shape=jax.ShapeDtypeStruct(x.shape, x.dtype),
        in_specs=[v],
        out_specs=v,
        scratch_shapes=[
            pltpu.VMEM((count, *x.shape), x.dtype),
            pltpu.SemaphoreType.DMA((count,)),
            pltpu.SemaphoreType.DMA((count,)),
        ],
        compiler_params=pltpu.CompilerParams(collective_id=0, has_side_effects=True),
    )(x)


SLOT = (0, 3, 1, 2)
HALF = 64
GROUPS = 4


def iota(shape, dim):
    return lax.broadcasted_iota(jnp.int32, shape, dim)


def weave(w_in, w_mid, w_out, bias, we, wm, wo, bi):
    feat = w_in.shape[2]
    wide = feat * len(SLOT)
    row, lane = iota((wide, wide), 0), iota((wide, wide), 1)
    at, ch = lax.rem(row, HALF), row // HALF
    slot = lane // feat
    pos = jnp.where(slot == 1, 3, jnp.where(slot == 0, 0, slot - 1))
    taps = w_in[...].astype(F32)
    for par in range(2):
        turned = lax.rem(at + (1 if par == 0 else HALF - 1), HALF)
        tap = lax.rem(turned, 4)
        base = jnp.zeros((wide, wide), F32)
        for c in range(3):
            for t in range(4):
                line = jnp.concatenate([taps[c, t : t + 1, :]] * len(SLOT), axis=1)
                base = jnp.where((ch == c) & (tap == t), line, base)
        for g in range(GROUPS):
            we[par * GROUPS + g] = jnp.where(turned // 4 == 4 * g + pos, base, 0.0).astype(BF16)
    zero = jnp.zeros((feat, feat), F32)
    mid = [w_mid[j].astype(F32) for j in range(3)]

    def block(came, goes):
        j = came - goes + 1
        return mid[j] if 0 <= j < 3 else zero

    for n, came in enumerate(SLOT):
        blocks = [block(came, goes) for goes in SLOT]
        wm[0, n * feat : (n + 1) * feat, :] = jnp.concatenate(blocks, axis=1).astype(BF16)
    for n in range(4):
        blocks = [zero] * 4
        blocks[n ^ 1] = mid[2 if n % 2 == 0 else 0]
        wm[1, n * feat : (n + 1) * feat, :] = jnp.concatenate(blocks, axis=1).astype(BF16)

    def sample(shape):
        col = iota(shape, 1)
        m = lax.rem(col, HALF)
        edge = jnp.where(m == HALF - 1, -1, jnp.where(m == 0, HALF, -4 * HALF))
        return jnp.where(col >= 2 * HALF, edge, m)

    near, far = sample((4, wide)), sample((feat, wide))
    for par in range(2):
        pick = jnp.where(lax.rem(near - 2 * par + 1 + 8 * HALF, 4) == iota((4, wide), 0), 1.0, 0.0).astype(BF16)
        base = lax.dot_general(w_out[...], pick, (((0,), (0,)), ((), ())), preferred_element_type=F32)
        for g in range(GROUPS):
            for n, i in enumerate(SLOT):
                d = far - 4 * (4 * g + i) - 2 * par + 1
                at = ((par * GROUPS + g) * len(SLOT) + n) * feat
                wo[at : at + feat, :] = jnp.where((d >= 0) & (d < 4), base, 0.0).astype(BF16)
    bi[...] = jnp.concatenate([bias[...]] * len(SLOT), axis=1)


def rectified(h, bias):
    cubes = h.reshape(h.shape[0] // bias.shape[0], bias.shape[0], h.shape[1])
    return jnp.maximum(cubes + bias[None], 0.0).reshape(h.shape)


def enter(zs, hs, we, b0, blocks):
    per = zs.shape[1] // blocks
    for par in range(2):
        for g in range(GROUPS):
            h = jnp.dot(zs[par], we[par * GROUPS + g], preferred_element_type=F32)
            h = rectified(h, b0).astype(BF16)
            for b in range(blocks):
                at = per + (b * GROUPS + g) * per
                hs[par, at : at + per, :] = h[b * per : (b + 1) * per]


def prepare(zs, pre, we, blocks):
    per = zs.shape[1] // blocks
    for par in range(2):
        for g in range(GROUPS):
            h = jnp.dot(zs[par], we[par * GROUPS + g], preferred_element_type=F32)
            for b in range(blocks):
                at = per + (b * GROUPS + g) * per
                pre[par, at : at + per, :] = h[b * per : (b + 1) * per]


def leave(hs, gs, ys, wm, wo, b1, b0=None):
    rows, wide = gs.shape[0], hs.shape[2]
    blocks = ys.shape[0] - 2
    per, half = rows // blocks, wide // 2
    low = iota((rows, half), 1) < half // 2
    for r in range(per, per + GROUPS * rows, rows):
        edge = [jnp.where(low, hs[par, r + per : r + per + rows, :half], hs[par, r - per : r - per + rows, :half]) for par in range(2)]
        if b0 is not None:
            edge = [rectified(e, b0[:, :half]).astype(BF16) for e in edge]
        edge = jnp.dot(jnp.concatenate(edge, axis=1), wm[1], preferred_element_type=F32)
        for par in range(2):
            here = hs[par, r : r + rows, :]
            if b0 is not None:
                here = rectified(here, b0).astype(BF16)
            g = jnp.dot(here, wm[0], preferred_element_type=F32)
            ends = g[:, :half] + edge[:, par * half : (par + 1) * half]
            g = [rectified(ends, b1[:, :half]), rectified(g[:, half:], b1[:, half:])]
            for n in range(rows // per):
                b, q = divmod(r // per - 1 + n, GROUPS)
                for i in range(2):
                    col = (par * GROUPS + q) * wide + i * half
                    gs[b * per : (b + 1) * per, col : col + half] = g[i][n * per : (n + 1) * per].astype(BF16)
    part = blocks // 4
    for b in range(0, blocks, part):
        y = jnp.dot(gs[b * per : (b + part) * per, :], wo[...], preferred_element_type=F32)
        ys[1 + b : 1 + b + part] = y.reshape(part, per, wide)


def patch_kernel(sizes, *refs):
    scalars, (guess, mixtures), refs = refs[:4], refs[4:6], refs[6:]
    lags, order, tallies, pace = refs[45:49]
    given, out = refs[:8], refs[8]
    (gbuf, mbuf, sendx, recvx, sendm, recvm, backs, backr, sende, recve) = refs[9:19]
    (xs, ps, mx, rolled, mf, member, zs, hs, gs, ys) = refs[19:29]
    pre = refs[49]
    ta, tb, held = refs[29:33], refs[33:37], refs[37:45]
    load_sem, ssem, rsem = refs[50:]
    n_shot, n_line, n_tm = sizes
    count = math.prod(sizes)
    axes = [lax.axis_index(a) for a in AXES]
    turns = [[axes[i]] + [lax.rem(axes[i] + d, n) for d in range(1, n)] for i, n in enumerate(sizes)]
    at_shot, at_line, at_tm = axes

    def number(s, l, t):
        return (s * n_line + l) * n_tm + t

    def device(s, l, t):
        return {"shot": s, "line": l, "tm": t}

    me = number(*axes)
    peers = [(s, l, t) for s in turns[0] for l in turns[1] for t in turns[2]][1:]
    shots = n_shot
    n_mix = mixtures.shape[0]
    run = shots // n_mix
    recv_n, tl = guess.shape[1:]
    lc = recv_n // count
    tile = 2 * HALF
    blocks = tl * n_tm // HALF
    each = tl // HALF
    back_kind = 2 + ITERS * n_line

    barrier = pltpu.get_barrier_semaphore()
    for p in peers:
        pl.semaphore_signal(barrier, inc=1, device_id=device(*p), device_id_type=pl.DeviceIdType.MESH)
    pairs = [(guess.at[0], gbuf), (mixtures, mbuf)] + list(zip(given, held)) + list(zip(scalars, refs[45:49]))
    loads = [pltpu.make_async_copy(a, b, load_sem.at[i]) for i, (a, b) in enumerate(pairs)]
    for copy in loads:
        copy.start()

    def link(which, src, dst, to, came):
        return pltpu.make_async_remote_copy(
            src_ref=src,
            dst_ref=dst,
            send_sem=ssem.at[which, number(*to)],
            recv_sem=rsem.at[which, came],
            device_id=device(*to),
            device_id_type=pl.DeviceIdType.MESH,
        )

    row, col = iota((recv_n, recv_n), 0), iota((recv_n, recv_n), 1)
    perm = jnp.where(col == lax.rem(row, lc) * count + row // lc, 1.0, 0.0).astype(BF16)
    loads[0].wait()
    v = jnp.dot(perm, gbuf[...], preferred_element_type=F32)
    for k in range(count):
        part = v[k * lc : (k + 1) * lc]
        sendx[k] = jnp.concatenate([part[:, : tl // 2], part[:, tl // 2 :]], axis=0).astype(BF16)
    pl.semaphore_wait(barrier, count - 1)
    for p in peers:
        link(0, sendx.at[number(*p)], recvx.at[me], p, me).start()

    loads[1].wait()
    other = (at_shot, n_line - 1 - at_line, at_tm)
    row, col = iota((2 * lc, recv_n), 0), iota((2 * lc, recv_n), 1)
    wanted = jnp.where(row < lc, me, number(*other))
    pick = jnp.where(col == lax.rem(row, lc) * count + wanted, 1.0, 0.0).astype(BF16)
    picked = [jnp.dot(pick, mbuf[g], preferred_element_type=F32) for g in range(n_mix)]
    sendm[...] = jnp.concatenate([p[lc:] for p in picked], axis=0).astype(BF16)
    link(1, sendm, recvm.at[at_line], other, me).start()
    recvm[at_line] = jnp.concatenate([p[:lc] for p in picked], axis=0).astype(BF16)
    recvx[me] = sendx[me]

    for copy in loads[2:]:
        copy.wait()
    weave(*held[:4], *ta)
    weave(*held[4:], *tb)
    edges = hs.shape[1] - (GROUPS * blocks + 1) * (hs.shape[1] // (GROUPS * blocks + 2))
    hs[:, :edges] = jnp.zeros_like(hs[:, :edges])
    hs[:, hs.shape[1] - edges :] = jnp.zeros_like(hs[:, :edges])
    silent = jnp.full((n_line, 2, edges, pre.shape[3]), -1e30, F32)
    pre[:, :, :edges] = silent
    pre[:, :, pre.shape[2] - edges :] = silent
    for ref in (ys, rolled, mf, xs):
        ref[0] = jnp.zeros_like(ref[0])
        ref[ref.shape[0] - 1] = jnp.zeros_like(ref[0])
    for ref, at in ((rolled, 1), (mf, blocks)):
        ref[at] = jnp.zeros_like(ref[at])
    sec = []
    for rows in ((lc, tile), (count, tile)):
        if rows[0] == lc:
            q = iota(rows, 0) * count + me
        else:
            q = lax.rem(iota(rows, 1), lc) * count + iota(rows, 0)
        edge, at, size = jnp.int32(0), jnp.zeros(rows, jnp.int32), jnp.zeros(rows, jnp.int32)
        for p in range(tallies.shape[0]):
            at = jnp.where(q >= edge, p, at)
            size = jnp.where(q >= edge, tallies[p], size)
            edge = edge + tallies[p]
        sec.append((at, size))
    scale = 1.0 / (sec[0][1] * (shots * tl * n_tm)).astype(F32)
    for k in range(count):
        member[k] = jnp.where(sec[0][0] == sec[1][0][k : k + 1, :], scale, 0.0)

    lane = iota((lc, tile), 1)
    low = lane < HALF
    inner = lax.rem(lane, HALF)

    def unfold(v):
        turned = pltpu.roll(v, HALF, 1)
        return jnp.where(low, v, turned), jnp.where(low, turned, v)

    for p in peers:
        link(0, sendx.at[number(*p)], recvx.at[number(*p)], p, number(*p)).wait_recv()
    for p in range(count):
        s, l, t = p // (n_line * n_tm), p // n_tm % n_line, p % n_tm
        v = recvx[p].astype(F32)
        for j in range(tl // tile):
            h, c = divmod(j * tile, tl // 2)
            two = unfold(v[h * lc : (h + 1) * lc, c : c + tile])
            for n in range(2):
                xs[1 + l, t * each + 2 * j + n, s] = two[n]

    def unfold_mixtures():
        link(1, sendm, recvm.at[n_line - 1 - at_line], other, number(*other)).wait_recv()
        for l in range(n_line):
            v = recvm[l].astype(F32)
            for g in range(n_mix):
                for j in range(blocks // 2):
                    two = unfold(v[g * lc : (g + 1) * lc, j * tile : (j + 1) * tile])
                    for n in range(2):
                        mx[2 * j + n, g * n_line + l] = two[n]

    cube = (shots, lc, tile)
    per = shots * lc
    clow = iota(cube, 2) < HALF
    line_of = iota(cube, 1)
    spot = lax.rem(iota((per, tile), 1), HALF)
    wide_spot = lax.rem(iota((per, 2 * tile), 1), HALF)
    early = spot < HALF // 2
    one = jnp.zeros((1, lc, tile), F32)
    nothing = jnp.zeros((per, 2 * tile), F32)

    def widen(make):
        ahead_of = [nothing, make(0)]
        for b in range(blocks):
            ahead_of.append(make(b + 1) if b + 1 < blocks else nothing)
            before, here, after = ahead_of[b : b + 3]
            zs[0, b * per : (b + 1) * per, :] = jnp.where(wide_spot == HALF - 1, before, here).astype(BF16)
            zs[1, b * per : (b + 1) * per, :] = jnp.where(wide_spot == 0, after, here).astype(BF16)

    def beside(before, here, after):
        both = jnp.where(clow, before, here)
        return jnp.concatenate([both.reshape(per, tile), after.reshape(per, tile)], axis=1)

    def change(b):
        return ys[b + 1, :, :tile] + jnp.where(early, ys[b, :, tile:], ys[b + 2, :, tile:])

    group = []
    for s in range(shots):
        found = jnp.int32(0)
        for k in range(shots):
            found = jnp.where(order[k] == s, k // run, found)
        group.append(found)
    rest = [lax.rem(lags[s], HALF) for s in range(shots)]
    far = [lags[s] // HALF for s in range(shots)]

    def over_lines(it, l):
        def make(b):
            x = xs[1 + l, b]
            before = jnp.where(line_of == lc - 1, xs[l, b], x)
            after = jnp.where(line_of == 0, xs[2 + l, b], x)
            return beside(pltpu.roll(before, 1, 1), x, pltpu.roll(after, lc - 1, 1))

        widen(make)
        biases = [jnp.broadcast_to(ta[3][i : i + 1, :], (lc, 2 * tile)) for i in range(2)]
        enter(zs, hs, ta[0], biases[0], blocks)
        leave(hs, gs, ys, *ta[1:3], biases[1])
        energy = jnp.zeros((lc, tile), F32)
        for b in range(blocks):
            x = (xs[1 + l, b] + change(b).reshape(cube)).astype(BF16).astype(F32)
            ps[l, b] = x
            energy = energy + jnp.sum(x * x, axis=0)
        energy = 0.5 * jnp.sum(energy, axis=1, keepdims=True)
        mine = jnp.sum(jnp.where(lane == iota((lc, tile), 0), energy, 0.0), axis=0, keepdims=True)
        at = it * n_line + l
        sende[at] = mine
        recve[at, me] = mine
        for p in peers:
            link(2 + at, sende.at[at], recve.at[at, me], p, me).start()

    def before_shots(l):
        def make(b):
            x = ps[l, b]
            return beside(jnp.concatenate([one, x[: shots - 1]], axis=0), x, jnp.concatenate([x[1:], one], axis=0))

        widen(make)
        prepare(zs, pre.at[l], tb[0], blocks)

    def over_shots(it, l):
        at = it * n_line + l
        for p in peers:
            link(2 + at, sende.at[at], recve.at[at, number(*p)], p, number(*p)).wait_recv()
        total = jnp.zeros((lc, tile), F32)
        for k in range(count):
            total = total + member[k] * recve[at, k]
        mean = jnp.sum(total, axis=1, keepdims=True)
        rms = jnp.broadcast_to(jnp.sqrt(mean + EPSILON), (lc, 2 * tile))
        biases = [rms * tb[3][i : i + 1, :] for i in range(2)]
        leave(pre.at[l], gs, ys, *tb[1:3], biases[1], biases[0])
        for b in range(blocks):
            x = (ps[l, b] + change(b).reshape(cube)).astype(BF16).astype(F32)
            ps[l, b] = x
            for s in range(shots):
                rolled[b + 2, s] = pltpu.roll(x[s], rest[s], 1)
        for g in range(n_mix):
            acc = -mx[:, g * n_line + l]
            for i in range(run):
                s = order[g * run + i]
                lag = lags[s]
                a = 2 - lag // HALF
                near, late = rolled[pl.ds(a, blocks), s], rolled[pl.ds(a - 1, blocks), s]
                acc = acc + jnp.where((inner >= lax.rem(lag, HALF))[None], near, late)
            mf[:blocks, g] = acc
        for s in range(shots):
            m = mf[:, group[s]]
            rolled[: blocks + 2, s] = pltpu.roll(m, lax.rem(tile - rest[s], tile), 2)
        for s in range(shots):
            near, late = rolled[pl.ds(far[s], blocks), s], rolled[pl.ds(far[s] + 1, blocks), s]
            back = jnp.where((inner < HALF - rest[s])[None], near, late)
            xs[1 + l, :, s] = (ps[l, :, s] - pace[it] * back).astype(BF16).astype(F32)
        rolled[:2] = jnp.zeros_like(rolled[:2])

        @pl.when(it == ITERS - 1)
        def _():
            for s in range(n_shot):
                for t in range(n_tm):
                    tiles = []
                    for j in range(tl // tile):
                        b = t * each + 2 * j
                        tiles.append(jnp.where(low, xs[1 + l, b, s], xs[1 + l, b + 1, s]))
                    n = len(tiles) // 2
                    halves = [jnp.concatenate(tiles[:n], axis=1), jnp.concatenate(tiles[n:], axis=1)]
                    backs[number(s, l, t)] = jnp.concatenate(halves, axis=0).astype(BF16)
            own = (at_shot, l, at_tm)
            for s in turns[0]:
                for t in turns[2]:
                    if s is at_shot and t is at_tm:
                        continue
                    link(back_kind, backs.at[number(s, l, t)], backr.at[me], (s, l, t), me).start()

            @pl.when(l != at_line)
            def _():
                link(back_kind, backs.at[number(*own)], backr.at[me], own, me).start()

    def iterate(it, carry):
        def lines(l, carry):
            over_lines(it, l)
            return carry

        def stations(l, carry):
            over_shots(it, l)
            return carry

        def first(l, carry):
            before_shots(l)
            return carry

        lax.fori_loop(0, n_line, lines, 0)
        lax.fori_loop(0, n_line, first, 0)

        @pl.when(it == 0)
        def _():
            unfold_mixtures()

        lax.fori_loop(0, n_line, stations, 0)
        return carry

    lax.fori_loop(0, ITERS, iterate, 0)

    backr[me] = backs[me]
    row, col = iota((recv_n, recv_n), 0), iota((recv_n, recv_n), 1)
    perm = jnp.where(row == lax.rem(col, lc) * count + col // lc, 1.0, 0.0).astype(BF16)
    for p in peers:
        link(back_kind, backs.at[number(*p)], backr.at[number(*p)], p, number(*p)).wait_recv()
    v = []
    for k in range(count):
        part = backr[k].astype(F32)
        v.append(jnp.concatenate([part[:lc], part[lc:]], axis=1))
    v = jnp.concatenate(v, axis=0).astype(BF16)
    out[0] = jnp.dot(perm, v, preferred_element_type=F32).astype(BF16)
    link(1, sendm, recvm.at[at_line], other, me).wait_send()
    for p in peers:
        link(0, sendx.at[number(*p)], recvx.at[me], p, me).wait_send()
        for at in range(ITERS * n_line):
            link(2 + at, sende.at[at], recve.at[at, me], p, me).wait_send()
        link(back_kind, backs.at[number(*p)], backr.at[me], p, me).wait_send()


def patch(guess, mixtures, lags, order, tallies, wa, wb, pace, sizes):
    count = math.prod(sizes)
    n_shot, n_line, n_tm = sizes
    recv, tl = guess.shape[1:]
    n_mix, nt = mixtures.shape[0], mixtures.shape[2]
    lc, tile = recv // count, 2 * HALF
    blocks = nt // HALF
    per, feat = n_shot * lc, wa[0].shape[2]
    wide = feat * len(SLOT)
    rows = blocks * per
    weights = [w.transpose(1, 0, 2) if i == 0 else w for part in (wa, wb) for i, w in enumerate(part)]
    v, h = (pl.BlockSpec(memory_space=m) for m in (pltpu.VMEM, pl.ANY))
    slab = pltpu.VMEM((count, 2 * lc, tl // 2), BF16)
    woven = [
        pltpu.VMEM((2 * GROUPS, wide, wide), BF16),
        pltpu.VMEM((2, wide, wide), BF16),
        pltpu.VMEM((2 * GROUPS * wide, wide), BF16),
        pltpu.VMEM((2, wide), F32),
    ]
    kinds = 3 + ITERS * n_line
    return pl.pallas_call(
        functools.partial(patch_kernel, sizes),
        out_shape=pltpu.VMEM(guess.shape, BF16),
        in_specs=[h] * 14,
        out_specs=v,
        scratch_shapes=[
            pltpu.VMEM((recv, tl), BF16),
            pltpu.VMEM(mixtures.shape, BF16),
            slab,
            slab,
            pltpu.VMEM((n_mix * lc, nt), BF16),
            pltpu.VMEM((n_line, n_mix * lc, nt), BF16),
            slab,
            slab,
            pltpu.VMEM((ITERS * n_line, 1, tile), F32),
            pltpu.VMEM((ITERS * n_line, count, 1, tile), F32),
            pltpu.VMEM((n_line + 2, blocks, n_shot, lc, tile), F32),
            pltpu.VMEM((n_line, blocks, n_shot, lc, tile), F32),
            pltpu.VMEM((blocks, n_mix * n_line, lc, tile), F32),
            pltpu.VMEM((blocks + 2, n_shot, lc, tile), F32),
            pltpu.VMEM((blocks + 2, n_mix, lc, tile), F32),
            pltpu.VMEM((count, lc, tile), F32),
            pltpu.VMEM((2, rows, wide), BF16),
            pltpu.VMEM((2, GROUPS * rows + 2 * per, wide), BF16),
            pltpu.VMEM((rows, 2 * GROUPS * wide), BF16),
            pltpu.VMEM((blocks + 2, per, wide), F32),
            *woven,
            *woven,
            *[pltpu.VMEM(w.shape, w.dtype) for w in weights],
            *[pltpu.SMEM(w.shape, w.dtype) for w in (lags, order, tallies, pace)],
            pltpu.VMEM((n_line, 2, GROUPS * rows + 2 * per, wide), F32),
            pltpu.SemaphoreType.DMA((6 + len(weights),)),
            pltpu.SemaphoreType.DMA((kinds, count)),
            pltpu.SemaphoreType.DMA((kinds, count)),
        ],
        compiler_params=pltpu.CompilerParams(vmem_limit_bytes=56 * 2**20, collective_id=1, has_side_effects=True),
    )(lags, order, tallies, pace, guess, mixtures, *weights)


def per_device(guess, mixtures, lags, order, tallies, e1, m1, x1, b1, e2, m2, x2, b2, pace):
    sh, recv, tl = guess.shape
    n_shot, n_line, n_tm = (lax.axis_size(a) for a in AXES)
    whole = RPL % (n_shot * n_line * n_tm) == 0
    where = AXES if whole else AXES[1:]
    parts = math.prod(lax.axis_size(a) for a in where)
    kp, lh = RPL // parts, recv // RPL
    lines, shots, nt = lh * n_line, sh * n_shot, tl * n_tm
    planes, s1 = nt // 2 // C, shots if whole else sh
    r1 = lines * kp
    r2 = r1 if whole else r1 // n_shot
    lanes1, lanes2 = 2 * s1 * r1, 2 * shots * r2
    sources = n_shot if whole else 1
    i32 = functools.partial(jnp.arange, dtype=jnp.int32)
    n_mix, feat = mixtures.shape[0], e1.shape[2]
    square = sh == 1 and kp == 1 and n_line == 2 and shots % n_mix == 0 and feat == HALF
    square = square and lh == C and tl % (4 * HALF) == 0 and n_mix * lh % 16 == 0
    square = square and lines == parts and 2 * (n_mix // n_line) == n_line
    if square:
        sizes = (n_shot, n_line, n_tm)
        return patch(guess, mixtures, lags, order, tallies, (e1, m1, x1, b1), (e2, m2, x2, b2), pace, sizes)

    at_shot = lax.axis_index("shot")
    n_mix, run = mixtures.shape[0], nt // C
    fused = whole and sh == 1 and kp == 1 and C % n_tm == 0 and n_shot * n_tm == C
    x = guess.reshape(sh, lh, parts, kp, tl).transpose(2, 0, 1, 3, 4)
    if fused:
        share = (at_shot * n_tm + lax.axis_index("tm")) * run
        mine = lax.dynamic_slice_in_dim(mixtures, share, run, axis=2).reshape(n_mix, lh, parts, run)
        mine = mine.transpose(2, 1, 0, 3).reshape(parts, lh, n_mix * run)
        x = jnp.concatenate([x.reshape(parts, lh, tl), mine], axis=2)
    x = lax.all_to_all(x, where, split_axis=0, concat_axis=0, tiled=False)
    if not fused:
        x = x.reshape(sources, n_line, n_tm, sh, lh, kp, tl).transpose(0, 3, 1, 4, 5, 2, 6)
        x = x.reshape(s1, r1, C, planes, 2).transpose(3, 2, 4, 0, 1).reshape(planes, C, lanes1)


    def first_k(line):
        block = line * n_tm + lax.axis_index("tm")
        return (at_shot * n_line * n_tm + block if whole else block) * kp

    if not fused:
        grid = mixtures.reshape(n_mix, lh, RPL, nt)
        sent = jnp.stack([lax.dynamic_slice_in_dim(grid, first_k(d), kp, axis=2) for d in range(n_line)])
        m = lax.all_to_all(sent, "line", split_axis=0, concat_axis=0)
        m = m.transpose(1, 0, 2, 3, 4).reshape(n_mix, r1, nt)
        if not whole:
            m = lax.dynamic_slice_in_dim(m, at_shot * r2, r2, axis=1)
        m = m.reshape(n_mix, r2, C, planes, 2).transpose(3, 2, 4, 0, 1).reshape(planes * C, 2 * n_mix * r2)

    np_ = tallies.shape[0]
    here = i32(np_)
    offsets = jnp.sum(jnp.where(here[None, :] < here[:, None], tallies[None, :], 0), axis=1)
    mine = first_k(lax.axis_index("line"))

    def one_hot(r):
        line, k = r // kp, mine + lax.rem(r, kp)
        q = lax.rem(line, lh) * RPL + k
        inside = (offsets[:, None] <= q[None, :]) & (q[None, :] < (offsets + tallies)[:, None])
        block = (line // lh)[None, :] == i32(n_line)[:, None]
        return (block[:, None, :] & inside[None, :, :]).reshape(n_line * np_, r.shape[0]).astype(F32)

    member = jnp.tile(one_hot(i32(r1)), (1, 2 * s1))
    r_own = i32(r2) if whole else at_shot * r2 + i32(r2)
    count = jnp.tile((tallies * (shots * nt)).astype(F32), n_line)
    spread = jnp.tile(one_hot(r_own) / count[:, None], (1, 2 * shots))

    sid = i32(shots)
    place = jnp.sum(jnp.where(order[None, :] == sid[:, None], sid[None, :], 0), axis=1)
    group = place // (shots // n_mix)
    same = (group[:, None] == group[None, :]).astype(BF16)
    chosen = (i32(n_mix)[:, None] == group[None, :]).astype(BF16)
    rest, two = jnp.eye(r2, dtype=BF16), jnp.eye(2, dtype=BF16)
    join = jnp.kron(two, jnp.kron(same, rest))
    take = jnp.kron(two, jnp.kron(chosen, rest))

    n1, n2 = s1 * r1, shots * r2
    a, b = np.arange(n1)[:, None], np.arange(n1)[None, :]
    near1 = np.stack([(a == b + (c - 1) * kp) & (a // r1 == b // r1) for c in range(3)])
    a, b = np.arange(n2)[:, None], np.arange(n2)[None, :]
    near2 = np.stack([a == b + (c - 1) * r2 for c in range(3)])
    wa = prepared(e1, m1, x1, b1, near1)
    wb = prepared(e2, m2, x2, b2, near2)

    rows = planes * C
    tot1, tot2 = pltpu.VMEM((rows, 2 * lanes1), F32), pltpu.VMEM((rows, 2 * lanes2), F32)
    feat = e1.shape[2]
    band = pltpu.VMEM((3 * PACK * feat, PACK * feat), BF16)
    buf = pltpu.VMEM((2, 2 * planes, C, lanes2), F32)
    spass = jax.ShapeDtypeStruct((planes, C, lanes1), BF16)
    part = jax.ShapeDtypeStruct((n_line * np_, 128), F32)
    moved = jax.ShapeDtypeStruct((planes, C, lanes2), BF16)

    def to_stations(y):
        y = y.reshape(rows, 2, sh, n_shot, r2)
        y = lax.all_to_all(y, "shot", split_axis=3, concat_axis=2, tiled=True)
        return y.reshape(planes, C, lanes2)

    def to_shots(y):
        y = y.reshape(rows, 2, shots, 1, r2)
        y = lax.all_to_all(y, "shot", split_axis=2, concat_axis=3, tiled=True)
        return y.reshape(planes, C, lanes1)

    dims = (n_shot, n_line, n_tm)
    cube = pltpu.VMEM((planes, C, lanes1), F32)
    if fused:
        mixed = jax.ShapeDtypeStruct((rows, 2 * n_mix * r2), BF16)
        side = pltpu.VMEM((planes, C, 2 * n_mix * r2), F32)
        sp, energy, m = call(
            functools.partial(entry_kernel, dims),
            (spass, part, mixed),
            (x, *wa, member),
            0,
            [tot1, band, cube, side],
        )
    else:
        sp, energy = call(first_kernel, (spass, part), (x, *wa, member), 0, [tot1, band])
    for it in range(ITERS):
        tot = summed(energy, (n_shot, n_line, n_tm)) if whole else lax.psum(energy, AXES)
        if not whole:
            sp = to_stations(sp)
        ins = (lags, pace, sp, tot, spread, *wb, join, m, take)
        if whole and it < ITERS - 1:
            sp, energy = call(
                functools.partial(both_kernel, it, shots), (spass, part), (*ins, *wa, member), 2, [buf, tot2, band]
            )
            continue
        if fused:
            back = jax.ShapeDtypeStruct((parts, lh, tl), BF16)
            x = call(functools.partial(exit_kernel, it, dims), back, ins, 2, [buf, tot2, band, cube])
            continue
        x = call(functools.partial(station_kernel, it, shots), moved, ins, 2, [buf, tot2, band])
        if not whole:
            x = to_shots(x)
            if it < ITERS - 1:
                sp, energy = call(first_kernel, (spass, part), (x, *wa, member), 0, [tot1, band])

    if not fused:
        x = x.reshape(planes, C, 2, s1, r1).transpose(3, 4, 1, 0, 2)
        x = x.reshape(sources, sh, n_line, lh, kp, n_tm, tl).transpose(0, 2, 5, 1, 3, 4, 6)
    x = lax.all_to_all(x.reshape(parts, sh, lh, kp, tl), where, split_axis=0, concat_axis=0)
    return x.transpose(1, 2, 0, 3, 4).reshape(sh, recv, tl)


def solution(mesh):
    spec = P(("group", "shot"), "line", "tm")
    placed = (spec, P("group", "line", None), P("group"), P("group"), P("group")) + (P(),) * 9
    return jax.shard_map(per_device, mesh=mesh, in_specs=placed, out_specs=spec, check_vma=False)
```

```python
import functools
import math

import jax
import jax.numpy as jnp
import numpy as np
from jax import lax
from jax.experimental import pallas as pl
from jax.experimental.pallas import tpu as pltpu
from jax.sharding import PartitionSpec as P

RPL = 16
ITERS = 2
EPSILON = 1e-05
C = 8
PACK = 4
TAPS = (1, 2, 3, 0)
F32, BF16 = jnp.float32, jnp.bfloat16
AXES = ("shot", "line", "tm")


def ahead(x, k):
    edge = pltpu.roll(x[:k], C - 1, 1)
    edge = jnp.where(lax.broadcasted_iota(jnp.int32, edge.shape, 1) == C - 1, 0.0, edge)
    return edge if k == x.shape[0] else jnp.concatenate([x[k:], edge], axis=0)


def behind(x, k):
    edge = pltpu.roll(x[x.shape[0] - k :], 1, 1)
    edge = jnp.where(lax.broadcasted_iota(jnp.int32, edge.shape, 1) == 0, 0.0, edge)
    return edge if k == x.shape[0] else jnp.concatenate([edge, x[: x.shape[0] - k]], axis=0)


def even_lanes(shape):
    return lax.broadcasted_iota(jnp.int32, shape, len(shape) - 1) < shape[-1] // 2


def net(x, w_in, pick, w_mid, w_out, place, bias, total, band):
    planes, _, lanes = x.shape
    rows = planes * C
    side = jnp.where(even_lanes(x.shape), ahead(x, 1), behind(x, 1))
    z = jnp.concatenate([x, side], axis=2).astype(BF16).reshape(rows, 2 * lanes)
    total[...] = jnp.zeros_like(total)
    wide = w_in.shape[1]
    feat = wide // PACK
    for j in range(3):
        tap = w_mid[j].astype(F32)
        for i in range(PACK):
            row = [tap if p == i else jnp.zeros_like(tap) for p in range(PACK)]
            at = (j * PACK + i) * feat
            band[at : at + feat, :] = jnp.concatenate(row, axis=1).astype(BF16)

    def step(q, carry):
        w_here = jnp.dot(pick[q], w_in[...], preferred_element_type=F32).astype(BF16)
        o_here = jnp.dot(w_out[...], place[q], preferred_element_type=F32).astype(BF16)
        h = jnp.dot(z, w_here, preferred_element_type=F32)
        h = jnp.maximum(h + bias[0:1, :], 0.0)
        cube = h.reshape(planes, C, wide)
        first = ahead(cube[:2], 2).reshape(2 * C, wide).astype(BF16)
        last = behind(cube[planes - 2 :], 2).reshape(2 * C, wide).astype(BF16)
        hb = h.astype(BF16)
        early = jnp.concatenate([last, hb[: rows - 2 * C]], axis=0)
        late = jnp.concatenate([hb[2 * C :], first], axis=0)
        g = jnp.dot(jnp.concatenate([early, hb, late], axis=1), band[...], preferred_element_type=F32)
        g = jnp.maximum(g + bias[1:2, :], 0.0).astype(BF16)
        total[...] += jnp.dot(g, o_here, preferred_element_type=F32)
        return carry

    lax.fori_loop(0, pick.shape[0], step, 0, unroll=2)
    y = total[...].reshape(planes, C, 2 * lanes)
    a, b = y[:, :, :lanes], y[:, :, lanes:]
    return a + jnp.where(even_lanes(b.shape), behind(b, 1), ahead(b, 1))


def shot_step(x, weights, member, out_ref, part_ref, total, band):
    y = (x + net(x, *weights, total, band)).astype(BF16)
    out_ref[...] = y
    y = y.astype(F32)
    energy = jnp.sum(jnp.sum(y * y, axis=0), axis=0, keepdims=True)
    sums = jnp.sum(member[...] * energy, axis=1, keepdims=True)
    part_ref[...] = jnp.broadcast_to(sums, part_ref.shape)


def shifted(buf, lag_ref, shots, forward):
    planes, lanes = buf.shape[1] // 2, buf.shape[3]
    shape = (planes, C, lanes)
    even = even_lanes(shape)
    per = lanes // 2 // shots
    lane_shot = lax.rem(lax.broadcasted_iota(jnp.int32, shape, 2), lanes // 2) // per
    out = jnp.zeros(shape, F32)
    for s in range(shots):
        lag = lag_ref[s]
        half, odd = lag // 2, lax.rem(lag, 2)
        at_even = half if forward else planes - half - odd
        at_odd = half + odd if forward else planes - half
        one = jnp.where(even, buf[odd, pl.ds(at_even, planes)], buf[odd, pl.ds(at_odd, planes)])
        out = jnp.where(lane_shot == s, one, out)
    return out


def station_step(shots, sp, tot_ref, spread, weights, lags, join, mix, take, pace, buf, total, band):
    planes, _, lanes = sp.shape
    rows = planes * C
    mean = jnp.sum(tot_ref[:, 0:1] * spread[...], axis=0, keepdims=True)
    rms = jnp.sqrt(mean + EPSILON).reshape(1, 1, lanes)
    normed = (sp / rms).astype(BF16).astype(F32)
    settled = (sp + rms * net(normed, *weights, total, band)).astype(BF16).astype(F32)

    def fill(x, forward):
        far = ahead(x, planes) if forward else behind(x, planes)
        near_at, far_at = (0, planes) if forward else (planes, 0)
        for v, at in ((x, near_at), (far, far_at)):
            buf[0, at : at + planes] = v
            h = lanes // 2
            buf[1, at : at + planes] = jnp.concatenate([v[:, :, h:], v[:, :, :h]], axis=2)

    fill(settled, False)
    fired = shifted(buf, lags, shots, False).astype(BF16).reshape(rows, lanes)
    misfit = jnp.dot(fired, join[...], preferred_element_type=F32)
    misfit -= jnp.dot(mix[...], take[...], preferred_element_type=F32)
    fill(misfit.reshape(planes, C, lanes), True)
    return (settled - pace * shifted(buf, lags, shots, True)).astype(BF16)


def by_phase(width):
    row = lax.broadcasted_iota(jnp.int32, (width, width), 0)
    col = lax.broadcasted_iota(jnp.int32, (width, width), 1)
    half = width // 2
    return jnp.where(col == 2 * lax.rem(row, half) + row // half, 1.0, 0.0).astype(BF16)


def unfold(read, into, sort):
    planes = into.shape[0]
    for c in range(C):
        v = lax.dot_general(sort, read(c), (((1,), (1,)), ((), ())), preferred_element_type=F32)
        into[:, c, :] = jnp.concatenate([v[:planes], v[planes:]], axis=1)


def entry_kernel(
    dims, x, wi, wp, wm, wo, wq, bi, member, out, part, mix, total, band, cube, side
):
    shots, blocks, halves = dims
    width = 2 * cube.shape[0]
    sort, each = by_phase(width), C // halves

    def traces(c):
        at, t = slice(c % each * width, (c % each + 1) * width), c // each
        rows = [x[(s * blocks + b) * halves + t, :, at].astype(F32) for s in range(shots) for b in range(blocks)]
        return jnp.concatenate(rows, axis=0).astype(BF16)

    tl = each * width

    def records(c):
        s, t = c // halves, c % halves
        rows = [
            x[(s * blocks + b) * halves + t, :, tl + g * width : tl + (g + 1) * width].astype(F32)
            for g in range((x.shape[2] - tl) // width)
            for b in range(blocks)
        ]
        return jnp.concatenate(rows, axis=0).astype(BF16)

    unfold(records, side, sort)
    mix[...] = side[...].astype(BF16).reshape(mix.shape)
    unfold(traces, cube, sort)
    shot_step(cube[...], (wi, wp, wm, wo, wq, bi), member, out, part, total, band)


def exit_kernel(
    it, dims, lags, pace, sp, tot, spread, wi, wp, wm, wo, wq, bi, join, mix, take, out, buf, total, band, cube
):
    shots, blocks, halves = dims
    width = 2 * cube.shape[0]
    sort, each = by_phase(width), C // halves
    x = station_step(
        shots, sp[...].astype(F32), tot, spread, (wi, wp, wm, wo, wq, bi), lags, join, mix, take, pace[it], buf, total, band
    )
    cube[...] = x.astype(F32)
    n, lh = cube.shape[2] // 2, out.shape[1]
    for c in range(C):
        v = cube[:, c, :]
        v = jnp.concatenate([v[:, :n], v[:, n:]], axis=0).T.astype(BF16)
        v = jnp.dot(v, sort, preferred_element_type=F32)
        at, t = slice(c % each * width, (c % each + 1) * width), c // each
        for j in range(shots * blocks):
            out[j * halves + t, :, at] = v[j * lh : (j + 1) * lh].astype(BF16)


def first_kernel(x, wi, wp, wm, wo, wq, bi, member, out, part, total, band):
    shot_step(x[...].astype(F32), (wi, wp, wm, wo, wq, bi), member, out, part, total, band)


def station_kernel(it, shots, lags, pace, sp, tot, spread, wi, wp, wm, wo, wq, bi, join, mix, take, out, buf, total, band):
    out[...] = station_step(
        shots, sp[...].astype(F32), tot, spread, (wi, wp, wm, wo, wq, bi), lags, join, mix, take, pace[it], buf, total, band
    )


def both_kernel(
    it, shots, lags, pace, sp, tot, spread, wi, wp, wm, wo, wq, bi, join, mix, take, vi, vp, vm, vo, vq, ci, member, out, part, buf, total, band
):
    x = station_step(
        shots, sp[...].astype(F32), tot, spread, (wi, wp, wm, wo, wq, bi), lags, join, mix, take, pace[it], buf, total, band
    )
    shot_step(x.astype(F32), (vi, vp, vm, vo, vq, ci), member, out, part, total, band)


def call(body, outs, ins, smem, scratch):
    v, s = pl.BlockSpec(memory_space=pltpu.VMEM), pl.BlockSpec(memory_space=pltpu.SMEM)
    return pl.pallas_call(
        body,
        out_shape=outs,
        in_specs=[s] * smem + [v] * (len(ins) - smem),
        out_specs=jax.tree.map(lambda _: v, outs),
        scratch_shapes=scratch,
        compiler_params=pltpu.CompilerParams(vmem_limit_bytes=48 * 2**20),
    )(*ins)


def prepared(w_in, w_mid, w_out, bias, near):
    n, feat = near.shape[1], w_in.shape[2]
    tiles = n // PACK
    cols = near.reshape(3, n, tiles, PACK).transpose(2, 1, 0, 3)
    pick = np.einsum("jk,tnci->tjnkci", np.eye(4)[list(TAPS)], cols).reshape(tiles, 4 * n, 12 * PACK)
    place = np.einsum("kj,tin->tjikn", np.eye(4)[list(TAPS)], np.eye(n).reshape(tiles, PACK, n)).reshape(tiles, 4 * PACK, 4 * n)
    w1 = w_in.reshape(12, 1, 1, feat)
    eye = jnp.eye(PACK, dtype=BF16)
    rows = (w1 * eye[None, :, :, None]).reshape(12 * PACK, PACK * feat)
    w2 = w_out.T.reshape(1, feat, 4, 1)
    ends = (w2 * eye[:, None, None, :]).reshape(PACK * feat, 4 * PACK)
    return rows, jnp.asarray(pick, BF16), w_mid, ends, jnp.asarray(place, BF16), jnp.tile(bias, (1, PACK))


def exchange_kernel(sizes, x, out, slots, send, recv):
    count = math.prod(sizes)
    me = (lax.axis_index("shot") * sizes[1] + lax.axis_index("line")) * sizes[2] + lax.axis_index("tm")

    def peer(off):
        at = lax.rem(me + off, count)
        return {
            "shot": at // (sizes[1] * sizes[2]),
            "line": lax.rem(at // sizes[2], sizes[1]),
            "tm": lax.rem(at, sizes[2]),
        }

    barrier = pltpu.get_barrier_semaphore()
    for off in range(1, count):
        pl.semaphore_signal(barrier, inc=1, device_id=peer(off), device_id_type=pl.DeviceIdType.MESH)
    pl.semaphore_wait(barrier, count - 1)
    copies = []
    for off in range(1, count):
        copy = pltpu.make_async_remote_copy(
            src_ref=x,
            dst_ref=slots.at[off],
            send_sem=send.at[off],
            recv_sem=recv.at[off],
            device_id=peer(off),
            device_id_type=pl.DeviceIdType.MESH,
        )
        copy.start()
        copies.append(copy)
    total = x[...]
    for off, copy in enumerate(copies, 1):
        copy.wait()
        total += slots[off]
    out[...] = total


def summed(x, sizes):
    count, v = math.prod(sizes), pl.BlockSpec(memory_space=pltpu.VMEM)
    return pl.pallas_call(
        functools.partial(exchange_kernel, sizes),
        out_shape=jax.ShapeDtypeStruct(x.shape, x.dtype),
        in_specs=[v],
        out_specs=v,
        scratch_shapes=[
            pltpu.VMEM((count, *x.shape), x.dtype),
            pltpu.SemaphoreType.DMA((count,)),
            pltpu.SemaphoreType.DMA((count,)),
        ],
        compiler_params=pltpu.CompilerParams(collective_id=0, has_side_effects=True),
    )(x)


SLOT = (0, 3, 1, 2)
HALF = 64
GROUPS = 4


def iota(shape, dim):
    return lax.broadcasted_iota(jnp.int32, shape, dim)


def weave(w_in, w_mid, w_out, bias, we, wm, wo, bi):
    feat = w_in.shape[2]
    wide = feat * len(SLOT)
    row, lane = iota((wide, wide), 0), iota((wide, wide), 1)
    at, ch = lax.rem(row, HALF), row // HALF
    slot = lane // feat
    pos = jnp.where(slot == 1, 3, jnp.where(slot == 0, 0, slot - 1))
    taps = w_in[...].astype(F32)
    for par in range(2):
        turned = lax.rem(at + (1 if par == 0 else HALF - 1), HALF)
        tap = lax.rem(turned, 4)
        base = jnp.zeros((wide, wide), F32)
        for c in range(3):
            for t in range(4):
                line = jnp.concatenate([taps[c, t : t + 1, :]] * len(SLOT), axis=1)
                base = jnp.where((ch == c) & (tap == t), line, base)
        for g in range(GROUPS):
            we[par * GROUPS + g] = jnp.where(turned // 4 == 4 * g + pos, base, 0.0).astype(BF16)
    zero = jnp.zeros((feat, feat), F32)
    mid = [w_mid[j].astype(F32) for j in range(3)]

    def block(came, goes):
        j = came - goes + 1
        return mid[j] if 0 <= j < 3 else zero

    for n, came in enumerate(SLOT):
        blocks = [block(came, goes) for goes in SLOT]
        wm[0, n * feat : (n + 1) * feat, :] = jnp.concatenate(blocks, axis=1).astype(BF16)
    for n in range(4):
        blocks = [zero] * 4
        blocks[n ^ 1] = mid[2 if n % 2 == 0 else 0]
        wm[1, n * feat : (n + 1) * feat, :] = jnp.concatenate(blocks, axis=1).astype(BF16)

    def sample(shape):
        col = iota(shape, 1)
        m = lax.rem(col, HALF)
        edge = jnp.where(m == HALF - 1, -1, jnp.where(m == 0, HALF, -4 * HALF))
        return jnp.where(col >= 2 * HALF, edge, m)

    near, far = sample((4, wide)), sample((feat, wide))
    for par in range(2):
        pick = jnp.where(lax.rem(near - 2 * par + 1 + 8 * HALF, 4) == iota((4, wide), 0), 1.0, 0.0).astype(BF16)
        base = lax.dot_general(w_out[...], pick, (((0,), (0,)), ((), ())), preferred_element_type=F32)
        for g in range(GROUPS):
            for n, i in enumerate(SLOT):
                d = far - 4 * (4 * g + i) - 2 * par + 1
                at = ((par * GROUPS + g) * len(SLOT) + n) * feat
                wo[at : at + feat, :] = jnp.where((d >= 0) & (d < 4), base, 0.0).astype(BF16)
    bi[...] = jnp.concatenate([bias[...]] * len(SLOT), axis=1)


def rectified(h, bias):
    cubes = h.reshape(h.shape[0] // bias.shape[0], bias.shape[0], h.shape[1])
    return jnp.maximum(cubes + bias[None], 0.0).reshape(h.shape)


def enter(zs, hs, we, b0, blocks):
    per = zs.shape[1] // blocks
    for par in range(2):
        for g in range(GROUPS):
            h = jnp.dot(zs[par], we[par * GROUPS + g], preferred_element_type=F32)
            h = rectified(h, b0).astype(BF16)
            for b in range(blocks):
                at = per + (b * GROUPS + g) * per
                hs[par, at : at + per, :] = h[b * per : (b + 1) * per]


def prepare(zs, pre, we, blocks):
    per = zs.shape[1] // blocks
    for par in range(2):
        for g in range(GROUPS):
            h = jnp.dot(zs[par], we[par * GROUPS + g], preferred_element_type=F32)
            for b in range(blocks):
                at = per + (b * GROUPS + g) * per
                pre[par, at : at + per, :] = h[b * per : (b + 1) * per]


def leave(hs, gs, ys, wm, wo, b1, b0=None):
    rows, wide = gs.shape[0], hs.shape[2]
    blocks = ys.shape[0] - 2
    per, half = rows // blocks, wide // 2
    low = iota((rows, half), 1) < half // 2
    for r in range(per, per + GROUPS * rows, rows):
        edge = [jnp.where(low, hs[par, r + per : r + per + rows, :half], hs[par, r - per : r - per + rows, :half]) for par in range(2)]
        if b0 is not None:
            edge = [rectified(e, b0[:, :half]).astype(BF16) for e in edge]
        edge = jnp.dot(jnp.concatenate(edge, axis=1), wm[1], preferred_element_type=F32)
        for par in range(2):
            here = hs[par, r : r + rows, :]
            if b0 is not None:
                here = rectified(here, b0).astype(BF16)
            g = jnp.dot(here, wm[0], preferred_element_type=F32)
            ends = g[:, :half] + edge[:, par * half : (par + 1) * half]
            g = [rectified(ends, b1[:, :half]), rectified(g[:, half:], b1[:, half:])]
            for n in range(rows // per):
                b, q = divmod(r // per - 1 + n, GROUPS)
                for i in range(2):
                    col = (par * GROUPS + q) * wide + i * half
                    gs[b * per : (b + 1) * per, col : col + half] = g[i][n * per : (n + 1) * per].astype(BF16)
    part = blocks // 4
    for b in range(0, blocks, part):
        y = jnp.dot(gs[b * per : (b + part) * per, :], wo[...], preferred_element_type=F32)
        ys[1 + b : 1 + b + part] = y.reshape(part, per, wide)


def patch_kernel(sizes, *refs):
    scalars, (guess, mixtures), refs = refs[:4], refs[4:6], refs[6:]
    lags, order, tallies, pace = refs[45:49]
    given, out = refs[:8], refs[8]
    (gbuf, mbuf, sendx, recvx, sendm, recvm, backs, backr, sende, recve) = refs[9:19]
    (xs, ps, mx, rolled, mf, member, zs, hs, gs, ys) = refs[19:29]
    pre = refs[49]
    ta, tb, held = refs[29:33], refs[33:37], refs[37:45]
    load_sem, ssem, rsem = refs[50:]
    n_shot, n_line, n_tm = sizes
    count = math.prod(sizes)
    axes = [lax.axis_index(a) for a in AXES]
    turns = [[axes[i]] + [lax.rem(axes[i] + d, n) for d in range(1, n)] for i, n in enumerate(sizes)]
    at_shot, at_line, at_tm = axes

    def number(s, l, t):
        return (s * n_line + l) * n_tm + t

    def device(s, l, t):
        return {"shot": s, "line": l, "tm": t}

    me = number(*axes)
    peers = [(s, l, t) for s in turns[0] for l in turns[1] for t in turns[2]][1:]
    shots = n_shot
    n_mix = mixtures.shape[0]
    run = shots // n_mix
    recv_n, tl = guess.shape[1:]
    lc = recv_n // count
    tile = 2 * HALF
    blocks = tl * n_tm // HALF
    each = tl // HALF
    back_kind = 2 + ITERS * n_line

    barrier = pltpu.get_barrier_semaphore()
    for p in peers:
        pl.semaphore_signal(barrier, inc=1, device_id=device(*p), device_id_type=pl.DeviceIdType.MESH)
    pairs = [(guess.at[0], gbuf), (mixtures, mbuf)] + list(zip(given, held)) + list(zip(scalars, refs[45:49]))
    loads = [pltpu.make_async_copy(a, b, load_sem.at[i]) for i, (a, b) in enumerate(pairs)]
    for copy in loads:
        copy.start()

    def link(which, src, dst, to, came):
        return pltpu.make_async_remote_copy(
            src_ref=src,
            dst_ref=dst,
            send_sem=ssem.at[which, number(*to)],
            recv_sem=rsem.at[which, came],
            device_id=device(*to),
            device_id_type=pl.DeviceIdType.MESH,
        )

    row, col = iota((recv_n, recv_n), 0), iota((recv_n, recv_n), 1)
    perm = jnp.where(col == lax.rem(row, lc) * count + row // lc, 1.0, 0.0).astype(BF16)
    loads[0].wait()
    v = jnp.dot(perm, gbuf[...], preferred_element_type=F32)
    for k in range(count):
        part = v[k * lc : (k + 1) * lc]
        sendx[k] = jnp.concatenate([part[:, : tl // 2], part[:, tl // 2 :]], axis=0).astype(BF16)
    pl.semaphore_wait(barrier, count - 1)
    for p in peers[::-1]:
        link(0, sendx.at[number(*p)], recvx.at[me], p, me).start()

    loads[1].wait()
    other = (at_shot, n_line - 1 - at_line, at_tm)
    row, col = iota((2 * lc, recv_n), 0), iota((2 * lc, recv_n), 1)
    wanted = jnp.where(row < lc, me, number(*other))
    pick = jnp.where(col == lax.rem(row, lc) * count + wanted, 1.0, 0.0).astype(BF16)
    picked = [jnp.dot(pick, mbuf[g], preferred_element_type=F32) for g in range(n_mix)]
    sendm[...] = jnp.concatenate([p[lc:] for p in picked], axis=0).astype(BF16)
    link(1, sendm, recvm.at[at_line], other, me).start()
    recvm[at_line] = jnp.concatenate([p[:lc] for p in picked], axis=0).astype(BF16)
    recvx[me] = sendx[me]

    for copy in loads[2:]:
        copy.wait()
    weave(*held[:4], *ta)
    weave(*held[4:], *tb)
    edges = hs.shape[1] - (GROUPS * blocks + 1) * (hs.shape[1] // (GROUPS * blocks + 2))
    hs[:, :edges] = jnp.zeros_like(hs[:, :edges])
    hs[:, hs.shape[1] - edges :] = jnp.zeros_like(hs[:, :edges])
    silent = jnp.full((n_line, 2, edges, pre.shape[3]), -1e30, F32)
    pre[:, :, :edges] = silent
    pre[:, :, pre.shape[2] - edges :] = silent
    for ref in (ys, rolled, mf, xs):
        ref[0] = jnp.zeros_like(ref[0])
        ref[ref.shape[0] - 1] = jnp.zeros_like(ref[0])
    for ref, at in ((rolled, 1), (mf, blocks)):
        ref[at] = jnp.zeros_like(ref[at])
    sec = []
    for rows in ((lc, tile), (count, tile)):
        if rows[0] == lc:
            q = iota(rows, 0) * count + me
        else:
            q = lax.rem(iota(rows, 1), lc) * count + iota(rows, 0)
        edge, at, size = jnp.int32(0), jnp.zeros(rows, jnp.int32), jnp.zeros(rows, jnp.int32)
        for p in range(tallies.shape[0]):
            at = jnp.where(q >= edge, p, at)
            size = jnp.where(q >= edge, tallies[p], size)
            edge = edge + tallies[p]
        sec.append((at, size))
    scale = 1.0 / (sec[0][1] * (shots * tl * n_tm)).astype(F32)
    for k in range(count):
        member[k] = jnp.where(sec[0][0] == sec[1][0][k : k + 1, :], scale, 0.0)

    lane = iota((lc, tile), 1)
    low = lane < HALF
    inner = lax.rem(lane, HALF)

    def unfold(v):
        turned = pltpu.roll(v, HALF, 1)
        return jnp.where(low, v, turned), jnp.where(low, turned, v)

    for p in peers:
        link(0, sendx.at[number(*p)], recvx.at[number(*p)], p, number(*p)).wait_recv()
    for p in range(count):
        s, l, t = p // (n_line * n_tm), p // n_tm % n_line, p % n_tm
        v = recvx[p].astype(F32)
        for j in range(tl // tile):
            h, c = divmod(j * tile, tl // 2)
            two = unfold(v[h * lc : (h + 1) * lc, c : c + tile])
            for n in range(2):
                xs[1 + l, t * each + 2 * j + n, s] = two[n]

    def unfold_mixtures():
        link(1, sendm, recvm.at[n_line - 1 - at_line], other, number(*other)).wait_recv()
        for l in range(n_line):
            v = recvm[l].astype(F32)
            for g in range(n_mix):
                for j in range(blocks // 2):
                    two = unfold(v[g * lc : (g + 1) * lc, j * tile : (j + 1) * tile])
                    for n in range(2):
                        mx[2 * j + n, g * n_line + l] = two[n]

    cube = (shots, lc, tile)
    per = shots * lc
    clow = iota(cube, 2) < HALF
    line_of = iota(cube, 1)
    spot = lax.rem(iota((per, tile), 1), HALF)
    wide_spot = lax.rem(iota((per, 2 * tile), 1), HALF)
    early = spot < HALF // 2
    one = jnp.zeros((1, lc, tile), F32)
    nothing = jnp.zeros((per, 2 * tile), F32)

    def widen(make):
        ahead_of = [nothing, make(0)]
        for b in range(blocks):
            ahead_of.append(make(b + 1) if b + 1 < blocks else nothing)
            before, here, after = ahead_of[b : b + 3]
            zs[0, b * per : (b + 1) * per, :] = jnp.where(wide_spot == HALF - 1, before, here).astype(BF16)
            zs[1, b * per : (b + 1) * per, :] = jnp.where(wide_spot == 0, after, here).astype(BF16)

    def beside(before, here, after):
        both = jnp.where(clow, before, here)
        return jnp.concatenate([both.reshape(per, tile), after.reshape(per, tile)], axis=1)

    def change(b):
        return ys[b + 1, :, :tile] + jnp.where(early, ys[b, :, tile:], ys[b + 2, :, tile:])

    group = []
    for s in range(shots):
        found = jnp.int32(0)
        for k in range(shots):
            found = jnp.where(order[k] == s, k // run, found)
        group.append(found)
    rest = [lax.rem(lags[s], HALF) for s in range(shots)]
    far = [lags[s] // HALF for s in range(shots)]

    def over_lines(it, l):
        def make(b):
            x = xs[1 + l, b]
            before = jnp.where(line_of == lc - 1, xs[l, b], x)
            after = jnp.where(line_of == 0, xs[2 + l, b], x)
            return beside(pltpu.roll(before, 1, 1), x, pltpu.roll(after, lc - 1, 1))

        widen(make)
        biases = [jnp.broadcast_to(ta[3][i : i + 1, :], (lc, 2 * tile)) for i in range(2)]
        enter(zs, hs, ta[0], biases[0], blocks)
        leave(hs, gs, ys, *ta[1:3], biases[1])
        energy = jnp.zeros((lc, tile), F32)
        for b in range(blocks):
            x = (xs[1 + l, b] + change(b).reshape(cube)).astype(BF16).astype(F32)
            ps[l, b] = x
            energy = energy + jnp.sum(x * x, axis=0)
        energy = 0.5 * jnp.sum(energy, axis=1, keepdims=True)
        mine = jnp.sum(jnp.where(lane == iota((lc, tile), 0), energy, 0.0), axis=0, keepdims=True)
        at = it * n_line + l
        sende[at] = mine
        recve[at, me] = mine
        for p in peers[::-1]:
            link(2 + at, sende.at[at], recve.at[at, me], p, me).start()

    def before_shots(l):
        def make(b):
            x = ps[l, b]
            return beside(jnp.concatenate([one, x[: shots - 1]], axis=0), x, jnp.concatenate([x[1:], one], axis=0))

        widen(make)
        prepare(zs, pre.at[l], tb[0], blocks)

    def over_shots(it, l):
        at = it * n_line + l
        for p in peers:
            link(2 + at, sende.at[at], recve.at[at, number(*p)], p, number(*p)).wait_recv()
        total = jnp.zeros((lc, tile), F32)
        for k in range(count):
            total = total + member[k] * recve[at, k]
        mean = jnp.sum(total, axis=1, keepdims=True)
        rms = jnp.broadcast_to(jnp.sqrt(mean + EPSILON), (lc, 2 * tile))
        biases = [rms * tb[3][i : i + 1, :] for i in range(2)]
        leave(pre.at[l], gs, ys, *tb[1:3], biases[1], biases[0])
        for b in range(blocks):
            x = (ps[l, b] + change(b).reshape(cube)).astype(BF16).astype(F32)
            ps[l, b] = x
            for s in range(shots):
                rolled[b + 2, s] = pltpu.roll(x[s], rest[s], 1)
        for g in range(n_mix):
            acc = -mx[:, g * n_line + l]
            for i in range(run):
                s = order[g * run + i]
                lag = lags[s]
                a = 2 - lag // HALF
                near, late = rolled[pl.ds(a, blocks), s], rolled[pl.ds(a - 1, blocks), s]
                acc = acc + jnp.where((inner >= lax.rem(lag, HALF))[None], near, late)
            mf[:blocks, g] = acc
        for s in range(shots):
            m = mf[:, group[s]]
            rolled[: blocks + 2, s] = pltpu.roll(m, lax.rem(tile - rest[s], tile), 2)
        for s in range(shots):
            near, late = rolled[pl.ds(far[s], blocks), s], rolled[pl.ds(far[s] + 1, blocks), s]
            back = jnp.where((inner < HALF - rest[s])[None], near, late)
            xs[1 + l, :, s] = (ps[l, :, s] - pace[it] * back).astype(BF16).astype(F32)
        rolled[:2] = jnp.zeros_like(rolled[:2])

        @pl.when(it == ITERS - 1)
        def _():
            for s in range(n_shot):
                for t in range(n_tm):
                    tiles = []
                    for j in range(tl // tile):
                        b = t * each + 2 * j
                        tiles.append(jnp.where(low, xs[1 + l, b, s], xs[1 + l, b + 1, s]))
                    n = len(tiles) // 2
                    halves = [jnp.concatenate(tiles[:n], axis=1), jnp.concatenate(tiles[n:], axis=1)]
                    backs[number(s, l, t)] = jnp.concatenate(halves, axis=0).astype(BF16)
            own = (at_shot, l, at_tm)
            for s in turns[0]:
                for t in turns[2]:
                    if s is at_shot and t is at_tm:
                        continue
                    link(back_kind, backs.at[number(s, l, t)], backr.at[me], (s, l, t), me).start()

            @pl.when(l != at_line)
            def _():
                link(back_kind, backs.at[number(*own)], backr.at[me], own, me).start()

    def iterate(it, carry):
        def lines(l, carry):
            over_lines(it, l)
            return carry

        def stations(l, carry):
            over_shots(it, l)
            return carry

        def first(l, carry):
            before_shots(l)
            return carry

        lax.fori_loop(0, n_line, lines, 0)
        lax.fori_loop(0, n_line, first, 0)

        @pl.when(it == 0)
        def _():
            unfold_mixtures()

        lax.fori_loop(0, n_line, stations, 0)
        return carry

    lax.fori_loop(0, ITERS, iterate, 0)

    backr[me] = backs[me]
    row, col = iota((recv_n, recv_n), 0), iota((recv_n, recv_n), 1)
    perm = jnp.where(row == lax.rem(col, lc) * count + col // lc, 1.0, 0.0).astype(BF16)
    link(1, sendm, recvm.at[at_line], other, me).wait_send()
    for p in peers:
        link(0, sendx.at[number(*p)], recvx.at[me], p, me).wait_send()
        for at in range(ITERS * n_line):
            link(2 + at, sende.at[at], recve.at[at, me], p, me).wait_send()
    for p in peers:
        link(back_kind, backs.at[number(*p)], backr.at[number(*p)], p, number(*p)).wait_recv()
    v = []
    for k in range(count):
        part = backr[k].astype(F32)
        v.append(jnp.concatenate([part[:lc], part[lc:]], axis=1))
    v = jnp.concatenate(v, axis=0).astype(BF16)
    out[0] = jnp.dot(perm, v, preferred_element_type=F32).astype(BF16)
    for p in peers:
        link(back_kind, backs.at[number(*p)], backr.at[me], p, me).wait_send()


def patch(guess, mixtures, lags, order, tallies, wa, wb, pace, sizes):
    count = math.prod(sizes)
    n_shot, n_line, n_tm = sizes
    recv, tl = guess.shape[1:]
    n_mix, nt = mixtures.shape[0], mixtures.shape[2]
    lc, tile = recv // count, 2 * HALF
    blocks = nt // HALF
    per, feat = n_shot * lc, wa[0].shape[2]
    wide = feat * len(SLOT)
    rows = blocks * per
    weights = [w.transpose(1, 0, 2) if i == 0 else w for part in (wa, wb) for i, w in enumerate(part)]
    v, h = (pl.BlockSpec(memory_space=m) for m in (pltpu.VMEM, pl.ANY))
    slab = pltpu.VMEM((count, 2 * lc, tl // 2), BF16)
    woven = [
        pltpu.VMEM((2 * GROUPS, wide, wide), BF16),
        pltpu.VMEM((2, wide, wide), BF16),
        pltpu.VMEM((2 * GROUPS * wide, wide), BF16),
        pltpu.VMEM((2, wide), F32),
    ]
    kinds = 3 + ITERS * n_line
    return pl.pallas_call(
        functools.partial(patch_kernel, sizes),
        out_shape=pltpu.VMEM(guess.shape, BF16),
        in_specs=[h] * 14,
        out_specs=v,
        scratch_shapes=[
            pltpu.VMEM((recv, tl), BF16),
            pltpu.VMEM(mixtures.shape, BF16),
            slab,
            slab,
            pltpu.VMEM((n_mix * lc, nt), BF16),
            pltpu.VMEM((n_line, n_mix * lc, nt), BF16),
            slab,
            slab,
            pltpu.VMEM((ITERS * n_line, 1, tile), F32),
            pltpu.VMEM((ITERS * n_line, count, 1, tile), F32),
            pltpu.VMEM((n_line + 2, blocks, n_shot, lc, tile), F32),
            pltpu.VMEM((n_line, blocks, n_shot, lc, tile), F32),
            pltpu.VMEM((blocks, n_mix * n_line, lc, tile), F32),
            pltpu.VMEM((blocks + 2, n_shot, lc, tile), F32),
            pltpu.VMEM((blocks + 2, n_mix, lc, tile), F32),
            pltpu.VMEM((count, lc, tile), F32),
            pltpu.VMEM((2, rows, wide), BF16),
            pltpu.VMEM((2, GROUPS * rows + 2 * per, wide), BF16),
            pltpu.VMEM((rows, 2 * GROUPS * wide), BF16),
            pltpu.VMEM((blocks + 2, per, wide), F32),
            *woven,
            *woven,
            *[pltpu.VMEM(w.shape, w.dtype) for w in weights],
            *[pltpu.SMEM(w.shape, w.dtype) for w in (lags, order, tallies, pace)],
            pltpu.VMEM((n_line, 2, GROUPS * rows + 2 * per, wide), F32),
            pltpu.SemaphoreType.DMA((6 + len(weights),)),
            pltpu.SemaphoreType.DMA((kinds, count)),
            pltpu.SemaphoreType.DMA((kinds, count)),
        ],
        compiler_params=pltpu.CompilerParams(vmem_limit_bytes=56 * 2**20, collective_id=1, has_side_effects=True),
    )(lags, order, tallies, pace, guess, mixtures, *weights)


def per_device(guess, mixtures, lags, order, tallies, e1, m1, x1, b1, e2, m2, x2, b2, pace):
    sh, recv, tl = guess.shape
    n_shot, n_line, n_tm = (lax.axis_size(a) for a in AXES)
    whole = RPL % (n_shot * n_line * n_tm) == 0
    where = AXES if whole else AXES[1:]
    parts = math.prod(lax.axis_size(a) for a in where)
    kp, lh = RPL // parts, recv // RPL
    lines, shots, nt = lh * n_line, sh * n_shot, tl * n_tm
    planes, s1 = nt // 2 // C, shots if whole else sh
    r1 = lines * kp
    r2 = r1 if whole else r1 // n_shot
    lanes1, lanes2 = 2 * s1 * r1, 2 * shots * r2
    sources = n_shot if whole else 1
    i32 = functools.partial(jnp.arange, dtype=jnp.int32)
    n_mix, feat = mixtures.shape[0], e1.shape[2]
    square = sh == 1 and kp == 1 and n_line == 2 and shots % n_mix == 0 and feat == HALF
    square = square and lh == C and tl % (4 * HALF) == 0 and n_mix * lh % 16 == 0
    square = square and lines == parts and 2 * (n_mix // n_line) == n_line
    if square:
        sizes = (n_shot, n_line, n_tm)
        return patch(guess, mixtures, lags, order, tallies, (e1, m1, x1, b1), (e2, m2, x2, b2), pace, sizes)

    at_shot = lax.axis_index("shot")
    n_mix, run = mixtures.shape[0], nt // C
    fused = whole and sh == 1 and kp == 1 and C % n_tm == 0 and n_shot * n_tm == C
    x = guess.reshape(sh, lh, parts, kp, tl).transpose(2, 0, 1, 3, 4)
    if fused:
        share = (at_shot * n_tm + lax.axis_index("tm")) * run
        mine = lax.dynamic_slice_in_dim(mixtures, share, run, axis=2).reshape(n_mix, lh, parts, run)
        mine = mine.transpose(2, 1, 0, 3).reshape(parts, lh, n_mix * run)
        x = jnp.concatenate([x.reshape(parts, lh, tl), mine], axis=2)
    x = lax.all_to_all(x, where, split_axis=0, concat_axis=0, tiled=False)
    if not fused:
        x = x.reshape(sources, n_line, n_tm, sh, lh, kp, tl).transpose(0, 3, 1, 4, 5, 2, 6)
        x = x.reshape(s1, r1, C, planes, 2).transpose(3, 2, 4, 0, 1).reshape(planes, C, lanes1)


    def first_k(line):
        block = line * n_tm + lax.axis_index("tm")
        return (at_shot * n_line * n_tm + block if whole else block) * kp

    if not fused:
        grid = mixtures.reshape(n_mix, lh, RPL, nt)
        sent = jnp.stack([lax.dynamic_slice_in_dim(grid, first_k(d), kp, axis=2) for d in range(n_line)])
        m = lax.all_to_all(sent, "line", split_axis=0, concat_axis=0)
        m = m.transpose(1, 0, 2, 3, 4).reshape(n_mix, r1, nt)
        if not whole:
            m = lax.dynamic_slice_in_dim(m, at_shot * r2, r2, axis=1)
        m = m.reshape(n_mix, r2, C, planes, 2).transpose(3, 2, 4, 0, 1).reshape(planes * C, 2 * n_mix * r2)

    np_ = tallies.shape[0]
    here = i32(np_)
    offsets = jnp.sum(jnp.where(here[None, :] < here[:, None], tallies[None, :], 0), axis=1)
    mine = first_k(lax.axis_index("line"))

    def one_hot(r):
        line, k = r // kp, mine + lax.rem(r, kp)
        q = lax.rem(line, lh) * RPL + k
        inside = (offsets[:, None] <= q[None, :]) & (q[None, :] < (offsets + tallies)[:, None])
        block = (line // lh)[None, :] == i32(n_line)[:, None]
        return (block[:, None, :] & inside[None, :, :]).reshape(n_line * np_, r.shape[0]).astype(F32)

    member = jnp.tile(one_hot(i32(r1)), (1, 2 * s1))
    r_own = i32(r2) if whole else at_shot * r2 + i32(r2)
    count = jnp.tile((tallies * (shots * nt)).astype(F32), n_line)
    spread = jnp.tile(one_hot(r_own) / count[:, None], (1, 2 * shots))

    sid = i32(shots)
    place = jnp.sum(jnp.where(order[None, :] == sid[:, None], sid[None, :], 0), axis=1)
    group = place // (shots // n_mix)
    same = (group[:, None] == group[None, :]).astype(BF16)
    chosen = (i32(n_mix)[:, None] == group[None, :]).astype(BF16)
    rest, two = jnp.eye(r2, dtype=BF16), jnp.eye(2, dtype=BF16)
    join = jnp.kron(two, jnp.kron(same, rest))
    take = jnp.kron(two, jnp.kron(chosen, rest))

    n1, n2 = s1 * r1, shots * r2
    a, b = np.arange(n1)[:, None], np.arange(n1)[None, :]
    near1 = np.stack([(a == b + (c - 1) * kp) & (a // r1 == b // r1) for c in range(3)])
    a, b = np.arange(n2)[:, None], np.arange(n2)[None, :]
    near2 = np.stack([a == b + (c - 1) * r2 for c in range(3)])
    wa = prepared(e1, m1, x1, b1, near1)
    wb = prepared(e2, m2, x2, b2, near2)

    rows = planes * C
    tot1, tot2 = pltpu.VMEM((rows, 2 * lanes1), F32), pltpu.VMEM((rows, 2 * lanes2), F32)
    feat = e1.shape[2]
    band = pltpu.VMEM((3 * PACK * feat, PACK * feat), BF16)
    buf = pltpu.VMEM((2, 2 * planes, C, lanes2), F32)
    spass = jax.ShapeDtypeStruct((planes, C, lanes1), BF16)
    part = jax.ShapeDtypeStruct((n_line * np_, 128), F32)
    moved = jax.ShapeDtypeStruct((planes, C, lanes2), BF16)

    def to_stations(y):
        y = y.reshape(rows, 2, sh, n_shot, r2)
        y = lax.all_to_all(y, "shot", split_axis=3, concat_axis=2, tiled=True)
        return y.reshape(planes, C, lanes2)

    def to_shots(y):
        y = y.reshape(rows, 2, shots, 1, r2)
        y = lax.all_to_all(y, "shot", split_axis=2, concat_axis=3, tiled=True)
        return y.reshape(planes, C, lanes1)

    dims = (n_shot, n_line, n_tm)
    cube = pltpu.VMEM((planes, C, lanes1), F32)
    if fused:
        mixed = jax.ShapeDtypeStruct((rows, 2 * n_mix * r2), BF16)
        side = pltpu.VMEM((planes, C, 2 * n_mix * r2), F32)
        sp, energy, m = call(
            functools.partial(entry_kernel, dims),
            (spass, part, mixed),
            (x, *wa, member),
            0,
            [tot1, band, cube, side],
        )
    else:
        sp, energy = call(first_kernel, (spass, part), (x, *wa, member), 0, [tot1, band])
    for it in range(ITERS):
        tot = summed(energy, (n_shot, n_line, n_tm)) if whole else lax.psum(energy, AXES)
        if not whole:
            sp = to_stations(sp)
        ins = (lags, pace, sp, tot, spread, *wb, join, m, take)
        if whole and it < ITERS - 1:
            sp, energy = call(
                functools.partial(both_kernel, it, shots), (spass, part), (*ins, *wa, member), 2, [buf, tot2, band]
            )
            continue
        if fused:
            back = jax.ShapeDtypeStruct((parts, lh, tl), BF16)
            x = call(functools.partial(exit_kernel, it, dims), back, ins, 2, [buf, tot2, band, cube])
            continue
        x = call(functools.partial(station_kernel, it, shots), moved, ins, 2, [buf, tot2, band])
        if not whole:
            x = to_shots(x)
            if it < ITERS - 1:
                sp, energy = call(first_kernel, (spass, part), (x, *wa, member), 0, [tot1, band])

    if not fused:
        x = x.reshape(planes, C, 2, s1, r1).transpose(3, 4, 1, 0, 2)
        x = x.reshape(sources, sh, n_line, lh, kp, n_tm, tl).transpose(0, 2, 5, 1, 3, 4, 6)
    x = lax.all_to_all(x.reshape(parts, sh, lh, kp, tl), where, split_axis=0, concat_axis=0)
    return x.transpose(1, 2, 0, 3, 4).reshape(sh, recv, tl)


def solution(mesh):
    spec = P(("group", "shot"), "line", "tm")
    placed = (spec, P("group", "line", None), P("group"), P("group"), P("group")) + (P(),) * 9
    return jax.shard_map(per_device, mesh=mesh, in_specs=placed, out_specs=spec, check_vma=False)
```

```python
import functools
import math

import jax
import jax.numpy as jnp
import numpy as np
from jax import lax
from jax.experimental import pallas as pl
from jax.experimental.pallas import tpu as pltpu
from jax.sharding import PartitionSpec as P

RPL = 16
ITERS = 2
EPSILON = 1e-05
C = 8
PACK = 4
TAPS = (1, 2, 3, 0)
F32, BF16 = jnp.float32, jnp.bfloat16
AXES = ("shot", "line", "tm")


def ahead(x, k):
    edge = pltpu.roll(x[:k], C - 1, 1)
    edge = jnp.where(lax.broadcasted_iota(jnp.int32, edge.shape, 1) == C - 1, 0.0, edge)
    return edge if k == x.shape[0] else jnp.concatenate([x[k:], edge], axis=0)


def behind(x, k):
    edge = pltpu.roll(x[x.shape[0] - k :], 1, 1)
    edge = jnp.where(lax.broadcasted_iota(jnp.int32, edge.shape, 1) == 0, 0.0, edge)
    return edge if k == x.shape[0] else jnp.concatenate([edge, x[: x.shape[0] - k]], axis=0)


def even_lanes(shape):
    return lax.broadcasted_iota(jnp.int32, shape, len(shape) - 1) < shape[-1] // 2


def net(x, w_in, pick, w_mid, w_out, place, bias, total, band):
    planes, _, lanes = x.shape
    rows = planes * C
    side = jnp.where(even_lanes(x.shape), ahead(x, 1), behind(x, 1))
    z = jnp.concatenate([x, side], axis=2).astype(BF16).reshape(rows, 2 * lanes)
    total[...] = jnp.zeros_like(total)
    wide = w_in.shape[1]
    feat = wide // PACK
    for j in range(3):
        tap = w_mid[j].astype(F32)
        for i in range(PACK):
            row = [tap if p == i else jnp.zeros_like(tap) for p in range(PACK)]
            at = (j * PACK + i) * feat
            band[at : at + feat, :] = jnp.concatenate(row, axis=1).astype(BF16)

    def step(q, carry):
        w_here = jnp.dot(pick[q], w_in[...], preferred_element_type=F32).astype(BF16)
        o_here = jnp.dot(w_out[...], place[q], preferred_element_type=F32).astype(BF16)
        h = jnp.dot(z, w_here, preferred_element_type=F32)
        h = jnp.maximum(h + bias[0:1, :], 0.0)
        cube = h.reshape(planes, C, wide)
        first = ahead(cube[:2], 2).reshape(2 * C, wide).astype(BF16)
        last = behind(cube[planes - 2 :], 2).reshape(2 * C, wide).astype(BF16)
        hb = h.astype(BF16)
        early = jnp.concatenate([last, hb[: rows - 2 * C]], axis=0)
        late = jnp.concatenate([hb[2 * C :], first], axis=0)
        g = jnp.dot(jnp.concatenate([early, hb, late], axis=1), band[...], preferred_element_type=F32)
        g = jnp.maximum(g + bias[1:2, :], 0.0).astype(BF16)
        total[...] += jnp.dot(g, o_here, preferred_element_type=F32)
        return carry

    lax.fori_loop(0, pick.shape[0], step, 0, unroll=2)
    y = total[...].reshape(planes, C, 2 * lanes)
    a, b = y[:, :, :lanes], y[:, :, lanes:]
    return a + jnp.where(even_lanes(b.shape), behind(b, 1), ahead(b, 1))


def shot_step(x, weights, member, out_ref, part_ref, total, band):
    y = (x + net(x, *weights, total, band)).astype(BF16)
    out_ref[...] = y
    y = y.astype(F32)
    energy = jnp.sum(jnp.sum(y * y, axis=0), axis=0, keepdims=True)
    sums = jnp.sum(member[...] * energy, axis=1, keepdims=True)
    part_ref[...] = jnp.broadcast_to(sums, part_ref.shape)


def shifted(buf, lag_ref, shots, forward):
    planes, lanes = buf.shape[1] // 2, buf.shape[3]
    shape = (planes, C, lanes)
    even = even_lanes(shape)
    per = lanes // 2 // shots
    lane_shot = lax.rem(lax.broadcasted_iota(jnp.int32, shape, 2), lanes // 2) // per
    out = jnp.zeros(shape, F32)
    for s in range(shots):
        lag = lag_ref[s]
        half, odd = lag // 2, lax.rem(lag, 2)
        at_even = half if forward else planes - half - odd
        at_odd = half + odd if forward else planes - half
        one = jnp.where(even, buf[odd, pl.ds(at_even, planes)], buf[odd, pl.ds(at_odd, planes)])
        out = jnp.where(lane_shot == s, one, out)
    return out


def station_step(shots, sp, tot_ref, spread, weights, lags, join, mix, take, pace, buf, total, band):
    planes, _, lanes = sp.shape
    rows = planes * C
    mean = jnp.sum(tot_ref[:, 0:1] * spread[...], axis=0, keepdims=True)
    rms = jnp.sqrt(mean + EPSILON).reshape(1, 1, lanes)
    normed = (sp / rms).astype(BF16).astype(F32)
    settled = (sp + rms * net(normed, *weights, total, band)).astype(BF16).astype(F32)

    def fill(x, forward):
        far = ahead(x, planes) if forward else behind(x, planes)
        near_at, far_at = (0, planes) if forward else (planes, 0)
        for v, at in ((x, near_at), (far, far_at)):
            buf[0, at : at + planes] = v
            h = lanes // 2
            buf[1, at : at + planes] = jnp.concatenate([v[:, :, h:], v[:, :, :h]], axis=2)

    fill(settled, False)
    fired = shifted(buf, lags, shots, False).astype(BF16).reshape(rows, lanes)
    misfit = jnp.dot(fired, join[...], preferred_element_type=F32)
    misfit -= jnp.dot(mix[...], take[...], preferred_element_type=F32)
    fill(misfit.reshape(planes, C, lanes), True)
    return (settled - pace * shifted(buf, lags, shots, True)).astype(BF16)


def by_phase(width):
    row = lax.broadcasted_iota(jnp.int32, (width, width), 0)
    col = lax.broadcasted_iota(jnp.int32, (width, width), 1)
    half = width // 2
    return jnp.where(col == 2 * lax.rem(row, half) + row // half, 1.0, 0.0).astype(BF16)


def unfold(read, into, sort):
    planes = into.shape[0]
    for c in range(C):
        v = lax.dot_general(sort, read(c), (((1,), (1,)), ((), ())), preferred_element_type=F32)
        into[:, c, :] = jnp.concatenate([v[:planes], v[planes:]], axis=1)


def entry_kernel(
    dims, x, wi, wp, wm, wo, wq, bi, member, out, part, mix, total, band, cube, side
):
    shots, blocks, halves = dims
    width = 2 * cube.shape[0]
    sort, each = by_phase(width), C // halves

    def traces(c):
        at, t = slice(c % each * width, (c % each + 1) * width), c // each
        rows = [x[(s * blocks + b) * halves + t, :, at].astype(F32) for s in range(shots) for b in range(blocks)]
        return jnp.concatenate(rows, axis=0).astype(BF16)

    tl = each * width

    def records(c):
        s, t = c // halves, c % halves
        rows = [
            x[(s * blocks + b) * halves + t, :, tl + g * width : tl + (g + 1) * width].astype(F32)
            for g in range((x.shape[2] - tl) // width)
            for b in range(blocks)
        ]
        return jnp.concatenate(rows, axis=0).astype(BF16)

    unfold(records, side, sort)
    mix[...] = side[...].astype(BF16).reshape(mix.shape)
    unfold(traces, cube, sort)
    shot_step(cube[...], (wi, wp, wm, wo, wq, bi), member, out, part, total, band)


def exit_kernel(
    it, dims, lags, pace, sp, tot, spread, wi, wp, wm, wo, wq, bi, join, mix, take, out, buf, total, band, cube
):
    shots, blocks, halves = dims
    width = 2 * cube.shape[0]
    sort, each = by_phase(width), C // halves
    x = station_step(
        shots, sp[...].astype(F32), tot, spread, (wi, wp, wm, wo, wq, bi), lags, join, mix, take, pace[it], buf, total, band
    )
    cube[...] = x.astype(F32)
    n, lh = cube.shape[2] // 2, out.shape[1]
    for c in range(C):
        v = cube[:, c, :]
        v = jnp.concatenate([v[:, :n], v[:, n:]], axis=0).T.astype(BF16)
        v = jnp.dot(v, sort, preferred_element_type=F32)
        at, t = slice(c % each * width, (c % each + 1) * width), c // each
        for j in range(shots * blocks):
            out[j * halves + t, :, at] = v[j * lh : (j + 1) * lh].astype(BF16)


def first_kernel(x, wi, wp, wm, wo, wq, bi, member, out, part, total, band):
    shot_step(x[...].astype(F32), (wi, wp, wm, wo, wq, bi), member, out, part, total, band)


def station_kernel(it, shots, lags, pace, sp, tot, spread, wi, wp, wm, wo, wq, bi, join, mix, take, out, buf, total, band):
    out[...] = station_step(
        shots, sp[...].astype(F32), tot, spread, (wi, wp, wm, wo, wq, bi), lags, join, mix, take, pace[it], buf, total, band
    )


def both_kernel(
    it, shots, lags, pace, sp, tot, spread, wi, wp, wm, wo, wq, bi, join, mix, take, vi, vp, vm, vo, vq, ci, member, out, part, buf, total, band
):
    x = station_step(
        shots, sp[...].astype(F32), tot, spread, (wi, wp, wm, wo, wq, bi), lags, join, mix, take, pace[it], buf, total, band
    )
    shot_step(x.astype(F32), (vi, vp, vm, vo, vq, ci), member, out, part, total, band)


def call(body, outs, ins, smem, scratch):
    v, s = pl.BlockSpec(memory_space=pltpu.VMEM), pl.BlockSpec(memory_space=pltpu.SMEM)
    return pl.pallas_call(
        body,
        out_shape=outs,
        in_specs=[s] * smem + [v] * (len(ins) - smem),
        out_specs=jax.tree.map(lambda _: v, outs),
        scratch_shapes=scratch,
        compiler_params=pltpu.CompilerParams(vmem_limit_bytes=48 * 2**20),
    )(*ins)


def prepared(w_in, w_mid, w_out, bias, near):
    n, feat = near.shape[1], w_in.shape[2]
    tiles = n // PACK
    cols = near.reshape(3, n, tiles, PACK).transpose(2, 1, 0, 3)
    pick = np.einsum("jk,tnci->tjnkci", np.eye(4)[list(TAPS)], cols).reshape(tiles, 4 * n, 12 * PACK)
    place = np.einsum("kj,tin->tjikn", np.eye(4)[list(TAPS)], np.eye(n).reshape(tiles, PACK, n)).reshape(tiles, 4 * PACK, 4 * n)
    w1 = w_in.reshape(12, 1, 1, feat)
    eye = jnp.eye(PACK, dtype=BF16)
    rows = (w1 * eye[None, :, :, None]).reshape(12 * PACK, PACK * feat)
    w2 = w_out.T.reshape(1, feat, 4, 1)
    ends = (w2 * eye[:, None, None, :]).reshape(PACK * feat, 4 * PACK)
    return rows, jnp.asarray(pick, BF16), w_mid, ends, jnp.asarray(place, BF16), jnp.tile(bias, (1, PACK))


def exchange_kernel(sizes, x, out, slots, send, recv):
    count = math.prod(sizes)
    me = (lax.axis_index("shot") * sizes[1] + lax.axis_index("line")) * sizes[2] + lax.axis_index("tm")

    def peer(off):
        at = lax.rem(me + off, count)
        return {
            "shot": at // (sizes[1] * sizes[2]),
            "line": lax.rem(at // sizes[2], sizes[1]),
            "tm": lax.rem(at, sizes[2]),
        }

    barrier = pltpu.get_barrier_semaphore()
    for off in range(1, count):
        pl.semaphore_signal(barrier, inc=1, device_id=peer(off), device_id_type=pl.DeviceIdType.MESH)
    pl.semaphore_wait(barrier, count - 1)
    copies = []
    for off in range(1, count):
        copy = pltpu.make_async_remote_copy(
            src_ref=x,
            dst_ref=slots.at[off],
            send_sem=send.at[off],
            recv_sem=recv.at[off],
            device_id=peer(off),
            device_id_type=pl.DeviceIdType.MESH,
        )
        copy.start()
        copies.append(copy)
    total = x[...]
    for off, copy in enumerate(copies, 1):
        copy.wait()
        total += slots[off]
    out[...] = total


def summed(x, sizes):
    count, v = math.prod(sizes), pl.BlockSpec(memory_space=pltpu.VMEM)
    return pl.pallas_call(
        functools.partial(exchange_kernel, sizes),
        out_shape=jax.ShapeDtypeStruct(x.shape, x.dtype),
        in_specs=[v],
        out_specs=v,
        scratch_shapes=[
            pltpu.VMEM((count, *x.shape), x.dtype),
            pltpu.SemaphoreType.DMA((count,)),
            pltpu.SemaphoreType.DMA((count,)),
        ],
        compiler_params=pltpu.CompilerParams(collective_id=0, has_side_effects=True),
    )(x)


SLOT = (0, 3, 1, 2)
HALF = 64
GROUPS = 4


def iota(shape, dim):
    return lax.broadcasted_iota(jnp.int32, shape, dim)


def weave(w_in, w_mid, w_out, bias, we, wm, wo, bi):
    feat = w_in.shape[2]
    wide = feat * len(SLOT)
    row, lane = iota((wide, wide), 0), iota((wide, wide), 1)
    at, ch = lax.rem(row, HALF), row // HALF
    slot = lane // feat
    pos = jnp.where(slot == 1, 3, jnp.where(slot == 0, 0, slot - 1))
    taps = w_in[...].astype(F32)
    for par in range(2):
        turned = lax.rem(at + (1 if par == 0 else HALF - 1), HALF)
        tap = lax.rem(turned, 4)
        base = jnp.zeros((wide, wide), F32)
        for c in range(3):
            for t in range(4):
                line = jnp.concatenate([taps[c, t : t + 1, :]] * len(SLOT), axis=1)
                base = jnp.where((ch == c) & (tap == t), line, base)
        for g in range(GROUPS):
            we[par * GROUPS + g] = jnp.where(turned // 4 == 4 * g + pos, base, 0.0).astype(BF16)
    zero = jnp.zeros((feat, feat), F32)
    mid = [w_mid[j].astype(F32) for j in range(3)]

    def block(came, goes):
        j = came - goes + 1
        return mid[j] if 0 <= j < 3 else zero

    for n, came in enumerate(SLOT):
        blocks = [block(came, goes) for goes in SLOT]
        wm[0, n * feat : (n + 1) * feat, :] = jnp.concatenate(blocks, axis=1).astype(BF16)
    for n in range(4):
        blocks = [zero] * 4
        blocks[n ^ 1] = mid[2 if n % 2 == 0 else 0]
        wm[1, n * feat : (n + 1) * feat, :] = jnp.concatenate(blocks, axis=1).astype(BF16)

    def sample(shape):
        col = iota(shape, 1)
        m = lax.rem(col, HALF)
        edge = jnp.where(m == HALF - 1, -1, jnp.where(m == 0, HALF, -4 * HALF))
        return jnp.where(col >= 2 * HALF, edge, m)

    near, far = sample((4, wide)), sample((feat, wide))
    for par in range(2):
        pick = jnp.where(lax.rem(near - 2 * par + 1 + 8 * HALF, 4) == iota((4, wide), 0), 1.0, 0.0).astype(BF16)
        base = lax.dot_general(w_out[...], pick, (((0,), (0,)), ((), ())), preferred_element_type=F32)
        for g in range(GROUPS):
            for n, i in enumerate(SLOT):
                d = far - 4 * (4 * g + i) - 2 * par + 1
                at = ((par * GROUPS + g) * len(SLOT) + n) * feat
                wo[at : at + feat, :] = jnp.where((d >= 0) & (d < 4), base, 0.0).astype(BF16)
    bi[...] = jnp.concatenate([bias[...]] * len(SLOT), axis=1)


def rectified(h, bias):
    cubes = h.reshape(h.shape[0] // bias.shape[0], bias.shape[0], h.shape[1])
    return jnp.maximum(cubes + bias[None], 0.0).reshape(h.shape)


def enter(zs, hs, we, b0, blocks):
    per = zs.shape[1] // blocks
    for par in range(2):
        for g in range(GROUPS):
            h = jnp.dot(zs[par], we[par * GROUPS + g], preferred_element_type=F32)
            h = rectified(h, b0).astype(BF16)
            for b in range(blocks):
                at = per + (b * GROUPS + g) * per
                hs[par, at : at + per, :] = h[b * per : (b + 1) * per]


def prepare(zs, pre, we, blocks):
    per = zs.shape[1] // blocks
    for par in range(2):
        for g in range(GROUPS):
            h = jnp.dot(zs[par], we[par * GROUPS + g], preferred_element_type=F32)
            for b in range(blocks):
                at = per + (b * GROUPS + g) * per
                pre[par, at : at + per, :] = h[b * per : (b + 1) * per]


def leave(hs, gs, ys, wm, wo, b1, b0=None):
    rows, wide = gs.shape[0], hs.shape[2]
    blocks = ys.shape[0] - 2
    per, half = rows // blocks, wide // 2
    low = iota((2 * rows, half), 1) < half // 2
    take = 2 * rows
    for r in range(per, per + GROUPS * rows, take):
        edge = [jnp.where(low, hs[par, r + per : r + per + take, :half], hs[par, r - per : r - per + take, :half]) for par in range(2)]
        if b0 is not None:
            edge = [rectified(e, b0[:, :half]).astype(BF16) for e in edge]
        edge = jnp.dot(jnp.concatenate(edge, axis=1), wm[1], preferred_element_type=F32)
        for par in range(2):
            here = hs[par, r : r + take, :]
            if b0 is not None:
                here = rectified(here, b0).astype(BF16)
            g = jnp.dot(here, wm[0], preferred_element_type=F32)
            ends = g[:, :half] + edge[:, par * half : (par + 1) * half]
            g = [rectified(ends, b1[:, :half]), rectified(g[:, half:], b1[:, half:])]
            for n in range(take // per):
                b, q = divmod(r // per - 1 + n, GROUPS)
                for i in range(2):
                    col = (par * GROUPS + q) * wide + i * half
                    gs[b * per : (b + 1) * per, col : col + half] = g[i][n * per : (n + 1) * per].astype(BF16)
    part = blocks // 4
    for b in range(0, blocks, part):
        y = jnp.dot(gs[b * per : (b + part) * per, :], wo[...], preferred_element_type=F32)
        ys[1 + b : 1 + b + part] = y.reshape(part, per, wide)


def patch_kernel(sizes, *refs):
    scalars, (guess, mixtures), refs = refs[:4], refs[4:6], refs[6:]
    lags, order, tallies, pace = refs[45:49]
    given, out = refs[:8], refs[8]
    (gbuf, mbuf, sendx, recvx, sendm, recvm, backs, backr, sende, recve) = refs[9:19]
    (xs, ps, mx, rolled, mf, member, zs, hs, gs, ys) = refs[19:29]
    pre = refs[49]
    ta, tb, held = refs[29:33], refs[33:37], refs[37:45]
    load_sem, ssem, rsem = refs[50:]
    n_shot, n_line, n_tm = sizes
    count = math.prod(sizes)
    axes = [lax.axis_index(a) for a in AXES]
    turns = [[axes[i]] + [lax.rem(axes[i] + d, n) for d in range(1, n)] for i, n in enumerate(sizes)]
    at_shot, at_line, at_tm = axes

    def number(s, l, t):
        return (s * n_line + l) * n_tm + t

    def device(s, l, t):
        return {"shot": s, "line": l, "tm": t}

    me = number(*axes)
    peers = [(s, l, t) for s in turns[0] for l in turns[1] for t in turns[2]][1:]
    shots = n_shot
    n_mix = mixtures.shape[0]
    run = shots // n_mix
    recv_n, tl = guess.shape[1:]
    lc = recv_n // count
    tile = 2 * HALF
    blocks = tl * n_tm // HALF
    each = tl // HALF
    back_kind = 2 + ITERS * n_line

    barrier = pltpu.get_barrier_semaphore()
    for p in peers:
        pl.semaphore_signal(barrier, inc=1, device_id=device(*p), device_id_type=pl.DeviceIdType.MESH)
    pairs = [(guess.at[0], gbuf), (mixtures, mbuf)] + list(zip(given, held)) + list(zip(scalars, refs[45:49]))
    loads = [pltpu.make_async_copy(a, b, load_sem.at[i]) for i, (a, b) in enumerate(pairs)]
    for copy in loads:
        copy.start()

    def link(which, src, dst, to, came):
        return pltpu.make_async_remote_copy(
            src_ref=src,
            dst_ref=dst,
            send_sem=ssem.at[which, number(*to)],
            recv_sem=rsem.at[which, came],
            device_id=device(*to),
            device_id_type=pl.DeviceIdType.MESH,
        )

    row, col = iota((recv_n, recv_n), 0), iota((recv_n, recv_n), 1)
    perm = jnp.where(col == lax.rem(row, lc) * count + row // lc, 1.0, 0.0).astype(BF16)
    loads[0].wait()
    v = jnp.dot(perm, gbuf[...], preferred_element_type=F32)
    for k in range(count):
        part = v[k * lc : (k + 1) * lc]
        sendx[k] = jnp.concatenate([part[:, : tl // 2], part[:, tl // 2 :]], axis=0).astype(BF16)
    pl.semaphore_wait(barrier, count - 1)
    for p in peers[::-1]:
        link(0, sendx.at[number(*p)], recvx.at[me], p, me).start()

    loads[1].wait()
    other = (at_shot, n_line - 1 - at_line, at_tm)
    row, col = iota((2 * lc, recv_n), 0), iota((2 * lc, recv_n), 1)
    wanted = jnp.where(row < lc, me, number(*other))
    pick = jnp.where(col == lax.rem(row, lc) * count + wanted, 1.0, 0.0).astype(BF16)
    picked = [jnp.dot(pick, mbuf[g], preferred_element_type=F32) for g in range(n_mix)]
    sendm[...] = jnp.concatenate([p[lc:] for p in picked], axis=0).astype(BF16)
    link(1, sendm, recvm.at[at_line], other, me).start()
    recvm[at_line] = jnp.concatenate([p[:lc] for p in picked], axis=0).astype(BF16)
    recvx[me] = sendx[me]

    for copy in loads[2:]:
        copy.wait()
    weave(*held[:4], *ta)
    weave(*held[4:], *tb)
    edges = hs.shape[1] - (GROUPS * blocks + 1) * (hs.shape[1] // (GROUPS * blocks + 2))
    hs[:, :edges] = jnp.zeros_like(hs[:, :edges])
    hs[:, hs.shape[1] - edges :] = jnp.zeros_like(hs[:, :edges])
    silent = jnp.full((n_line, 2, edges, pre.shape[3]), -1e30, F32)
    pre[:, :, :edges] = silent
    pre[:, :, pre.shape[2] - edges :] = silent
    for ref in (ys, rolled, mf, xs):
        ref[0] = jnp.zeros_like(ref[0])
        ref[ref.shape[0] - 1] = jnp.zeros_like(ref[0])
    for ref, at in ((rolled, 1), (mf, blocks)):
        ref[at] = jnp.zeros_like(ref[at])
    sec = []
    for rows in ((lc, tile), (count, tile)):
        if rows[0] == lc:
            q = iota(rows, 0) * count + me
        else:
            q = lax.rem(iota(rows, 1), lc) * count + iota(rows, 0)
        edge, at, size = jnp.int32(0), jnp.zeros(rows, jnp.int32), jnp.zeros(rows, jnp.int32)
        for p in range(tallies.shape[0]):
            at = jnp.where(q >= edge, p, at)
            size = jnp.where(q >= edge, tallies[p], size)
            edge = edge + tallies[p]
        sec.append((at, size))
    scale = 1.0 / (sec[0][1] * (shots * tl * n_tm)).astype(F32)
    for k in range(count):
        member[k] = jnp.where(sec[0][0] == sec[1][0][k : k + 1, :], scale, 0.0)

    lane = iota((lc, tile), 1)
    low = lane < HALF
    inner = lax.rem(lane, HALF)

    def unfold(v):
        turned = pltpu.roll(v, HALF, 1)
        return jnp.where(low, v, turned), jnp.where(low, turned, v)

    for p in peers:
        link(0, sendx.at[number(*p)], recvx.at[number(*p)], p, number(*p)).wait_recv()
    for p in range(count):
        s, l, t = p // (n_line * n_tm), p // n_tm % n_line, p % n_tm
        v = recvx[p].astype(F32)
        for j in range(tl // tile):
            h, c = divmod(j * tile, tl // 2)
            two = unfold(v[h * lc : (h + 1) * lc, c : c + tile])
            for n in range(2):
                xs[1 + l, t * each + 2 * j + n, s] = two[n]

    def unfold_mixtures():
        link(1, sendm, recvm.at[n_line - 1 - at_line], other, number(*other)).wait_recv()
        for l in range(n_line):
            v = recvm[l].astype(F32)
            for g in range(n_mix):
                for j in range(blocks // 2):
                    two = unfold(v[g * lc : (g + 1) * lc, j * tile : (j + 1) * tile])
                    for n in range(2):
                        mx[2 * j + n, g * n_line + l] = two[n]

    cube = (shots, lc, tile)
    per = shots * lc
    clow = iota(cube, 2) < HALF
    line_of = iota(cube, 1)
    spot = lax.rem(iota((per, tile), 1), HALF)
    wide_spot = lax.rem(iota((per, 2 * tile), 1), HALF)
    early = spot < HALF // 2
    one = jnp.zeros((1, lc, tile), F32)
    nothing = jnp.zeros((per, 2 * tile), F32)

    def widen(make):
        ahead_of = [nothing, make(0)]
        for b in range(blocks):
            ahead_of.append(make(b + 1) if b + 1 < blocks else nothing)
            before, here, after = ahead_of[b : b + 3]
            zs[0, b * per : (b + 1) * per, :] = jnp.where(wide_spot == HALF - 1, before, here).astype(BF16)
            zs[1, b * per : (b + 1) * per, :] = jnp.where(wide_spot == 0, after, here).astype(BF16)

    def beside(before, here, after):
        both = jnp.where(clow, before, here)
        return jnp.concatenate([both.reshape(per, tile), after.reshape(per, tile)], axis=1)

    def change(b):
        return ys[b + 1, :, :tile] + jnp.where(early, ys[b, :, tile:], ys[b + 2, :, tile:])

    group = []
    for s in range(shots):
        found = jnp.int32(0)
        for k in range(shots):
            found = jnp.where(order[k] == s, k // run, found)
        group.append(found)
    rest = [lax.rem(lags[s], HALF) for s in range(shots)]
    far = [lags[s] // HALF for s in range(shots)]

    def over_lines(it, l):
        def make(b):
            x = xs[1 + l, b]
            before = jnp.where(line_of == lc - 1, xs[l, b], x)
            after = jnp.where(line_of == 0, xs[2 + l, b], x)
            return beside(pltpu.roll(before, 1, 1), x, pltpu.roll(after, lc - 1, 1))

        widen(make)
        biases = [jnp.broadcast_to(ta[3][i : i + 1, :], (lc, 2 * tile)) for i in range(2)]
        enter(zs, hs, ta[0], biases[0], blocks)
        leave(hs, gs, ys, *ta[1:3], biases[1])
        energy = jnp.zeros((lc, tile), F32)
        for b in range(blocks):
            x = (xs[1 + l, b] + change(b).reshape(cube)).astype(BF16).astype(F32)
            ps[l, b] = x
            energy = energy + jnp.sum(x * x, axis=0)
        energy = 0.5 * jnp.sum(energy, axis=1, keepdims=True)
        mine = jnp.sum(jnp.where(lane == iota((lc, tile), 0), energy, 0.0), axis=0, keepdims=True)
        at = it * n_line + l
        sende[at] = mine
        recve[at, me] = mine
        for p in peers[::-1]:
            link(2 + at, sende.at[at], recve.at[at, me], p, me).start()

    def before_shots(l):
        def make(b):
            x = ps[l, b]
            return beside(jnp.concatenate([one, x[: shots - 1]], axis=0), x, jnp.concatenate([x[1:], one], axis=0))

        widen(make)
        prepare(zs, pre.at[l], tb[0], blocks)

    def over_shots(it, l):
        at = it * n_line + l
        for p in peers:
            link(2 + at, sende.at[at], recve.at[at, number(*p)], p, number(*p)).wait_recv()
        total = jnp.zeros((lc, tile), F32)
        for k in range(count):
            total = total + member[k] * recve[at, k]
        mean = jnp.sum(total, axis=1, keepdims=True)
        rms = jnp.broadcast_to(jnp.sqrt(mean + EPSILON), (lc, 2 * tile))
        biases = [rms * tb[3][i : i + 1, :] for i in range(2)]
        leave(pre.at[l], gs, ys, *tb[1:3], biases[1], biases[0])
        for b in range(blocks):
            x = (ps[l, b] + change(b).reshape(cube)).astype(BF16).astype(F32)
            ps[l, b] = x
            for s in range(shots):
                rolled[b + 2, s] = pltpu.roll(x[s], rest[s], 1)
        for g in range(n_mix):
            acc = -mx[:, g * n_line + l]
            for i in range(run):
                s = order[g * run + i]
                lag = lags[s]
                a = 2 - lag // HALF
                near, late = rolled[pl.ds(a, blocks), s], rolled[pl.ds(a - 1, blocks), s]
                acc = acc + jnp.where((inner >= lax.rem(lag, HALF))[None], near, late)
            mf[:blocks, g] = acc
        for s in range(shots):
            m = mf[:, group[s]]
            rolled[: blocks + 2, s] = pltpu.roll(m, lax.rem(tile - rest[s], tile), 2)
        for s in range(shots):
            near, late = rolled[pl.ds(far[s], blocks), s], rolled[pl.ds(far[s] + 1, blocks), s]
            back = jnp.where((inner < HALF - rest[s])[None], near, late)
            xs[1 + l, :, s] = (ps[l, :, s] - pace[it] * back).astype(BF16).astype(F32)
        rolled[:2] = jnp.zeros_like(rolled[:2])

        @pl.when(it == ITERS - 1)
        def _():
            for s in range(n_shot):
                for t in range(n_tm):
                    tiles = []
                    for j in range(tl // tile):
                        b = t * each + 2 * j
                        tiles.append(jnp.where(low, xs[1 + l, b, s], xs[1 + l, b + 1, s]))
                    n = len(tiles) // 2
                    halves = [jnp.concatenate(tiles[:n], axis=1), jnp.concatenate(tiles[n:], axis=1)]
                    backs[number(s, l, t)] = jnp.concatenate(halves, axis=0).astype(BF16)
            own = (at_shot, l, at_tm)
            for s in turns[0][::-1]:
                for t in turns[2][::-1]:
                    if s is at_shot and t is at_tm:
                        continue
                    link(back_kind, backs.at[number(s, l, t)], backr.at[me], (s, l, t), me).start()

            @pl.when(l != at_line)
            def _():
                link(back_kind, backs.at[number(*own)], backr.at[me], own, me).start()

    def iterate(it, carry):
        def lines(l, carry):
            over_lines(it, l)
            return carry

        def stations(l, carry):
            over_shots(it, l)
            return carry

        def first(l, carry):
            before_shots(l)
            return carry

        lax.fori_loop(0, n_line, lines, 0)
        lax.fori_loop(0, n_line, first, 0)

        @pl.when(it == 0)
        def _():
            unfold_mixtures()

        lax.fori_loop(0, n_line, stations, 0)
        return carry

    lax.fori_loop(0, ITERS, iterate, 0)

    backr[me] = backs[me]
    row, col = iota((recv_n, recv_n), 0), iota((recv_n, recv_n), 1)
    perm = jnp.where(row == lax.rem(col, lc) * count + col // lc, 1.0, 0.0).astype(BF16)
    link(1, sendm, recvm.at[at_line], other, me).wait_send()
    for p in peers:
        link(0, sendx.at[number(*p)], recvx.at[me], p, me).wait_send()
        for at in range(ITERS * n_line):
            link(2 + at, sende.at[at], recve.at[at, me], p, me).wait_send()
    for p in peers:
        link(back_kind, backs.at[number(*p)], backr.at[number(*p)], p, number(*p)).wait_recv()
    v = []
    for k in range(count):
        part = backr[k].astype(F32)
        v.append(jnp.concatenate([part[:lc], part[lc:]], axis=1))
    v = jnp.concatenate(v, axis=0).astype(BF16)
    out[0] = jnp.dot(perm, v, preferred_element_type=F32).astype(BF16)
    for p in peers:
        link(back_kind, backs.at[number(*p)], backr.at[me], p, me).wait_send()


def patch(guess, mixtures, lags, order, tallies, wa, wb, pace, sizes):
    count = math.prod(sizes)
    n_shot, n_line, n_tm = sizes
    recv, tl = guess.shape[1:]
    n_mix, nt = mixtures.shape[0], mixtures.shape[2]
    lc, tile = recv // count, 2 * HALF
    blocks = nt // HALF
    per, feat = n_shot * lc, wa[0].shape[2]
    wide = feat * len(SLOT)
    rows = blocks * per
    weights = [w.transpose(1, 0, 2) if i == 0 else w for part in (wa, wb) for i, w in enumerate(part)]
    v, h = (pl.BlockSpec(memory_space=m) for m in (pltpu.VMEM, pl.ANY))
    slab = pltpu.VMEM((count, 2 * lc, tl // 2), BF16)
    woven = [
        pltpu.VMEM((2 * GROUPS, wide, wide), BF16),
        pltpu.VMEM((2, wide, wide), BF16),
        pltpu.VMEM((2 * GROUPS * wide, wide), BF16),
        pltpu.VMEM((2, wide), F32),
    ]
    kinds = 3 + ITERS * n_line
    return pl.pallas_call(
        functools.partial(patch_kernel, sizes),
        out_shape=pltpu.VMEM(guess.shape, BF16),
        in_specs=[h] * 14,
        out_specs=v,
        scratch_shapes=[
            pltpu.VMEM((recv, tl), BF16),
            pltpu.VMEM(mixtures.shape, BF16),
            slab,
            slab,
            pltpu.VMEM((n_mix * lc, nt), BF16),
            pltpu.VMEM((n_line, n_mix * lc, nt), BF16),
            slab,
            slab,
            pltpu.VMEM((ITERS * n_line, 1, tile), F32),
            pltpu.VMEM((ITERS * n_line, count, 1, tile), F32),
            pltpu.VMEM((n_line + 2, blocks, n_shot, lc, tile), F32),
            pltpu.VMEM((n_line, blocks, n_shot, lc, tile), F32),
            pltpu.VMEM((blocks, n_mix * n_line, lc, tile), F32),
            pltpu.VMEM((blocks + 2, n_shot, lc, tile), F32),
            pltpu.VMEM((blocks + 2, n_mix, lc, tile), F32),
            pltpu.VMEM((count, lc, tile), F32),
            pltpu.VMEM((2, rows, wide), BF16),
            pltpu.VMEM((2, GROUPS * rows + 2 * per, wide), BF16),
            pltpu.VMEM((rows, 2 * GROUPS * wide), BF16),
            pltpu.VMEM((blocks + 2, per, wide), F32),
            *woven,
            *woven,
            *[pltpu.VMEM(w.shape, w.dtype) for w in weights],
            *[pltpu.SMEM(w.shape, w.dtype) for w in (lags, order, tallies, pace)],
            pltpu.VMEM((n_line, 2, GROUPS * rows + 2 * per, wide), F32),
            pltpu.SemaphoreType.DMA((6 + len(weights),)),
            pltpu.SemaphoreType.DMA((kinds, count)),
            pltpu.SemaphoreType.DMA((kinds, count)),
        ],
        compiler_params=pltpu.CompilerParams(vmem_limit_bytes=56 * 2**20, collective_id=1, has_side_effects=True),
    )(lags, order, tallies, pace, guess, mixtures, *weights)


def per_device(guess, mixtures, lags, order, tallies, e1, m1, x1, b1, e2, m2, x2, b2, pace):
    sh, recv, tl = guess.shape
    n_shot, n_line, n_tm = (lax.axis_size(a) for a in AXES)
    whole = RPL % (n_shot * n_line * n_tm) == 0
    where = AXES if whole else AXES[1:]
    parts = math.prod(lax.axis_size(a) for a in where)
    kp, lh = RPL // parts, recv // RPL
    lines, shots, nt = lh * n_line, sh * n_shot, tl * n_tm
    planes, s1 = nt // 2 // C, shots if whole else sh
    r1 = lines * kp
    r2 = r1 if whole else r1 // n_shot
    lanes1, lanes2 = 2 * s1 * r1, 2 * shots * r2
    sources = n_shot if whole else 1
    i32 = functools.partial(jnp.arange, dtype=jnp.int32)
    n_mix, feat = mixtures.shape[0], e1.shape[2]
    square = sh == 1 and kp == 1 and n_line == 2 and shots % n_mix == 0 and feat == HALF
    square = square and lh == C and tl % (4 * HALF) == 0 and n_mix * lh % 16 == 0
    square = square and lines == parts and 2 * (n_mix // n_line) == n_line
    if square:
        sizes = (n_shot, n_line, n_tm)
        return patch(guess, mixtures, lags, order, tallies, (e1, m1, x1, b1), (e2, m2, x2, b2), pace, sizes)

    at_shot = lax.axis_index("shot")
    n_mix, run = mixtures.shape[0], nt // C
    fused = whole and sh == 1 and kp == 1 and C % n_tm == 0 and n_shot * n_tm == C
    x = guess.reshape(sh, lh, parts, kp, tl).transpose(2, 0, 1, 3, 4)
    if fused:
        share = (at_shot * n_tm + lax.axis_index("tm")) * run
        mine = lax.dynamic_slice_in_dim(mixtures, share, run, axis=2).reshape(n_mix, lh, parts, run)
        mine = mine.transpose(2, 1, 0, 3).reshape(parts, lh, n_mix * run)
        x = jnp.concatenate([x.reshape(parts, lh, tl), mine], axis=2)
    x = lax.all_to_all(x, where, split_axis=0, concat_axis=0, tiled=False)
    if not fused:
        x = x.reshape(sources, n_line, n_tm, sh, lh, kp, tl).transpose(0, 3, 1, 4, 5, 2, 6)
        x = x.reshape(s1, r1, C, planes, 2).transpose(3, 2, 4, 0, 1).reshape(planes, C, lanes1)


    def first_k(line):
        block = line * n_tm + lax.axis_index("tm")
        return (at_shot * n_line * n_tm + block if whole else block) * kp

    if not fused:
        grid = mixtures.reshape(n_mix, lh, RPL, nt)
        sent = jnp.stack([lax.dynamic_slice_in_dim(grid, first_k(d), kp, axis=2) for d in range(n_line)])
        m = lax.all_to_all(sent, "line", split_axis=0, concat_axis=0)
        m = m.transpose(1, 0, 2, 3, 4).reshape(n_mix, r1, nt)
        if not whole:
            m = lax.dynamic_slice_in_dim(m, at_shot * r2, r2, axis=1)
        m = m.reshape(n_mix, r2, C, planes, 2).transpose(3, 2, 4, 0, 1).reshape(planes * C, 2 * n_mix * r2)

    np_ = tallies.shape[0]
    here = i32(np_)
    offsets = jnp.sum(jnp.where(here[None, :] < here[:, None], tallies[None, :], 0), axis=1)
    mine = first_k(lax.axis_index("line"))

    def one_hot(r):
        line, k = r // kp, mine + lax.rem(r, kp)
        q = lax.rem(line, lh) * RPL + k
        inside = (offsets[:, None] <= q[None, :]) & (q[None, :] < (offsets + tallies)[:, None])
        block = (line // lh)[None, :] == i32(n_line)[:, None]
        return (block[:, None, :] & inside[None, :, :]).reshape(n_line * np_, r.shape[0]).astype(F32)

    member = jnp.tile(one_hot(i32(r1)), (1, 2 * s1))
    r_own = i32(r2) if whole else at_shot * r2 + i32(r2)
    count = jnp.tile((tallies * (shots * nt)).astype(F32), n_line)
    spread = jnp.tile(one_hot(r_own) / count[:, None], (1, 2 * shots))

    sid = i32(shots)
    place = jnp.sum(jnp.where(order[None, :] == sid[:, None], sid[None, :], 0), axis=1)
    group = place // (shots // n_mix)
    same = (group[:, None] == group[None, :]).astype(BF16)
    chosen = (i32(n_mix)[:, None] == group[None, :]).astype(BF16)
    rest, two = jnp.eye(r2, dtype=BF16), jnp.eye(2, dtype=BF16)
    join = jnp.kron(two, jnp.kron(same, rest))
    take = jnp.kron(two, jnp.kron(chosen, rest))

    n1, n2 = s1 * r1, shots * r2
    a, b = np.arange(n1)[:, None], np.arange(n1)[None, :]
    near1 = np.stack([(a == b + (c - 1) * kp) & (a // r1 == b // r1) for c in range(3)])
    a, b = np.arange(n2)[:, None], np.arange(n2)[None, :]
    near2 = np.stack([a == b + (c - 1) * r2 for c in range(3)])
    wa = prepared(e1, m1, x1, b1, near1)
    wb = prepared(e2, m2, x2, b2, near2)

    rows = planes * C
    tot1, tot2 = pltpu.VMEM((rows, 2 * lanes1), F32), pltpu.VMEM((rows, 2 * lanes2), F32)
    feat = e1.shape[2]
    band = pltpu.VMEM((3 * PACK * feat, PACK * feat), BF16)
    buf = pltpu.VMEM((2, 2 * planes, C, lanes2), F32)
    spass = jax.ShapeDtypeStruct((planes, C, lanes1), BF16)
    part = jax.ShapeDtypeStruct((n_line * np_, 128), F32)
    moved = jax.ShapeDtypeStruct((planes, C, lanes2), BF16)

    def to_stations(y):
        y = y.reshape(rows, 2, sh, n_shot, r2)
        y = lax.all_to_all(y, "shot", split_axis=3, concat_axis=2, tiled=True)
        return y.reshape(planes, C, lanes2)

    def to_shots(y):
        y = y.reshape(rows, 2, shots, 1, r2)
        y = lax.all_to_all(y, "shot", split_axis=2, concat_axis=3, tiled=True)
        return y.reshape(planes, C, lanes1)

    dims = (n_shot, n_line, n_tm)
    cube = pltpu.VMEM((planes, C, lanes1), F32)
    if fused:
        mixed = jax.ShapeDtypeStruct((rows, 2 * n_mix * r2), BF16)
        side = pltpu.VMEM((planes, C, 2 * n_mix * r2), F32)
        sp, energy, m = call(
            functools.partial(entry_kernel, dims),
            (spass, part, mixed),
            (x, *wa, member),
            0,
            [tot1, band, cube, side],
        )
    else:
        sp, energy = call(first_kernel, (spass, part), (x, *wa, member), 0, [tot1, band])
    for it in range(ITERS):
        tot = summed(energy, (n_shot, n_line, n_tm)) if whole else lax.psum(energy, AXES)
        if not whole:
            sp = to_stations(sp)
        ins = (lags, pace, sp, tot, spread, *wb, join, m, take)
        if whole and it < ITERS - 1:
            sp, energy = call(
                functools.partial(both_kernel, it, shots), (spass, part), (*ins, *wa, member), 2, [buf, tot2, band]
            )
            continue
        if fused:
            back = jax.ShapeDtypeStruct((parts, lh, tl), BF16)
            x = call(functools.partial(exit_kernel, it, dims), back, ins, 2, [buf, tot2, band, cube])
            continue
        x = call(functools.partial(station_kernel, it, shots), moved, ins, 2, [buf, tot2, band])
        if not whole:
            x = to_shots(x)
            if it < ITERS - 1:
                sp, energy = call(first_kernel, (spass, part), (x, *wa, member), 0, [tot1, band])

    if not fused:
        x = x.reshape(planes, C, 2, s1, r1).transpose(3, 4, 1, 0, 2)
        x = x.reshape(sources, sh, n_line, lh, kp, n_tm, tl).transpose(0, 2, 5, 1, 3, 4, 6)
    x = lax.all_to_all(x.reshape(parts, sh, lh, kp, tl), where, split_axis=0, concat_axis=0)
    return x.transpose(1, 2, 0, 3, 4).reshape(sh, recv, tl)


def solution(mesh):
    spec = P(("group", "shot"), "line", "tm")
    placed = (spec, P("group", "line", None), P("group"), P("group"), P("group")) + (P(),) * 9
    return jax.shard_map(per_device, mesh=mesh, in_specs=placed, out_specs=spec, check_vma=False)
```
